128 devices in a mesh: seq: 64 (over y, x, z_lo, core), tp: 2 (over z_hi).
Axes of the slice: x: 4, y: 4, z: 4 (z_hi: 2, z_lo: 2; z = z_hi * 2 + z_lo), core: 2. Of those that a mesh axis runs over, the one named last changes fastest.
Arguments:
- block_in: bfloat16 [8192, 2048], P(('seq', 'tp')), may hold values from -6 to 6
- cotangent: bfloat16 [8192, 2048], P(('seq', 'tp')), may hold values from -6 to 6
- segments: int32 [8192], replicated, may hold values from 0 to 8191, as said below
- gains: float32 [4224], replicated, may hold values from 0.5 to 1.5
- joined_weight: float32 [2048, 8, 384], P('seq', 'tp'), may hold values from -0.125 to 0.125
- output_weight: float32 [2048, 2048], P('seq', 'tp'), may hold values from -1.5 to 1.5
- expand_weight: float32 [2048, 2, 8192], P('seq', None, 'tp'), may hold values from -0.125 to 0.125
- reduce_weight: float32 [2048, 8192], P('seq', 'tp'), may hold values from -0.0625 to 0.0625
- gains_first: float32 [4224], replicated, may hold values from -512 to 512
- gains_squares: float32 [4224], replicated, may hold values from 8192 to 32768
- joined_first: float32 [2048, 8, 384], P('seq', 'tp'), may hold values from -512 to 512
- joined_squares: float32 [2048, 8, 384], P('seq', 'tp'), may hold values from 8192 to 32768
- output_first: float32 [2048, 2048], P('seq', 'tp'), may hold values from -40 to 40
- output_squares: float32 [2048, 2048], P('seq', 'tp'), may hold values from 52.4288 to 209.7152
- expand_first: float32 [2048, 2, 8192], P('seq', None, 'tp'), may hold values from -160 to 160
- expand_squares: float32 [2048, 2, 8192], P('seq', None, 'tp'), may hold values from 737.28 to 2949.12
- reduce_first: float32 [2048, 8192], P('seq', 'tp'), may hold values from -320 to 320
- reduce_squares: float32 [2048, 8192], P('seq', 'tp'), may hold values from 2949.12 to 11796.48
Outputs:
- block_out: bfloat16 [8192, 2048], P(('seq', 'tp'))
- input_grad: bfloat16 [8192, 2048], P(('seq', 'tp'))
- joined_moment: float32 [2048, 8, 384], P('seq', 'tp')
- joined_second: float32 [2048, 8, 384], P('seq', 'tp')
- joined_master: float32 [2048, 8, 384], P('seq', 'tp')
- joined_copy: bfloat16 [2048, 8, 384], P('seq', 'tp')
- output_moment: float32 [2048, 2048], P('seq', 'tp')
- output_second: float32 [2048, 2048], P('seq', 'tp')
- output_master: float32 [2048, 2048], P('seq', 'tp')
- output_copy: bfloat16 [2048, 2048], P('seq', 'tp')
- expand_moment: float32 [2048, 2, 8192], P('seq', None, 'tp')
- expand_second: float32 [2048, 2, 8192], P('seq', None, 'tp')
- expand_master: float32 [2048, 2, 8192], P('seq', None, 'tp')
- expand_copy: bfloat16 [2048, 2, 8192], P('seq', None, 'tp')
- reduce_moment: float32 [2048, 8192], P('seq', 'tp')
- reduce_second: float32 [2048, 8192], P('seq', 'tp')
- reduce_master: float32 [2048, 8192], P('seq', 'tp')
- reduce_copy: bfloat16 [2048, 8192], P('seq', 'tp')
- gains_moment: float32 [4224], replicated
- gains_second: float32 [4224], replicated
- gains_master: float32 [4224], replicated
The draws below stay inside these ranges and needn't reach their ends.
Inputs may be any that keep to these rules, and one draw needn't show every extreme that they name: `segments`: A document's number is the index of its first token. Never falls from one token to the next; the first token begins a document and the last token is a document of its own. One document holds every token from index 127 to index 8064; the tokens before and after it form shorter documents.
All inputs are finite; a program needn't handle non-finite values.
Results may differ from the reference program's by a relative error of at most 0.019.
Values may be sent and summed in bfloat16 or wider, within the bound.
A program may use at most 320 MiB of HBM per device.

```python
import math
import jax
import jax.numpy as jnp
from jax import lax

D = 2048
H = 32
KV = 8
HD = 64
FF = 8192
RUN = 128
STEP = 10
COLS = 384
SEQLEN = 8192
TOKENS = 8192
NG = 4224


def draw_segments(key, part):
    key = jax.random.fold_in(key, 11)
    count = TOKENS // SEQLEN
    key_start, key_end, key_flags = jax.random.split(key, 3)
    starts = jax.random.randint(key_start, (count, 1), 0, RUN)
    ends = jax.random.randint(key_end, (count, 1), SEQLEN - RUN + 1, SEQLEN)
    flags = (jax.random.randint(key_flags, (count, SEQLEN), 0, 8) == 0).astype(jnp.int32)
    place = jnp.arange(SEQLEN, dtype=jnp.int32)[None, :]
    flags = jnp.where((place == 0) | (place == starts) | (place == ends) | (place == SEQLEN - 1), 1, flags)
    flags = jnp.where((place > starts) & (place < ends), 0, flags)
    index = jnp.arange(count * SEQLEN, dtype=jnp.int32)
    first_index = jnp.where(flags.reshape(-1) == 1, index, 0)
    return lax.cummax(first_index, axis=0).astype(jnp.int32)


def shard_levels(rng, dims, cuts, least, high):
    level, own = 1.0, jax.random.fold_in(rng, 6)
    for axis_at, blocks in cuts:
        draws = jnp.exp(jax.random.uniform(jax.random.fold_in(own, axis_at), (blocks,), jnp.float32, least / len(cuts), high / len(cuts)))
        level = level * jnp.repeat(draws, dims[axis_at] // blocks).reshape([-1 if axis == axis_at else 1 for axis in range(len(dims))])
    return level


def normal_values(rng, extent, deviation, limit, cuts=(), kind=jnp.bfloat16):
    factor_of = shard_levels(rng, extent, cuts, -0.22, 0.18) if cuts else 1.0
    array = jax.random.normal(rng, extent, jnp.float32) * deviation * factor_of
    return jnp.minimum(jnp.maximum(array, -limit), limit).astype(kind)


def setup_inputs(seed: int = 0) -> dict:
    arg_keys = jax.random.split(jax.random.key(seed), 19)
    block_in = normal_values(arg_keys[0], (TOKENS, D), 1.0, 6.0, ((0, 128),))
    cotangent = normal_values(arg_keys[1], (TOKENS, D), 1.0, 6.0, ((0, 128),))
    segments = draw_segments(jax.random.fold_in(arg_keys[18], 71), 0)
    gains = jnp.clip(jax.random.uniform(arg_keys[3], (NG,), jnp.float32, 0.5, 1.5), 0.5, 1.5)
    joined_weight = normal_values(arg_keys[4], (D, KV, COLS), D ** -0.5, 0.125, ((0, 64), (1, 2)), jnp.float32)
    output_weight = normal_values(arg_keys[5], (D, H * HD), (max(1, H * HD // 128)) ** -0.5, 1.5, ((0, 64), (1, 2)), jnp.float32)
    expand_weight = normal_values(arg_keys[6], (D, 2, FF), D ** -0.5, 0.125, ((0, 64), (2, 2)), jnp.float32)
    reduce_weight = normal_values(arg_keys[7], (D, FF), FF ** -0.5, 0.0625, ((0, 64), (1, 2)), jnp.float32)
    gains_first = normal_values(arg_keys[8], (NG,), (TOKENS ** 0.5), 512.0, (), jnp.float32)
    gains_squares = jnp.clip(jnp.exp(jax.random.uniform(arg_keys[9], (NG,), jnp.float32, math.log(8192.0), math.log(32768.0))), 8192.0, 32768.0)
    joined_first = normal_values(arg_keys[10], (D, KV, COLS), (TOKENS ** 0.5), 512.0, ((0, 64), (1, 2)), jnp.float32)
    joined_squares = jnp.clip(jnp.exp(math.log(32768.0) - 1.3862944 * jax.random.uniform(arg_keys[11], (D, KV, COLS), jnp.float32) ** shard_levels(arg_keys[11], (D, KV, COLS), ((0, 64), (1, 2)), -0.2, 0.2)), 8192.0, 32768.0)
    output_first = normal_values(arg_keys[12], (D, H * HD), (0.08 * TOKENS ** 0.5), 40.0, ((0, 64), (1, 2)), jnp.float32)
    output_squares = jnp.clip(jnp.exp(math.log(209.7152) - 1.3862944 * jax.random.uniform(arg_keys[13], (D, H * HD), jnp.float32) ** shard_levels(arg_keys[13], (D, H * HD), ((0, 64), (1, 2)), -0.2, 0.2)), 52.4288, 209.7152)
    expand_first = normal_values(arg_keys[14], (D, 2, FF), (0.3 * TOKENS ** 0.5), 160.0, ((0, 64), (2, 2)), jnp.float32)
    expand_squares = jnp.clip(jnp.exp(math.log(2949.12) - 1.3862944 * jax.random.uniform(arg_keys[15], (D, 2, FF), jnp.float32) ** shard_levels(arg_keys[15], (D, 2, FF), ((0, 64), (2, 2)), -0.2, 0.2)), 737.28, 2949.12)
    reduce_first = normal_values(arg_keys[16], (D, FF), (0.6 * TOKENS ** 0.5), 320.0, ((0, 64), (1, 2)), jnp.float32)
    reduce_squares = jnp.clip(jnp.exp(math.log(11796.48) - 1.3862944 * jax.random.uniform(arg_keys[17], (D, FF), jnp.float32) ** shard_levels(arg_keys[17], (D, FF), ((0, 64), (1, 2)), -0.2, 0.2)), 2949.12, 11796.48)
    return {"block_in": block_in, "cotangent": cotangent, "segments": segments, "gains": gains, "joined_weight": joined_weight, "output_weight": output_weight, "expand_weight": expand_weight, "reduce_weight": reduce_weight, "gains_first": gains_first, "gains_squares": gains_squares, "joined_first": joined_first, "joined_squares": joined_squares, "output_first": output_first, "output_squares": output_squares, "expand_first": expand_first, "expand_squares": expand_squares, "reduce_first": reduce_first, "reduce_squares": reduce_squares}


EPS_NORM = 1e-05
THETA = 1000000.0
BETA_ONE = 0.5
BETA_TWO = 0.5
ADAM_EPS = 1e-08
DECAY = 0.1
GAIN_RATE = 0.2
HIGHEST = lax.Precision.HIGHEST

@jax.custom_vjp
def low(v):
    return lax.optimization_barrier(v.astype(jnp.bfloat16)).astype(jnp.float32)

@jax.custom_vjp
def low_back(v):
    return v

def low_keep(v):
    return (low(v), None)

def low_pass(kept, grad):
    return (grad,)

def back_keep(v):
    return (v, None)

def back_low(kept, grad):
    return (low(grad),)
low.defvjp(low_keep, low_pass)
low_back.defvjp(back_keep, back_low)

def rmsnorm(values, weight):
    return values * lax.rsqrt(lax.optimization_barrier(jnp.mean(values * values, axis=-1, keepdims=True)) + EPS_NORM) * weight

def tables(positions, width):
    inverse = THETA ** (-(jnp.arange(0, width, 2).astype(jnp.float32) / width))
    angles = positions.astype(jnp.float32)[:, None] * inverse[None, :]
    angles = jnp.concatenate([angles, angles], axis=-1)
    return (jnp.cos(angles), jnp.sin(angles))

def rotate(values, cosine, sine):
    half = values.shape[-1] // 2
    turned = jnp.concatenate([-values[..., half:], values[..., :half]], axis=-1)
    return values * cosine + turned * sine

def prepare(query_raw, key_raw, gain_query, gain_key, cosine, sine):
    query_rot = rotate(rmsnorm(query_raw, gain_query), cosine[:, None, None, :], sine[:, None, None, :])
    key_rot = rotate(rmsnorm(key_raw, gain_key), cosine[:, None, :], sine[:, None, :])
    return (query_rot, key_rot)

def swiglu(both):
    return jax.nn.silu(both[:, 0]) * both[:, 1]

def forward(block_in, gains, joined_weight, output_weight, expand_weight, reduce_weight, segments):
    tokens = block_in.shape[0]
    per_group = H // KV
    gain_attn = gains[:D]
    gain_ffn = gains[D:2 * D]
    gain_query = gains[2 * D:2 * D + HD]
    gain_key = gains[2 * D + HD:]
    attn_rows = low(rmsnorm(block_in, gain_attn))
    projected = low_back(jnp.einsum('rd,dgc->rgc', attn_rows, low(joined_weight), precision=HIGHEST))
    query_raw = projected[:, :, :per_group * HD].reshape(tokens, KV, per_group, HD)
    key_raw = projected[:, :, per_group * HD:(per_group + 1) * HD]
    value_raw = projected[:, :, (per_group + 1) * HD:]
    positions = jnp.arange(tokens, dtype=jnp.int32) % SEQLEN
    cosine, sine = tables(positions, HD)
    query_rot, key_rot = prepare(query_raw, key_raw, gain_query, gain_key, cosine, sine)
    queries = low(query_rot)
    keys = low(key_rot)
    values = low(value_raw)
    order = jnp.arange(tokens, dtype=jnp.int32)

    def attend_block(pieces):
        query_block, seg_block, index_block = pieces
        raw = jnp.einsum('rghd,kgd->grhk', query_block, keys, precision=HIGHEST) * HD ** (-0.5)
        raw = low_back(raw)
        allowed = (order[None, :] <= index_block[:, None]) & (segments[None, :] == seg_block[:, None])
        masked = jnp.where(allowed[None, :, None, :], raw, -1e+30)
        probs = low(jax.nn.softmax(masked, axis=-1))
        return jnp.einsum('grhk,kgd->rghd', probs, values, precision=HIGHEST)
    qblock = min(256, tokens)
    count = tokens // qblock
    attended = lax.map(jax.checkpoint(attend_block), (queries.reshape(count, qblock, KV, per_group, HD), segments.reshape(count, qblock), order.reshape(count, qblock)))
    attn_out = low_back(low(attended.reshape(tokens, H * HD)))
    middle = block_in + low_back(jnp.einsum('rc,dc->rd', attn_out, low(output_weight), precision=HIGHEST))
    ffn_rows = low(rmsnorm(middle, gain_ffn))
    both = low_back(jnp.einsum('rd,dcf->rcf', ffn_rows, low(expand_weight), precision=HIGHEST))
    hidden = low(swiglu(both))
    return middle + low_back(jnp.einsum('rf,df->rd', hidden, low(reduce_weight), precision=HIGHEST))

def adamw(master, gradient, first, second, rate):
    moment = BETA_ONE * first + (1.0 - BETA_ONE) * gradient
    squares = BETA_TWO * second + (1.0 - BETA_TWO) * gradient * gradient
    scaled_one = moment / (1.0 - BETA_ONE ** STEP)
    scaled_two = squares / (1.0 - BETA_TWO ** STEP)
    updated = master - rate * (scaled_one / (jnp.sqrt(scaled_two) + ADAM_EPS) + DECAY * master)
    return (moment, squares, updated)

def reference(block_in, cotangent, segments, gains, joined_weight, output_weight, expand_weight, reduce_weight, gains_first, gains_squares, joined_first, joined_squares, output_first, output_squares, expand_first, expand_squares, reduce_first, reduce_squares):

    def run(rows_in, gain_all, weight_one, weight_two, weight_three, weight_four):
        return forward(rows_in, gain_all, weight_one, weight_two, weight_three, weight_four, segments)
    result, pullback = jax.vjp(run, block_in.astype(jnp.float32), gains, joined_weight, output_weight, expand_weight, reduce_weight)
    grad_x, grad_gains, grad_joined, grad_output, grad_expand, grad_reduce = pullback(cotangent.astype(jnp.float32))
    joined = adamw(joined_weight, grad_joined, joined_first, joined_squares, D ** (-0.5))
    output = adamw(output_weight, grad_output, output_first, output_squares, max(1, H * HD // 128) ** (-0.5))
    expand = adamw(expand_weight, grad_expand, expand_first, expand_squares, D ** (-0.5))
    reduce_new = adamw(reduce_weight, grad_reduce, reduce_first, reduce_squares, FF ** (-0.5))
    gain_new = adamw(gains, grad_gains, gains_first, gains_squares, GAIN_RATE)
    return (result.astype(jnp.bfloat16), grad_x.astype(jnp.bfloat16), joined[0], joined[1], joined[2], joined[2].astype(jnp.bfloat16), output[0], output[1], output[2], output[2].astype(jnp.bfloat16), expand[0], expand[1], expand[2], expand[2].astype(jnp.bfloat16), reduce_new[0], reduce_new[1], reduce_new[2], reduce_new[2].astype(jnp.bfloat16), gain_new[0], gain_new[1], gain_new[2])
```

```python
import functools

import jax
import jax.numpy as jnp
from jax import lax
from jax.experimental import pallas as pl
from jax.experimental.pallas import tpu as pltpu
from jax.sharding import Mesh
from jax.sharding import PartitionSpec as P

D = 2048
H = 32
HD = 64
FF = 8192
STEP = 10

EPS_NORM = 1e-05
THETA = 1000000.0
BETA_ONE = 0.5
BETA_TWO = 0.5
ADAM_EPS = 1e-08
DECAY = 0.1
GAIN_RATE = 0.2

AXES = ("y", "x", "zl", "c", "zh")
SEQ = ("y", "x", "zl", "c")
SIDE = 4
TEAMS = 16
TEAM = 8
GROUP_HEADS = 4
BF = jnp.bfloat16
F32 = jnp.float32
MESHID = pl.DeviceIdType.MESH
ANY = pl.BlockSpec(memory_space=pl.ANY)
VM = pl.BlockSpec(memory_space=pltpu.VMEM)
DMA = pltpu.SemaphoreType.DMA


def rmsnorm(values, weight):
    return values * lax.rsqrt(jnp.mean(values * values, axis=-1, keepdims=True) + EPS_NORM) * weight


def tables(positions, width):
    inverse = THETA ** (-(jnp.arange(0, width, 2).astype(jnp.float32) / width))
    angles = positions.astype(jnp.float32)[:, None] * inverse[None, :]
    angles = jnp.concatenate([angles, angles], axis=-1)
    return (jnp.cos(angles), jnp.sin(angles))


def rotate(values, cosine, sine):
    half = values.shape[-1] // 2
    turned = jnp.concatenate([-values[..., half:], values[..., :half]], axis=-1)
    return values * cosine + turned * sine


def prepare(query_raw, key_raw, gain_query, gain_key, cosine, sine):
    query_rot = rotate(rmsnorm(query_raw, gain_query), cosine[:, None, :], sine[:, None, :])
    key_rot = rotate(rmsnorm(key_raw, gain_key), cosine, sine)
    return (query_rot, key_rot)


def swiglu(both):
    half = both.shape[-1] // 2
    return jax.nn.silu(both[:, :half]) * both[:, half:]


def adamw(master, gradient, first, second, rate):
    moment = BETA_ONE * first + (1.0 - BETA_ONE) * gradient
    squares = BETA_TWO * second + (1.0 - BETA_TWO) * gradient * gradient
    scaled_one = moment / (1.0 - BETA_ONE**STEP)
    scaled_two = squares / (1.0 - BETA_TWO**STEP)
    updated = master - rate * (scaled_one / (jnp.sqrt(scaled_two) + ADAM_EPS) + DECAY * master)
    return (moment, squares, updated)


def here():
    return {a: lax.axis_index(a) for a in AXES}


def moved(at, axis, step=1):
    to = dict(at)
    if axis == "z":
        z = lax.rem(at["zh"] * 2 + at["zl"] + step + SIDE, SIDE)
        to["zh"] = z // 2
        to["zl"] = lax.rem(z, 2)
    elif axis == "quad":
        if step & 1:
            to["c"] = 1 - at["c"]
        if step & 2:
            to["zl"] = 1 - at["zl"]
    elif axis == "c":
        to["c"] = 1 - at["c"]
    else:
        to[axis] = lax.rem(at[axis] + step + SIDE, SIDE)
    return to


def ident(at):
    return tuple(at[a] for a in AXES)


def greet(at, moves):
    barrier = pltpu.get_barrier_semaphore()
    for axis, step in moves:
        pl.semaphore_signal(
            barrier, inc=1, device_id=ident(moved(at, axis, step)), device_id_type=MESHID
        )
    pl.semaphore_wait(barrier, len(moves))


def remote(src, dst, ssem, rsem, to):
    return pltpu.make_async_remote_copy(
        src_ref=src,
        dst_ref=dst,
        send_sem=ssem,
        recv_sem=rsem,
        device_id=ident(to),
        device_id_type=MESHID,
    )


def params(cid, vmem=48):
    return pltpu.CompilerParams(
        collective_id=cid, has_side_effects=True, vmem_limit_bytes=vmem << 20
    )


def place(z, c):
    return (lax.rem(z, 2) * 2 + c) * 2 + z // 2


QUAD = (("quad", 1), ("quad", 2), ("quad", 3))
NEAR = (("x", 1), ("x", -1), ("y", 1), ("y", -1))
FAR = tuple((axis, step) for axis in ("x", "y") for step in (1, 2, 3))
RING = (("z", 1), ("z", -1), ("z", 2), ("c", 1))


class Spread:
    def __init__(self, at, first, second, out, lo, rows, ssem, rsem):
        self.at, self.f, self.s, self.out = at, first, second, out
        self.lo, self.rows, self.ssem, self.rsem = lo, rows, ssem, rsem
        self.sent = []

    def slot(self, df, ds, part=None):
        f = lax.rem(self.at[self.f] + df + SIDE, SIDE)
        s = lax.rem(self.at[self.s] + ds + SIDE, SIDE)
        y, x = (f, s) if self.f == "y" else (s, f)
        lo, n = self.lo, self.rows
        if part is not None:
            n = n // 2
            lo = lo + part * n
        return self.out.at[y * SIDE + x, pl.ds(lo, n)]

    def send(self, block, k, axis, step):
        copy = remote(block, block, self.ssem.at[k], self.rsem.at[k], moved(self.at, axis, step))
        copy.start()
        self.sent.append(copy)

    def wait(self, block, k):
        to = moved(self.at, self.f, 1)
        remote(block, block, self.ssem.at[k], self.rsem.at[k], to).wait_recv()

    def one_a(self):
        self.send(self.slot(0, 0), 0, self.f, 1)
        self.send(self.slot(0, 0), 1, self.f, -1)

    def one_b(self, side):
        df = -1 if side == 0 else 1
        self.wait(self.slot(df, 0), side)
        self.send(self.slot(df, 0, side), 2 + side, self.f, -df)

    def one_c(self):
        self.wait(self.slot(2, 0, 0), 2)
        self.wait(self.slot(2, 0, 1), 3)

    STEPS = (0, -1, 1, 2)

    def two_a(self, j):
        block = self.slot(self.STEPS[j], 0)
        self.send(block, 4 + 4 * j, self.s, 1)
        self.send(block, 5 + 4 * j, self.s, -1)

    def two_b(self, j, side):
        ds = -1 if side == 0 else 1
        self.wait(self.slot(self.STEPS[j], ds), 4 + 4 * j + side)
        self.send(self.slot(self.STEPS[j], ds, side), 6 + 4 * j + side, self.s, -ds)

    def two_c(self, j):
        self.wait(self.slot(self.STEPS[j], 2, 0), 6 + 4 * j)
        self.wait(self.slot(self.STEPS[j], 2, 1), 7 + 4 * j)

    def done(self):
        for copy in self.sent:
            copy.wait_send()


def spread_rest(halves):
    for side in (0, 1):
        for h in halves:
            h.one_b(side)
            h.two_a(1 + side)
    for side in (0, 1):
        for h in halves:
            h.two_b(0, side)
    for h in halves:
        h.one_c()
        h.two_a(3)
    for j in (1, 2, 3):
        for side in (0, 1):
            for h in halves:
                h.two_b(j, side)
    for j in range(4):
        for h in halves:
            h.two_c(j)
    for h in halves:
        h.done()


def weights_kernel(count, *refs):
    pieces, outs = refs[:count], refs[count : 2 * count]
    ssem, rsem, qs, qr, lsem = refs[2 * count :]
    at = here()
    mine = at["y"] * SIDE + at["x"]
    quad = at["zl"] * 2 + at["c"]
    near = pl.multiple_of(at["zl"] * 64, 64)
    far = pl.multiple_of(64 - at["zl"] * 64, 64)
    greet(at, NEAR + QUAD)
    quads, locals_ = [], []
    for k, (piece, out) in enumerate(zip(pieces, outs)):
        rows = out.at[mine, pl.ds(pl.multiple_of(quad * 32, 32), 32)]
        local = pltpu.make_async_copy(piece.at[quad], rows, lsem.at[k])
        local.start()
        locals_.append(local)
        for step in (1, 2, 3):
            to = moved(at, "quad", step)
            copy = remote(
                piece.at[to["zl"] * 2 + to["c"]], rows, qs.at[k, step - 1], qr.at[k, step - 1], to
            )
            copy.start()
            quads.append(copy)
    firsts, seconds = [], []
    for k, out in enumerate(outs):
        firsts.append(Spread(at, "x", "y", out, near, 64, ssem.at[k, 0], rsem.at[k, 0]))
        seconds.append(Spread(at, "y", "x", out, far, 64, ssem.at[k, 1], rsem.at[k, 1]))
    for k in range(count):
        locals_[k].wait()
        quads[3 * k].wait_recv()
        firsts[k].one_a()
        firsts[k].two_a(0)
    for k in range(count):
        quads[3 * k + 1].wait_recv()
        quads[3 * k + 2].wait_recv()
        seconds[k].one_a()
        seconds[k].two_a(0)
    spread_rest(firsts + seconds)
    for copy in quads:
        copy.wait_send()


def gather_weights(pieces, cid):
    count = len(pieces)
    return pl.pallas_call(
        functools.partial(weights_kernel, count),
        out_shape=[jax.ShapeDtypeStruct((TEAMS, 128, p.shape[2]), p.dtype) for p in pieces],
        in_specs=[ANY] * count,
        out_specs=[ANY] * count,
        scratch_shapes=[
            DMA((count, 2, 20)),
            DMA((count, 2, 20)),
            DMA((count, 3)),
            DMA((count, 3)),
            DMA((count,)),
        ],
        compiler_params=params(cid),
    )(*pieces)


def plane_kernel(src, out, ssem, rsem, lsem):
    at = here()
    mine = at["y"] * SIDE + at["x"]
    half = src.shape[0] // 2
    greet(at, NEAR)
    local = pltpu.make_async_copy(src, out.at[mine], lsem)
    local.start()
    halves = [
        Spread(at, "x", "y", out, 0, half, ssem.at[0], rsem.at[0]),
        Spread(at, "y", "x", out, half, half, ssem.at[1], rsem.at[1]),
    ]
    local.wait()
    for h in halves:
        h.one_a()
        h.two_a(0)
    spread_rest(halves)


def gather_plane(rows, cid):
    return pl.pallas_call(
        plane_kernel,
        out_shape=jax.ShapeDtypeStruct((TEAMS,) + rows.shape, rows.dtype),
        in_specs=[ANY],
        out_specs=ANY,
        scratch_shapes=[DMA((2, 20)), DMA((2, 20)), DMA],
        compiler_params=params(cid),
    )(rows)


class Gather:
    def __init__(self, at, first, second, src, lo, own, one, held, two, ssem, rsem, lsem):
        self.at, self.f, self.s, self.src, self.lo = at, first, second, src, lo
        self.own, self.one, self.held, self.two = own, one, held, two
        self.ssem, self.rsem, self.lsem = ssem, rsem, lsem
        self.rows = own.shape[1]

    def block(self, f, s):
        y, x = (f, s) if self.f == "y" else (s, f)
        return self.src.at[y * SIDE + x, pl.ds(self.lo, self.rows)]

    def start(self):
        self.sent, self.kept = [], []
        for d in (2, 1, 3):
            f = lax.rem(self.at[self.f] + d, SIDE)
            for s in range(SIDE):
                k = (d - 1) * 4 + s
                copy = remote(
                    self.block(f, s),
                    self.one.at[d - 1, s],
                    self.ssem.at[k],
                    self.rsem.at[k],
                    moved(self.at, self.f, d),
                )
                copy.start()
                self.sent.append((d, s, copy))
        for s in range(SIDE):
            copy = pltpu.make_async_copy(
                self.block(self.at[self.f], s), self.own.at[s], self.lsem.at[s]
            )
            copy.start()
            self.kept.append(copy)

    def middle(self):
        for copy in self.kept:
            copy.wait()
        for d, s, copy in self.sent:
            copy.wait_recv()

        def add(s, carry):
            total = self.own[s].astype(F32)
            for d in range(3):
                total = total + self.one[d, s].astype(F32)
            self.held[s] = total.astype(BF)
            return carry

        lax.fori_loop(0, SIDE, add, 0)
        for d in (2, 1, 3):
            copy = remote(
                self.held.at[lax.rem(self.at[self.s] + d, SIDE)],
                self.two.at[d - 1],
                self.ssem.at[11 + d],
                self.rsem.at[11 + d],
                moved(self.at, self.s, d),
            )
            copy.start()
            self.sent.append((d, 0, copy))

    def finish(self):
        for d, s, copy in self.sent[12:]:
            copy.wait_recv()
        total = self.held[self.at[self.s]].astype(F32)
        for d in range(3):
            total = total + self.two[d].astype(F32)
        return total

    def done(self):
        for d, s, copy in self.sent:
            copy.wait_send()


def grads_kernel(count, *refs):
    srcs, outs = refs[:count], refs[count : 2 * count]
    scratch = refs[2 * count :]
    qs, qr = scratch[-2:]
    at = here()
    quad = at["zl"] * 2 + at["c"]
    greet(at, FAR + QUAD)
    halves = []
    for k in range(count):
        own, one, held, two, total, ssem, rsem, lsem = scratch[8 * k : 8 * k + 8]
        halves.append(
            [
                Gather(
                    at,
                    f,
                    s,
                    srcs[k],
                    64 * n,
                    own.at[n],
                    one.at[n],
                    held.at[n],
                    two.at[n],
                    ssem.at[n],
                    rsem.at[n],
                    lsem.at[n],
                )
                for n, (f, s) in enumerate((("y", "x"), ("x", "y")))
            ]
        )
    for pair in halves:
        for h in pair:
            h.start()
    for pair in halves:
        for h in pair:
            h.middle()
    quads = []
    for k, pair in enumerate(halves):
        total = scratch[8 * k + 4]
        for n, h in enumerate(pair):
            total[n] = h.finish().astype(BF)
        for step in (3, 2, 1):
            to = moved(at, "quad", step)
            copy = remote(
                total.at[to["zl"], pl.ds(pl.multiple_of(to["c"] * 32, 32), 32)],
                outs[k].at[quad],
                qs.at[k, step - 1],
                qr.at[k, step - 1],
                to,
            )
            copy.start()
            quads.append(copy)
        outs[k][quad] = total[at["zl"], pl.ds(pl.multiple_of(at["c"] * 32, 32), 32)]
    for copy in quads:
        copy.wait()
    for pair in halves:
        for h in pair:
            h.done()


def reduce_grads(grads, cid):
    count = len(grads)
    scratch = []
    for g in grads:
        n = g.shape[2]
        scratch += [
            pltpu.VMEM((2, SIDE, 64, n), BF),
            pltpu.VMEM((2, 3, SIDE, 64, n), BF),
            pltpu.VMEM((2, SIDE, 64, n), BF),
            pltpu.VMEM((2, 3, 64, n), BF),
            pltpu.VMEM((2, 64, n), BF),
            DMA((2, 15)),
            DMA((2, 15)),
            DMA((2, 4)),
        ]
    scratch += [DMA((count, 3)), DMA((count, 3))]
    return pl.pallas_call(
        functools.partial(grads_kernel, count),
        out_shape=[jax.ShapeDtypeStruct((4, 32, g.shape[2]), BF) for g in grads],
        in_specs=[ANY] * count,
        out_specs=[VM] * count,
        scratch_shapes=scratch,
        compiler_params=params(cid),
    )(*grads)


def pairs_kernel(src, out, own, one, held, two, ssem, rsem, lsem):
    at = here()
    half = own.shape[2]
    greet(at, FAR)
    halves = [
        Gather(
            at,
            f,
            s,
            src,
            half * n,
            own.at[n],
            one.at[n],
            held.at[n],
            two.at[n],
            ssem.at[n],
            rsem.at[n],
            lsem.at[n],
        )
        for n, (f, s) in enumerate((("y", "x"), ("x", "y")))
    ]
    for h in halves:
        h.start()
    for h in halves:
        h.middle()
    for n, h in enumerate(halves):
        out[pl.ds(half * n, half)] = h.finish()
    for h in halves:
        h.done()


def reduce_plane(grads, cid):
    _, rows, n = grads.shape
    half = rows // 2
    return pl.pallas_call(
        pairs_kernel,
        out_shape=jax.ShapeDtypeStruct((rows, n), F32),
        in_specs=[ANY],
        out_specs=VM,
        scratch_shapes=[
            pltpu.VMEM((2, SIDE, half, n), BF),
            pltpu.VMEM((2, 3, SIDE, half, n), BF),
            pltpu.VMEM((2, SIDE, half, n), BF),
            pltpu.VMEM((2, 3, half, n), BF),
            DMA((2, 15)),
            DMA((2, 15)),
            DMA((2, 4)),
        ],
        compiler_params=params(cid),
    )(grads)


def team_gather_kernel(src, out, ssem, rsem, fsem, gsem, lsem):
    at = here()
    c, z = at["c"], at["zh"] * 2 + at["zl"]
    mine = out.at[place(z, c)]
    greet(at, RING)
    local = pltpu.make_async_copy(src, mine, lsem)
    local.start()
    sibling = moved(at, "c")
    ring, pair = [], []
    for k, d in enumerate((2, 1, -1)):
        copy = remote(src, mine, ssem.at[k], rsem.at[k], moved(at, "z", d))
        copy.start()
        ring.append(copy)
    copy = remote(src, mine, fsem.at[3], gsem.at[3], sibling)
    copy.start()
    pair.append(copy)
    for k, d in ((1, 1), (2, -1), (0, 2)):
        slot = out.at[place(lax.rem(z - d + SIDE, SIDE), c)]
        ring[k].wait_recv()
        copy = remote(slot, slot, fsem.at[k], gsem.at[k], sibling)
        copy.start()
        pair.append(copy)
    for copy in ring:
        copy.wait_send()
    for copy in pair:
        copy.wait()
    local.wait()


def team_gather(rows, cid):
    count, width = rows.shape
    out = pl.pallas_call(
        team_gather_kernel,
        out_shape=jax.ShapeDtypeStruct((TEAM, count, width), rows.dtype),
        in_specs=[ANY],
        out_specs=ANY,
        scratch_shapes=[DMA((3,)), DMA((3,)), DMA((4,)), DMA((4,)), DMA],
        compiler_params=params(cid),
    )(rows)
    return out.reshape(TEAM * count, width)


def team_reduce_kernel(part, out, one, held, two, ssem, rsem, s2, r2):
    at = here()
    c, z = at["c"], at["zh"] * 2 + at["zl"]
    greet(at, RING)
    sibling = moved(at, "c")
    order = (2, 1, -1, 0)
    first, second = [], []
    for k, d in enumerate(order):
        slot = place(lax.rem(z + d + SIDE, SIDE), 1 - c)
        copy = remote(part.at[slot], one.at[k], ssem.at[k], rsem.at[k], sibling)
        copy.start()
        first.append(copy)
    for k, d in enumerate(order):
        first[k].wait_recv()
        slot = place(lax.rem(z + d + SIDE, SIDE), c)
        total = part[slot].astype(F32) + one[k].astype(F32)
        if d == 0:
            out[...] = total
        else:
            held[k] = total.astype(BF)
            copy = remote(held.at[k], two.at[k], s2.at[k], r2.at[k], moved(at, "z", d))
            copy.start()
            second.append(copy)
    for k in (1, 2, 0):
        second[k].wait_recv()
        out[...] += two[k].astype(F32)
    for copy in first + second:
        copy.wait_send()


def team_reduce(part, cid):
    count, width = part.shape[0] // TEAM, part.shape[1]
    return pl.pallas_call(
        team_reduce_kernel,
        out_shape=jax.ShapeDtypeStruct((count, width), F32),
        in_specs=[VM],
        out_specs=VM,
        scratch_shapes=[
            pltpu.VMEM((4, count, width), BF),
            pltpu.VMEM((3, count, width), BF),
            pltpu.VMEM((3, count, width), BF),
            DMA((4,)),
            DMA((4,)),
            DMA((3,)),
            DMA((3,)),
        ],
        compiler_params=params(cid),
    )(part.reshape(TEAM, count, width))


def sum_kernel(src, out, pair, ring, row, column, ssem, rsem):
    at = here()
    z = at["zh"] * 2 + at["zl"]
    greet(at, RING + FAR)
    out[...] = src[...]
    k = 0
    for axis, buffer, me in (
        ("c", pair, at["c"]),
        ("z", ring, z),
        ("x", row, at["x"]),
        ("y", column, at["y"]),
    ):
        buffer[me] = out[...]
        copies = []
        for step in range(1, buffer.shape[0]):
            copy = remote(
                buffer.at[me], buffer.at[me], ssem.at[k], rsem.at[k], moved(at, axis, step)
            )
            copy.start()
            copies.append(copy)
            k += 1
        for copy in copies:
            copy.wait()
        total = buffer[0]
        for n in range(1, buffer.shape[0]):
            total = total + buffer[n]
        out[...] = total


def sum_all(vector, cid):
    lines = vector.shape[0] // 128
    shape = (lines, 128)
    return pl.pallas_call(
        sum_kernel,
        out_shape=jax.ShapeDtypeStruct(shape, F32),
        in_specs=[VM],
        out_specs=VM,
        scratch_shapes=[
            pltpu.VMEM((2,) + shape, F32),
            pltpu.VMEM((4,) + shape, F32),
            pltpu.VMEM((4,) + shape, F32),
            pltpu.VMEM((4,) + shape, F32),
            DMA((10,)),
            DMA((10,)),
        ],
        compiler_params=params(cid),
    )(vector.reshape(shape)).reshape(vector.shape)


def dot_last(a, b):
    return lax.dot_general(a, b, (((1,), (1,)), ((), ())), preferred_element_type=F32)


def dot_first(a, b):
    return lax.dot_general(a, b, (((0,), (0,)), ((), ())), preferred_element_type=F32)


def attend_kernel(q_ref, kv_ref, segc_ref, segr_ref, main_ref, out_ref, sum_ref):
    team = lax.axis_index("y") * SIDE + lax.axis_index("x")
    rows = q_ref.shape[1]
    out_ref[...] = jnp.zeros_like(out_ref)
    sum_ref[...] = jnp.zeros_like(sum_ref)

    def block(number, allowed):
        pairs = kv_ref[number]
        for h in range(GROUP_HEADS):
            weights = jnp.exp(dot_last(q_ref[h], pairs))
            if allowed is not None:
                weights = jnp.where(allowed, weights, 0.0)
            part = weights[:, :128]
            for lane in range(128, rows, 128):
                part = part + weights[:, lane : lane + 128]
            sum_ref[h] += part
            out_ref[h] += jnp.dot(weights.astype(BF), pairs, preferred_element_type=F32)

    def inner(number, carry):
        block(number, None)
        return carry

    lax.fori_loop(1, team, inner, 0)
    for h in range(GROUP_HEADS):
        out_ref[h] *= main_ref[...]
        sum_ref[h] *= main_ref[...]

    def edge(step, carry):
        number = step * team
        ahead = (number - team) * rows
        row = lax.broadcasted_iota(jnp.int32, (rows, rows), 0)
        column = lax.broadcasted_iota(jnp.int32, (rows, rows), 1) + ahead
        block(number, (column <= row) & (segc_ref[...] == segr_ref[number]))
        return carry

    lax.fori_loop(jnp.where(team == 0, 1, 0), 2, edge, 0)
    for h in range(GROUP_HEADS):
        total = jnp.sum(sum_ref[h], axis=-1, keepdims=True)
        sum_ref[h] = jnp.broadcast_to(total, sum_ref.shape[1:])


def attend(queries, every, seg_columns, seg_rows, main_column):
    rows = queries.shape[1]
    return pl.pallas_call(
        attend_kernel,
        out_shape=[jax.ShapeDtypeStruct((GROUP_HEADS, rows, 128), F32)] * 2,
        in_specs=[VM] * 5,
        out_specs=[VM] * 2,
        compiler_params=pltpu.CompilerParams(vmem_limit_bytes=48 << 20),
    )(queries, every, seg_columns, seg_rows, main_column)


def attend_back_kernel(
    q_ref,
    do_ref,
    inner_ref,
    kv_ref,
    segc_ref,
    segr_ref,
    mainc_ref,
    mainr_ref,
    dq_ref,
    dkv_ref,
    qm_ref,
    dom_ref,
    innerm_ref,
):
    team = lax.axis_index("y") * SIDE + lax.axis_index("x")
    rows = q_ref.shape[1]
    dq_ref[...] = jnp.zeros_like(dq_ref)
    low = mainc_ref[...].astype(BF)
    for h in range(GROUP_HEADS):
        qm_ref[h] = q_ref[h] * low
        dom_ref[h] = do_ref[h] * low
        innerm_ref[h] = inner_ref[h] * mainr_ref[...]

    def block(number, allowed, q, do, inner):
        pairs = kv_ref[number]
        total = jnp.zeros(pairs.shape, F32)
        for h in range(GROUP_HEADS):
            weights = jnp.exp(dot_last(pairs, q[h]))
            if allowed is not None:
                weights = jnp.where(allowed, weights, 0.0)
            grad = (weights * (dot_last(pairs, do[h]) - inner[h])).astype(BF)
            total = total + jnp.dot(grad, q[h], preferred_element_type=F32)
            total = total + jnp.dot(weights.astype(BF), do[h], preferred_element_type=F32)
            dq_ref[h] += dot_first(pairs, grad)
        dkv_ref[number] = total.astype(BF)

    def interior(number, carry):
        block(number, None, qm_ref, dom_ref, innerm_ref)
        return carry

    lax.fori_loop(1, team, interior, 0)

    def edge(step, carry):
        number = step * team
        ahead = (number - team) * rows
        row = lax.broadcasted_iota(jnp.int32, (rows, rows), 1)
        column = lax.broadcasted_iota(jnp.int32, (rows, rows), 0) + ahead
        allowed = (column <= row) & (segc_ref[number] == segr_ref[...])
        block(number, allowed, q_ref, do_ref, inner_ref)
        return carry

    lax.fori_loop(jnp.where(team == 0, 1, 0), 2, edge, 0)

    def rest(number, carry):
        dkv_ref[number] = jnp.zeros(dkv_ref.shape[1:], BF)
        return carry

    lax.fori_loop(team + 1, TEAMS, rest, 0)


def attend_back(queries, grads, inner, every, seg_columns, seg_rows, main_column, main_row):
    rows = queries.shape[1]
    return pl.pallas_call(
        attend_back_kernel,
        out_shape=[
            jax.ShapeDtypeStruct((GROUP_HEADS, 128, rows), F32),
            jax.ShapeDtypeStruct(every.shape, BF),
        ],
        in_specs=[VM] * 8,
        out_specs=[VM] * 2,
        scratch_shapes=[
            pltpu.VMEM(queries.shape, BF),
            pltpu.VMEM(grads.shape, BF),
            pltpu.VMEM(inner.shape, F32),
        ],
        compiler_params=pltpu.CompilerParams(vmem_limit_bytes=48 << 20),
    )(queries, grads, inner, every, seg_columns, seg_rows, main_column, main_row)


def matmul(a, b, contract, kind=F32):
    return lax.dot_general(a, b, ((contract[:1], contract[1:]), ((), ())), preferred_element_type=F32).astype(kind)


def on_device(
    block_in,
    cotangent,
    segments,
    gains,
    joined_weight,
    output_weight,
    expand_weight,
    reduce_weight,
    gains_first,
    gains_squares,
    joined_first,
    joined_squares,
    output_first,
    output_squares,
    expand_first,
    expand_squares,
    reduce_first,
    reduce_squares,
):
    model, width = D, HD
    factor = width ** (-0.5)
    team = lax.axis_index("y") * SIDE + lax.axis_index("x")
    gain_attn = gains[:model]
    gain_ffn = gains[model : 2 * model]
    gain_query = gains[2 * model : 2 * model + width]
    gain_key = gains[2 * model + width :]

    joined_pieces = joined_weight.astype(BF).transpose(1, 0, 2)
    output_pieces = output_weight.astype(BF).reshape(32, 4, 256).transpose(1, 0, 2)
    expand_pieces = (
        expand_weight.astype(BF).reshape(32, 2, 4, 1024).transpose(2, 0, 1, 3).reshape(4, 32, 2048)
    )
    reduce_pieces = reduce_weight.astype(BF).reshape(32, 4, 1024).transpose(1, 0, 2)
    joined_all, output_all = gather_weights([joined_pieces, output_pieces], 1)
    expand_all, reduce_all = gather_weights([expand_pieces, reduce_pieces], 2)
    joined_all = joined_all.reshape(model, -1)
    output_all = output_all.reshape(model, -1)
    expand_all = expand_all.reshape(model, -1)
    reduce_all = reduce_all.reshape(model, -1)

    residual = block_in.astype(F32)
    normed, norm_one_back = jax.vjp(rmsnorm, residual, gain_attn)
    attn_rows = team_gather(normed.astype(BF), 3)
    grad_rows = team_gather(cotangent, 3)
    rows = attn_rows.shape[0]
    projected = matmul(attn_rows, joined_all, (1, 0))
    query_raw = projected[:, : GROUP_HEADS * width].reshape(rows, GROUP_HEADS, width)
    key_raw = projected[:, GROUP_HEADS * width : (GROUP_HEADS + 1) * width]
    value_raw = projected[:, (GROUP_HEADS + 1) * width :]
    first_row = team * rows
    query_index = first_row + jnp.arange(rows, dtype=jnp.int32)
    cosine, sine = tables(query_index, width)

    def prepared(query_part, key_part, query_gain, key_gain):
        return prepare(query_part, key_part, query_gain, key_gain, cosine, sine)

    (query_rot, key_rot), prep_back = jax.vjp(prepared, query_raw, key_raw, gain_query, gain_key)
    queries = query_rot.astype(BF).transpose(1, 0, 2) * jnp.asarray(factor, BF)
    queries = jnp.pad(queries, ((0, 0), (0, 0), (0, 128 - width)))
    own_pairs = jnp.concatenate([key_rot.astype(BF), value_raw.astype(BF)], axis=1)
    every = gather_plane(own_pairs, 4)

    query_seg = lax.dynamic_slice_in_dim(segments, first_row, rows)
    main = (query_seg == segments[127]).astype(F32)
    seg_blocks = segments.reshape(TEAMS, rows)
    attended, total = attend(
        queries, every, query_seg[:, None], seg_blocks[:, None, :], main[:, None]
    )
    total = total[:, :, :1]
    attended = attended[:, :, width:] / total
    attn_out = attended.astype(BF).transpose(1, 0, 2).reshape(rows, GROUP_HEADS * width)
    branch = matmul(attn_out, output_all, (1, 1), BF)
    middle = residual + team_reduce(branch, 5)
    normed_two, norm_two_back = jax.vjp(rmsnorm, middle, gain_ffn)
    ffn_rows = team_gather(normed_two.astype(BF), 3)
    both = matmul(ffn_rows, expand_all, (1, 0))
    hidden, swiglu_back = jax.vjp(swiglu, both)
    hidden_low = hidden.astype(BF)
    branch_two = matmul(hidden_low, reduce_all, (1, 1), BF)
    grad_out = cotangent.astype(F32)
    grad_reduce = matmul(grad_rows, hidden_low, (0, 0), BF)
    grad_hidden = matmul(grad_rows, reduce_all, (1, 0))
    (grad_both,) = swiglu_back(grad_hidden)
    grad_both_low = grad_both.astype(BF)
    grad_expand = matmul(ffn_rows, grad_both_low, (0, 0), BF)
    grad_ffn_rows = team_reduce(matmul(grad_both_low, expand_all, (1, 1), BF), 5)
    block_out = (middle + team_reduce(branch_two, 5)).astype(BF)
    grad_middle_norm, grad_gain_ffn = norm_two_back(grad_ffn_rows)
    grad_middle = grad_out + grad_middle_norm
    grad_branch = team_gather(grad_middle.astype(BF), 3)
    grad_output = matmul(grad_branch, attn_out, (0, 0), BF)
    grad_attended = matmul(grad_branch, output_all, (1, 0))
    grad_attended = grad_attended.reshape(rows, GROUP_HEADS, width).transpose(1, 0, 2)
    scaled = (grad_attended / total).astype(BF)
    inner = jnp.sum(scaled.astype(F32) * attended, axis=-1)
    scaled = jnp.pad(scaled, ((0, 0), (0, 0), (128 - width, 0)))
    grad_queries, grad_blocks = attend_back(
        queries,
        scaled,
        inner[:, None, :],
        every,
        seg_blocks[:, :, None],
        query_seg[None, :],
        main[:, None],
        main[None, :],
    )
    own_grad = reduce_plane(grad_blocks, 6)
    grad_queries = grad_queries[:, :width].transpose(2, 0, 1) * factor
    grad_query_raw, grad_key_raw, grad_gain_query, grad_gain_key = prep_back(
        (grad_queries, own_grad[:, :width])
    )
    grad_projected = jnp.concatenate(
        [grad_query_raw.reshape(rows, GROUP_HEADS * width), grad_key_raw, own_grad[:, width:]],
        axis=-1,
    ).astype(BF)
    grad_joined = matmul(attn_rows, grad_projected, (0, 0), BF)
    grad_attn_rows = team_reduce(matmul(grad_projected, joined_all, (1, 1), BF), 5)
    grad_res_norm, grad_gain_attn = norm_one_back(grad_attn_rows)
    input_grad = (grad_middle + grad_res_norm).astype(BF)
    gain_grad = sum_all(
        jnp.concatenate([grad_gain_attn, grad_gain_ffn, grad_gain_query, grad_gain_key]), 7
    )

    def blocks(grad):
        return grad.reshape(TEAMS, 128, -1)

    shard_expand, shard_reduce = reduce_grads([blocks(grad_expand), blocks(grad_reduce)], 8)
    shard_joined, shard_output = reduce_grads([blocks(grad_joined), blocks(grad_output)], 9)
    shard_joined = shard_joined.transpose(1, 0, 2).astype(F32)
    shard_output = shard_output.transpose(1, 0, 2).reshape(32, 1024).astype(F32)
    shard_expand = (
        shard_expand.reshape(4, 32, 2, 1024).transpose(1, 2, 0, 3).reshape(32, 2, 4096).astype(F32)
    )
    shard_reduce = shard_reduce.transpose(1, 0, 2).reshape(32, 4096).astype(F32)
    joined = adamw(joined_weight, shard_joined, joined_first, joined_squares, D ** (-0.5))
    output = adamw(
        output_weight, shard_output, output_first, output_squares, max(1, H * HD // 128) ** (-0.5)
    )
    expand = adamw(expand_weight, shard_expand, expand_first, expand_squares, D ** (-0.5))
    reduce_new = adamw(reduce_weight, shard_reduce, reduce_first, reduce_squares, FF ** (-0.5))
    gain_new = adamw(gains, gain_grad, gains_first, gains_squares, GAIN_RATE)
    return (
        block_out,
        input_grad,
        joined[0],
        joined[1],
        joined[2],
        joined[2].astype(BF),
        output[0],
        output[1],
        output[2],
        output[2].astype(BF),
        expand[0],
        expand[1],
        expand[2],
        expand[2].astype(BF),
        reduce_new[0],
        reduce_new[1],
        reduce_new[2],
        reduce_new[2].astype(BF),
        gain_new[0],
        gain_new[1],
        gain_new[2],
    )


def solution(mesh):
    physical = Mesh(mesh.devices.reshape(SIDE, SIDE, 2, 2, 2), AXES)
    rows = P(AXES, None)
    joined = P(SEQ, "zh", None)
    plain = P(SEQ, "zh")
    expand = P(SEQ, None, "zh")
    placed = (
        (rows, rows, P(), P(), joined, plain, expand, plain, P(), P())
        + (joined,) * 2
        + (plain,) * 2
        + (expand,) * 2
        + (plain,) * 2
    )
    return jax.shard_map(
        on_device,
        mesh=physical,
        in_specs=placed,
        out_specs=(rows, rows)
        + (joined,) * 4
        + (plain,) * 4
        + (expand,) * 4
        + (plain,) * 4
        + (P(),) * 3,
        check_vma=False,
    )
```

```python
import functools

import jax
import jax.numpy as jnp
from jax import lax
from jax.experimental import pallas as pl
from jax.experimental.pallas import tpu as pltpu
from jax.sharding import Mesh
from jax.sharding import PartitionSpec as P

D = 2048
H = 32
HD = 64
FF = 8192
STEP = 10

EPS_NORM = 1e-05
THETA = 1000000.0
BETA_ONE = 0.5
BETA_TWO = 0.5
ADAM_EPS = 1e-08
DECAY = 0.1
GAIN_RATE = 0.2

AXES = ("y", "x", "zl", "c", "zh")
SEQ = ("y", "x", "zl", "c")
SIDE = 4
TEAMS = 16
TEAM = 8
GROUP_HEADS = 4
BF = jnp.bfloat16
F32 = jnp.float32
MESHID = pl.DeviceIdType.MESH
ANY = pl.BlockSpec(memory_space=pl.ANY)
VM = pl.BlockSpec(memory_space=pltpu.VMEM)
DMA = pltpu.SemaphoreType.DMA


def rmsnorm(values, weight):
    return values * lax.rsqrt(jnp.mean(values * values, axis=-1, keepdims=True) + EPS_NORM) * weight


def tables(positions, width):
    inverse = THETA ** (-(jnp.arange(0, width, 2).astype(jnp.float32) / width))
    angles = positions.astype(jnp.float32)[:, None] * inverse[None, :]
    angles = jnp.concatenate([angles, angles], axis=-1)
    return (jnp.cos(angles), jnp.sin(angles))


def rotate(values, cosine, sine):
    half = values.shape[-1] // 2
    turned = jnp.concatenate([-values[..., half:], values[..., :half]], axis=-1)
    return values * cosine + turned * sine


def prepare(query_raw, key_raw, gain_query, gain_key, cosine, sine):
    query_rot = rotate(rmsnorm(query_raw, gain_query), cosine[:, None, :], sine[:, None, :])
    key_rot = rotate(rmsnorm(key_raw, gain_key), cosine, sine)
    return (query_rot, key_rot)


def swiglu(both):
    half = both.shape[-1] // 2
    return jax.nn.silu(both[:, :half]) * both[:, half:]


def adamw(master, gradient, first, second, rate):
    moment = BETA_ONE * first + (1.0 - BETA_ONE) * gradient
    squares = BETA_TWO * second + (1.0 - BETA_TWO) * gradient * gradient
    scaled_one = moment / (1.0 - BETA_ONE**STEP)
    scaled_two = squares / (1.0 - BETA_TWO**STEP)
    updated = master - rate * (scaled_one / (jnp.sqrt(scaled_two) + ADAM_EPS) + DECAY * master)
    return (moment, squares, updated)


def here():
    return {a: lax.axis_index(a) for a in AXES}


def moved(at, axis, step=1):
    to = dict(at)
    if axis == "z":
        z = lax.rem(at["zh"] * 2 + at["zl"] + step + SIDE, SIDE)
        to["zh"] = z // 2
        to["zl"] = lax.rem(z, 2)
    elif axis == "quad":
        if step & 1:
            to["c"] = 1 - at["c"]
        if step & 2:
            to["zl"] = 1 - at["zl"]
    elif axis == "c":
        to["c"] = 1 - at["c"]
    else:
        to[axis] = lax.rem(at[axis] + step + SIDE, SIDE)
    return to


def ident(at):
    return tuple(at[a] for a in AXES)


def greet(at, moves):
    barrier = pltpu.get_barrier_semaphore()
    for axis, step in moves:
        pl.semaphore_signal(
            barrier, inc=1, device_id=ident(moved(at, axis, step)), device_id_type=MESHID
        )
    pl.semaphore_wait(barrier, len(moves))


def remote(src, dst, ssem, rsem, to):
    return pltpu.make_async_remote_copy(
        src_ref=src,
        dst_ref=dst,
        send_sem=ssem,
        recv_sem=rsem,
        device_id=ident(to),
        device_id_type=MESHID,
    )


def params(cid, vmem=48):
    return pltpu.CompilerParams(
        collective_id=cid, has_side_effects=True, vmem_limit_bytes=vmem << 20
    )


def place(z, c):
    return (lax.rem(z, 2) * 2 + c) * 2 + z // 2


QUAD = (("quad", 1), ("quad", 2), ("quad", 3))
NEAR = (("x", 1), ("x", -1), ("y", 1), ("y", -1))
FAR = tuple((axis, step) for axis in ("x", "y") for step in (1, 2, 3))
RING = (("z", 1), ("z", -1), ("z", 2), ("c", 1))


class Spread:
    def __init__(self, at, first, second, out, lo, rows, ssem, rsem):
        self.at, self.f, self.s, self.out = at, first, second, out
        self.lo, self.rows, self.ssem, self.rsem = lo, rows, ssem, rsem
        self.sent = []

    def slot(self, df, ds, part=None):
        f = lax.rem(self.at[self.f] + df + SIDE, SIDE)
        s = lax.rem(self.at[self.s] + ds + SIDE, SIDE)
        y, x = (f, s) if self.f == "y" else (s, f)
        lo, n = self.lo, self.rows
        if part is not None:
            n = n // 2
            lo = lo + part * n
        return self.out.at[y * SIDE + x, pl.ds(lo, n)]

    def send(self, block, k, axis, step):
        copy = remote(block, block, self.ssem.at[k], self.rsem.at[k], moved(self.at, axis, step))
        copy.start()
        self.sent.append(copy)

    def wait(self, block, k):
        to = moved(self.at, self.f, 1)
        remote(block, block, self.ssem.at[k], self.rsem.at[k], to).wait_recv()

    def one_a(self):
        self.send(self.slot(0, 0), 0, self.f, 1)
        self.send(self.slot(0, 0), 1, self.f, -1)

    def one_b(self, side):
        df = -1 if side == 0 else 1
        self.wait(self.slot(df, 0), side)
        self.send(self.slot(df, 0, side), 2 + side, self.f, -df)

    def one_c(self):
        self.wait(self.slot(2, 0, 0), 2)
        self.wait(self.slot(2, 0, 1), 3)

    STEPS = (0, -1, 1, 2)

    def two_a(self, j):
        block = self.slot(self.STEPS[j], 0)
        self.send(block, 4 + 4 * j, self.s, 1)
        self.send(block, 5 + 4 * j, self.s, -1)

    def two_b(self, j, side):
        ds = -1 if side == 0 else 1
        self.wait(self.slot(self.STEPS[j], ds), 4 + 4 * j + side)
        self.send(self.slot(self.STEPS[j], ds, side), 6 + 4 * j + side, self.s, -ds)

    def two_c(self, j):
        self.wait(self.slot(self.STEPS[j], 2, 0), 6 + 4 * j)
        self.wait(self.slot(self.STEPS[j], 2, 1), 7 + 4 * j)

    def done(self):
        for copy in self.sent:
            copy.wait_send()


def spread_rest(halves):
    for side in (0, 1):
        for h in halves:
            h.one_b(side)
            h.two_a(1 + side)
    yield
    for side in (0, 1):
        for h in halves:
            h.two_b(0, side)
    yield
    for h in halves:
        h.one_c()
        h.two_a(3)
    yield
    for j in (1, 2, 3):
        for side in (0, 1):
            for h in halves:
                h.two_b(j, side)
        yield
    for j in range(4):
        for h in halves:
            h.two_c(j)
    for h in halves:
        h.done()


class Weights:
    def __init__(self, at, pieces, outs, ssem, rsem, qs, qr, lsem):
        self.at, self.pieces, self.outs = at, pieces, outs
        self.ssem, self.rsem, self.qs, self.qr, self.lsem = ssem, rsem, qs, qr, lsem

    def steps(self):
        at = self.at
        mine = at["y"] * SIDE + at["x"]
        quad = at["zl"] * 2 + at["c"]
        near = pl.multiple_of(at["zl"] * 64, 64)
        far = pl.multiple_of(64 - at["zl"] * 64, 64)
        quads, owned = [], []
        for k, (piece, out) in enumerate(zip(self.pieces, self.outs)):
            rows = out.at[mine, pl.ds(pl.multiple_of(quad * 32, 32), 32)]
            local = pltpu.make_async_copy(piece.at[quad], rows, self.lsem.at[k])
            local.start()
            owned.append(local)
            for step in (1, 2, 3):
                to = moved(at, "quad", step)
                copy = remote(
                    piece.at[to["zl"] * 2 + to["c"]],
                    rows,
                    self.qs.at[k, step - 1],
                    self.qr.at[k, step - 1],
                    to,
                )
                copy.start()
                quads.append(copy)
        yield
        firsts, seconds = [], []
        for k, out in enumerate(self.outs):
            s, r = self.ssem, self.rsem
            firsts.append(Spread(at, "x", "y", out, near, 64, s.at[k, 0], r.at[k, 0]))
            seconds.append(Spread(at, "y", "x", out, far, 64, s.at[k, 1], r.at[k, 1]))
        for k, half in enumerate(firsts):
            owned[k].wait()
            quads[3 * k].wait_recv()
            half.one_a()
            half.two_a(0)
        yield
        for k, half in enumerate(seconds):
            quads[3 * k + 1].wait_recv()
            quads[3 * k + 2].wait_recv()
            half.one_a()
            half.two_a(0)
        yield
        yield from spread_rest(firsts + seconds)
        for copy in quads:
            copy.wait_send()

    @staticmethod
    def scratch(count):
        return [
            DMA((count, 2, 20)),
            DMA((count, 2, 20)),
            DMA((count, 3)),
            DMA((count, 3)),
            DMA((count,)),
        ]


def run(steps):
    for _ in steps:
        pass


class Gather:
    def __init__(self, at, first, second, src, lo, own, one, held, two, ssem, rsem, lsem):
        self.at, self.f, self.s, self.src, self.lo = at, first, second, src, lo
        self.own, self.one, self.held, self.two = own, one, held, two
        self.ssem, self.rsem, self.lsem = ssem, rsem, lsem
        self.rows = own.shape[1]

    def block(self, f, s):
        y, x = (f, s) if self.f == "y" else (s, f)
        return self.src.at[y * SIDE + x, pl.ds(self.lo, self.rows)]

    def start(self):
        self.sent, self.kept = [], []
        for d in (2, 1, 3):
            f = lax.rem(self.at[self.f] + d, SIDE)
            for s in range(SIDE):
                k = (d - 1) * 4 + s
                copy = remote(
                    self.block(f, s),
                    self.one.at[d - 1, s],
                    self.ssem.at[k],
                    self.rsem.at[k],
                    moved(self.at, self.f, d),
                )
                copy.start()
                self.sent.append((d, s, copy))
        for s in range(SIDE):
            copy = pltpu.make_async_copy(
                self.block(self.at[self.f], s), self.own.at[s], self.lsem.at[s]
            )
            copy.start()
            self.kept.append(copy)

    def middle(self):
        for copy in self.kept:
            copy.wait()
        for d, s, copy in self.sent:
            copy.wait_recv()

        def add(s, carry):
            total = self.own[s].astype(F32)
            for d in range(3):
                total = total + self.one[d, s].astype(F32)
            self.held[s] = total.astype(BF)
            return carry

        lax.fori_loop(0, SIDE, add, 0)
        for d in (2, 1, 3):
            copy = remote(
                self.held.at[lax.rem(self.at[self.s] + d, SIDE)],
                self.two.at[d - 1],
                self.ssem.at[11 + d],
                self.rsem.at[11 + d],
                moved(self.at, self.s, d),
            )
            copy.start()
            self.sent.append((d, 0, copy))

    def finish(self):
        for d, s, copy in self.sent[12:]:
            copy.wait_recv()
        total = self.held[self.at[self.s]].astype(F32)
        for d in range(3):
            total = total + self.two[d].astype(F32)
        return total

    def done(self):
        for d, s, copy in self.sent:
            copy.wait_send()


def grads_kernel(count, *refs):
    srcs, outs = refs[:count], refs[count : 2 * count]
    scratch = refs[2 * count :]
    qs, qr = scratch[-2:]
    at = here()
    quad = at["zl"] * 2 + at["c"]
    greet(at, FAR + QUAD)
    halves = []
    for k in range(count):
        own, one, held, two, total, ssem, rsem, lsem = scratch[8 * k : 8 * k + 8]
        halves.append(
            [
                Gather(
                    at,
                    f,
                    s,
                    srcs[k],
                    64 * n,
                    own.at[n],
                    one.at[n],
                    held.at[n],
                    two.at[n],
                    ssem.at[n],
                    rsem.at[n],
                    lsem.at[n],
                )
                for n, (f, s) in enumerate((("y", "x"), ("x", "y")))
            ]
        )
    for pair in halves:
        for h in pair:
            h.start()
    for pair in halves:
        for h in pair:
            h.middle()
    quads = []
    for k, pair in enumerate(halves):
        total = scratch[8 * k + 4]
        for n, h in enumerate(pair):
            total[n] = h.finish().astype(BF)
        for step in (3, 2, 1):
            to = moved(at, "quad", step)
            copy = remote(
                total.at[to["zl"], pl.ds(pl.multiple_of(to["c"] * 32, 32), 32)],
                outs[k].at[quad],
                qs.at[k, step - 1],
                qr.at[k, step - 1],
                to,
            )
            copy.start()
            quads.append(copy)
        outs[k][quad] = total[at["zl"], pl.ds(pl.multiple_of(at["c"] * 32, 32), 32)]
    for copy in quads:
        copy.wait()
    for pair in halves:
        for h in pair:
            h.done()


def reduce_grads(grads, cid):
    count = len(grads)
    scratch = []
    for g in grads:
        n = g.shape[2]
        scratch += [
            pltpu.VMEM((2, SIDE, 64, n), BF),
            pltpu.VMEM((2, 3, SIDE, 64, n), BF),
            pltpu.VMEM((2, SIDE, 64, n), BF),
            pltpu.VMEM((2, 3, 64, n), BF),
            pltpu.VMEM((2, 64, n), BF),
            DMA((2, 15)),
            DMA((2, 15)),
            DMA((2, 4)),
        ]
    scratch += [DMA((count, 3)), DMA((count, 3))]
    return pl.pallas_call(
        functools.partial(grads_kernel, count),
        out_shape=[jax.ShapeDtypeStruct((4, 32, g.shape[2]), BF) for g in grads],
        in_specs=[ANY] * count,
        out_specs=[VM] * count,
        scratch_shapes=scratch,
        compiler_params=params(cid),
    )(*grads)


def pairs_kernel(src, out, own, one, held, two, ssem, rsem, lsem):
    at = here()
    half = own.shape[2]
    greet(at, FAR)
    halves = [
        Gather(
            at,
            f,
            s,
            src,
            half * n,
            own.at[n],
            one.at[n],
            held.at[n],
            two.at[n],
            ssem.at[n],
            rsem.at[n],
            lsem.at[n],
        )
        for n, (f, s) in enumerate((("y", "x"), ("x", "y")))
    ]
    for h in halves:
        h.start()
    for h in halves:
        h.middle()
    for n, h in enumerate(halves):
        out[pl.ds(half * n, half)] = h.finish()
    for h in halves:
        h.done()


def reduce_plane(grads, cid):
    _, rows, n = grads.shape
    half = rows // 2
    return pl.pallas_call(
        pairs_kernel,
        out_shape=jax.ShapeDtypeStruct((rows, n), F32),
        in_specs=[ANY],
        out_specs=VM,
        scratch_shapes=[
            pltpu.VMEM((2, SIDE, half, n), BF),
            pltpu.VMEM((2, 3, SIDE, half, n), BF),
            pltpu.VMEM((2, SIDE, half, n), BF),
            pltpu.VMEM((2, 3, half, n), BF),
            DMA((2, 15)),
            DMA((2, 15)),
            DMA((2, 4)),
        ],
        compiler_params=params(cid),
    )(grads)


class TeamGather:
    def __init__(self, at, out, ssem, rsem):
        self.at, self.out, self.ssem, self.rsem = at, out, ssem, rsem

    def start(self, src=None):
        at, out = self.at, self.out
        c, z = at["c"], at["zh"] * 2 + at["zl"]
        mine = out.at[place(z, c)]
        src = mine if src is None else src
        self.ring = []
        for k, d in enumerate((2, 1, -1)):
            copy = remote(src, mine, self.ssem.at[k], self.rsem.at[k], moved(at, "z", d))
            copy.start()
            self.ring.append(copy)
        copy = remote(src, mine, self.ssem.at[6], self.rsem.at[6], moved(at, "c"))
        copy.start()
        self.pair = [copy]

    def forward(self):
        at, out = self.at, self.out
        c, z = at["c"], at["zh"] * 2 + at["zl"]
        for k, d in ((1, 1), (2, -1), (0, 2)):
            slot = out.at[place(lax.rem(z - d + SIDE, SIDE), c)]
            self.ring[k].wait_recv()
            copy = remote(slot, slot, self.ssem.at[3 + k], self.rsem.at[3 + k], moved(at, "c"))
            copy.start()
            self.pair.append(copy)

    def finish(self):
        for copy in self.pair:
            copy.wait_recv()

    def done(self):
        for copy in self.ring + self.pair:
            copy.wait_send()


def team_gather_kernel(src, out, ssem, rsem, lsem):
    at = here()
    greet(at, RING)
    local = pltpu.make_async_copy(src, out.at[place(at["zh"] * 2 + at["zl"], at["c"])], lsem)
    local.start()
    gather = TeamGather(at, out, ssem, rsem)
    gather.start(src)
    gather.forward()
    gather.finish()
    gather.done()
    local.wait()


def team_gather(rows, cid):
    count, width = rows.shape
    out = pl.pallas_call(
        team_gather_kernel,
        out_shape=jax.ShapeDtypeStruct((TEAM, count, width), rows.dtype),
        in_specs=[ANY],
        out_specs=ANY,
        scratch_shapes=[DMA((7,)), DMA((7,)), DMA],
        compiler_params=params(cid),
    )(rows)
    return out.reshape(TEAM * count, width)


class TeamReduce:
    ORDER = (2, 1, -1, 0)

    def __init__(self, at, part, one, held, two, ssem, rsem):
        self.at, self.part, self.one, self.held, self.two = at, part, one, held, two
        self.ssem, self.rsem = ssem, rsem

    def slot(self, d, c):
        return place(lax.rem(self.at["zh"] * 2 + self.at["zl"] + d + SIDE, SIDE), c)

    def start(self):
        self.first, self.second = [], []
        for k, d in enumerate(self.ORDER):
            copy = remote(
                self.part.at[self.slot(d, 1 - self.at["c"])],
                self.one.at[k],
                self.ssem.at[k],
                self.rsem.at[k],
                moved(self.at, "c"),
            )
            copy.start()
            self.first.append(copy)

    def middle(self):
        for k, d in enumerate(self.ORDER):
            self.first[k].wait_recv()
            if d == 0:
                continue
            mine = self.part[self.slot(d, self.at["c"])].astype(F32)
            self.held[k] = (mine + self.one[k].astype(F32)).astype(BF)
            copy = remote(
                self.held.at[k],
                self.two.at[k],
                self.ssem.at[4 + k],
                self.rsem.at[4 + k],
                moved(self.at, "z", d),
            )
            copy.start()
            self.second.append(copy)

    def finish(self):
        total = self.part[self.slot(0, self.at["c"])].astype(F32) + self.one[3].astype(F32)
        for k in (1, 2, 0):
            self.second[k].wait_recv()
            total = total + self.two[k].astype(F32)
        return total

    def done(self):
        for copy in self.first + self.second:
            copy.wait_send()

    @staticmethod
    def scratch(count, width):
        return [
            pltpu.VMEM((4, count, width), BF),
            pltpu.VMEM((3, count, width), BF),
            pltpu.VMEM((3, count, width), BF),
            DMA((7,)),
            DMA((7,)),
        ]


def team_reduce_kernel(part, out, *scratch):
    at = here()
    greet(at, RING)
    reduce = TeamReduce(at, part, *scratch)
    reduce.start()
    reduce.middle()
    out[...] = reduce.finish()
    reduce.done()


def team_reduce(part, cid):
    count, width = part.shape[0] // TEAM, part.shape[1]
    return pl.pallas_call(
        team_reduce_kernel,
        out_shape=jax.ShapeDtypeStruct((count, width), F32),
        in_specs=[VM],
        out_specs=VM,
        scratch_shapes=TeamReduce.scratch(count, width),
        compiler_params=params(cid),
    )(part.reshape(TEAM, count, width))


def sum_kernel(src, out, pair, ring, row, column, ssem, rsem):
    at = here()
    z = at["zh"] * 2 + at["zl"]
    greet(at, RING + FAR)
    out[...] = src[...]
    k = 0
    for axis, buffer, me in (
        ("c", pair, at["c"]),
        ("z", ring, z),
        ("x", row, at["x"]),
        ("y", column, at["y"]),
    ):
        buffer[me] = out[...]
        copies = []
        for step in range(1, buffer.shape[0]):
            copy = remote(
                buffer.at[me], buffer.at[me], ssem.at[k], rsem.at[k], moved(at, axis, step)
            )
            copy.start()
            copies.append(copy)
            k += 1
        for copy in copies:
            copy.wait()
        total = buffer[0]
        for n in range(1, buffer.shape[0]):
            total = total + buffer[n]
        out[...] = total


def sum_all(vector, cid):
    lines = vector.shape[0] // 128
    shape = (lines, 128)
    return pl.pallas_call(
        sum_kernel,
        out_shape=jax.ShapeDtypeStruct(shape, F32),
        in_specs=[VM],
        out_specs=VM,
        scratch_shapes=[
            pltpu.VMEM((2,) + shape, F32),
            pltpu.VMEM((4,) + shape, F32),
            pltpu.VMEM((4,) + shape, F32),
            pltpu.VMEM((4,) + shape, F32),
            DMA((10,)),
            DMA((10,)),
        ],
        compiler_params=params(cid),
    )(vector.reshape(shape)).reshape(vector.shape)


def dot_last(a, b):
    return lax.dot_general(a, b, (((1,), (1,)), ((), ())), preferred_element_type=F32)


def dot_first(a, b):
    return lax.dot_general(a, b, (((0,), (0,)), ((), ())), preferred_element_type=F32)


def lanes_of(value):
    return lax.broadcasted_iota(jnp.int32, value.shape, 1)


def turn(value):
    low = lax.rem(lanes_of(value), 64) < 32
    return jnp.where(low, -pltpu.roll(value, 96, 1), pltpu.roll(value, 32, 1))


def normalize(value):
    left = lanes_of(value) < 64
    square = value * value
    one = jnp.sum(jnp.where(left, square, 0.0), axis=-1, keepdims=True)
    two = jnp.sum(jnp.where(left, 0.0, square), axis=-1, keepdims=True)
    return value * lax.rsqrt(jnp.where(left, one, two) / HD + EPS_NORM)


def forward_kernel(*refs):
    (x_ref, ct_ref, gains_ref, heads_ref, cos_ref, sin_ref, segc_ref, segr_ref, main_ref) = refs[:9]
    pieces = refs[9:13]
    (rows_out, grads_out, joined_out, output_out, expand_out, reduce_out) = refs[13:19]
    (projected_out, queries_out, every_out, out_ref, sum_ref, attn_out, middle_out, ffn_out) = refs[
        19:27
    ]
    part = refs[27]
    reduce_scratch = refs[28:33]
    small_scratch, large_scratch = refs[33:38], refs[38:43]
    ks, kr, gs, gr, lsem = refs[43:]
    at = here()
    team = at["y"] * SIDE + at["x"]
    me = place(at["zh"] * 2 + at["zl"], at["c"])
    rows = queries_out.shape[1]
    greet(at, RING + NEAR + QUAD[1:2] + QUAD[2:])

    small = Weights(at, pieces[:2], [joined_out, output_out], *small_scratch).steps()
    large = Weights(at, pieces[2:], [expand_out, reduce_out], *large_scratch).steps()
    next(small)

    residual = x_ref[...].astype(F32)
    scale = lax.rsqrt(jnp.mean(residual * residual, axis=-1, keepdims=True) + EPS_NORM)
    rows_out[me] = (residual * scale * gains_ref[0:1]).astype(BF)
    gather = TeamGather(at, rows_out, gs.at[0], gr.at[0])
    gather.start()
    run(small)
    gather.forward()
    next(large)
    gather.finish()
    local = pltpu.make_async_copy(ct_ref, grads_out.at[me], lsem)
    local.start()
    cotangents = TeamGather(at, grads_out, gs.at[1], gr.at[1])
    cotangents.start(ct_ref)

    projected_out[...] = jnp.dot(
        rows_out[...].reshape(rows, D),
        joined_out[...].reshape(D, 384),
        preferred_element_type=F32,
    )
    next(large)
    cosine, sine = cos_ref[...], sin_ref[...]
    left = lax.broadcasted_iota(jnp.int32, (rows, 128), 1) < 64
    raw = projected_out[:, 256:]
    key = normalize(raw) * heads_ref[1:2]
    key = key * cosine + turn(key) * sine
    every_out[team] = jnp.where(left, key, raw).astype(BF)
    halves = [
        Spread(at, "x", "y", every_out, 0, rows // 2, ks.at[0], kr.at[0]),
        Spread(at, "y", "x", every_out, rows // 2, rows // 2, ks.at[1], kr.at[1]),
    ]
    for h in halves:
        h.one_a()
        h.two_a(0)
    for n in range(2):
        query = normalize(projected_out[:, 128 * n : 128 * n + 128]) * heads_ref[0:1]
        query = query * cosine + turn(query) * sine
        query = query.astype(BF).astype(F32) * (HD**-0.5)
        queries_out[2 * n] = jnp.where(left, query, 0.0).astype(BF)
        queries_out[2 * n + 1] = jnp.where(left, pltpu.roll(query, 64, 1), 0.0).astype(BF)
    cotangents.forward()
    run(spread_rest(halves))
    next(large)

    out_ref[...] = jnp.zeros_like(out_ref)
    sum_ref[...] = jnp.zeros_like(sum_ref)

    def block(number, allowed):
        pairs = every_out[number]
        for h in range(GROUP_HEADS):
            weights = jnp.exp(dot_last(queries_out[h], pairs))
            if allowed is not None:
                weights = jnp.where(allowed, weights, 0.0)
            add = weights[:, :128]
            for lane in range(128, rows, 128):
                add = add + weights[:, lane : lane + 128]
            sum_ref[h] += add
            out_ref[h] += jnp.dot(weights.astype(BF), pairs, preferred_element_type=F32)

    def inner(number, carry):
        block(number, None)
        return carry

    lax.fori_loop(1, jnp.maximum(team - 6, 1), inner, 0)
    next(large)
    lax.fori_loop(jnp.maximum(team - 6, 1), team, inner, 0)
    next(large)
    for h in range(GROUP_HEADS):
        out_ref[h] *= main_ref[...]
        sum_ref[h] *= main_ref[...]

    def edge(step, carry):
        number = step * team
        ahead = (number - team) * rows
        row = lax.broadcasted_iota(jnp.int32, (rows, rows), 0)
        column = lax.broadcasted_iota(jnp.int32, (rows, rows), 1) + ahead
        block(number, (column <= row) & (segc_ref[...] == segr_ref[number]))
        return carry

    lax.fori_loop(jnp.where(team == 0, 1, 0), 2, edge, 0)
    for h in range(GROUP_HEADS):
        total = jnp.sum(sum_ref[h], axis=-1, keepdims=True)
        sum_ref[h] = jnp.broadcast_to(total, sum_ref.shape[1:])
        out_ref[h] = out_ref[h] / sum_ref[h]
    for n in range(2):
        one, two = out_ref[2 * n], out_ref[2 * n + 1]
        attn_out[:, 128 * n : 128 * n + 128] = jnp.where(left, pltpu.roll(one, 64, 1), two).astype(BF)

    def project(n, carry):
        columns = pl.ds(pl.multiple_of(n * 512, 512), 512)
        weight = output_out[pl.ds(n * 4, 4)].reshape(512, 256)
        branch = dot_last(attn_out[...], weight).astype(BF)
        part[:, :, columns] = branch.reshape(TEAM, 64, 512)
        return carry

    lax.fori_loop(0, 4, project, 0)
    branch = TeamReduce(at, part, *reduce_scratch)
    branch.start()
    branch.middle()
    next(large)
    middle = residual + branch.finish()
    middle_out[...] = middle
    scale = lax.rsqrt(jnp.mean(middle * middle, axis=-1, keepdims=True) + EPS_NORM)
    ffn_out[me] = (middle * scale * gains_ref[1:2]).astype(BF)
    second = TeamGather(at, ffn_out, gs.at[2], gr.at[2])
    second.start()
    next(large)
    second.forward()
    next(large)
    second.finish()
    run(large)
    cotangents.finish()
    local.wait()
    for transfer in (gather, cotangents, second, branch):
        transfer.done()


def forward(x, ct, gains, heads, cosine, sine, seg_columns, seg_rows, main, pieces, cid):
    rows = TEAM * 64

    def out(shape, kind=BF):
        return jax.ShapeDtypeStruct(shape, kind)

    return pl.pallas_call(
        forward_kernel,
        out_shape=[
            out((TEAM, 64, D)),
            out((TEAM, 64, D)),
            out((TEAMS, 128, 384)),
            out((TEAMS, 128, 256)),
            out((TEAMS, 128, 2048)),
            out((TEAMS, 128, 1024)),
            out((rows, 384), F32),
            out((GROUP_HEADS, rows, 128)),
            out((TEAMS, rows, 128)),
            out((GROUP_HEADS, rows, 128), F32),
            out((GROUP_HEADS, rows, 128), F32),
            out((rows, 256)),
            out((64, D), F32),
            out((TEAM, 64, D)),
        ],
        in_specs=[VM, ANY] + [VM] * 7 + [ANY] * 4,
        out_specs=[VM, ANY, VM, VM, ANY, ANY] + [VM] * 8,
        scratch_shapes=[pltpu.VMEM((TEAM, 64, D), BF)]
        + TeamReduce.scratch(64, D)
        + Weights.scratch(2)
        + Weights.scratch(2)
        + [DMA((2, 20)), DMA((2, 20)), DMA((3, 7)), DMA((3, 7)), DMA],
        compiler_params=params(cid, 56),
    )(x, ct, gains, heads, cosine, sine, seg_columns, seg_rows, main, *pieces)


def attend_back_kernel(
    q_ref,
    do_ref,
    inner_ref,
    kv_ref,
    segc_ref,
    segr_ref,
    mainc_ref,
    mainr_ref,
    dq_ref,
    dkv_ref,
    qm_ref,
    dom_ref,
    innerm_ref,
):
    team = lax.axis_index("y") * SIDE + lax.axis_index("x")
    rows = q_ref.shape[1]
    dq_ref[...] = jnp.zeros_like(dq_ref)
    low = mainc_ref[...].astype(BF)
    for h in range(GROUP_HEADS):
        qm_ref[h] = q_ref[h] * low
        dom_ref[h] = do_ref[h] * low
        innerm_ref[h] = inner_ref[h] * mainr_ref[...]

    def block(number, allowed, q, do, inner):
        pairs = kv_ref[number]
        total = jnp.zeros(pairs.shape, F32)
        for h in range(GROUP_HEADS):
            weights = jnp.exp(dot_last(pairs, q[h]))
            if allowed is not None:
                weights = jnp.where(allowed, weights, 0.0)
            grad = (weights * (dot_last(pairs, do[h]) - inner[h])).astype(BF)
            total = total + jnp.dot(grad, q[h], preferred_element_type=F32)
            total = total + jnp.dot(weights.astype(BF), do[h], preferred_element_type=F32)
            dq_ref[h] += dot_first(pairs, grad)
        dkv_ref[number] = total.astype(BF)

    def interior(number, carry):
        block(number, None, qm_ref, dom_ref, innerm_ref)
        return carry

    lax.fori_loop(1, team, interior, 0)

    def edge(step, carry):
        number = step * team
        ahead = (number - team) * rows
        row = lax.broadcasted_iota(jnp.int32, (rows, rows), 1)
        column = lax.broadcasted_iota(jnp.int32, (rows, rows), 0) + ahead
        allowed = (column <= row) & (segc_ref[number] == segr_ref[...])
        block(number, allowed, q_ref, do_ref, inner_ref)
        return carry

    lax.fori_loop(jnp.where(team == 0, 1, 0), 2, edge, 0)

    def rest(number, carry):
        dkv_ref[number] = jnp.zeros(dkv_ref.shape[1:], BF)
        return carry

    lax.fori_loop(team + 1, TEAMS, rest, 0)


def attend_back(queries, grads, inner, every, seg_columns, seg_rows, main_column, main_row):
    rows = queries.shape[1]
    return pl.pallas_call(
        attend_back_kernel,
        out_shape=[
            jax.ShapeDtypeStruct((GROUP_HEADS, 128, rows), F32),
            jax.ShapeDtypeStruct(every.shape, BF),
        ],
        in_specs=[VM] * 8,
        out_specs=[VM] * 2,
        scratch_shapes=[
            pltpu.VMEM(queries.shape, BF),
            pltpu.VMEM(grads.shape, BF),
            pltpu.VMEM(inner.shape, F32),
        ],
        compiler_params=pltpu.CompilerParams(vmem_limit_bytes=48 << 20),
    )(queries, grads, inner, every, seg_columns, seg_rows, main_column, main_row)


def matmul(a, b, contract, kind=F32):
    return lax.dot_general(a, b, ((contract[:1], contract[1:]), ((), ())), preferred_element_type=F32).astype(kind)


def on_device(
    block_in,
    cotangent,
    segments,
    gains,
    joined_weight,
    output_weight,
    expand_weight,
    reduce_weight,
    gains_first,
    gains_squares,
    joined_first,
    joined_squares,
    output_first,
    output_squares,
    expand_first,
    expand_squares,
    reduce_first,
    reduce_squares,
):
    model, width = D, HD
    factor = width ** (-0.5)
    team = lax.axis_index("y") * SIDE + lax.axis_index("x")
    gain_attn = gains[:model]
    gain_ffn = gains[model : 2 * model]
    gain_query = gains[2 * model : 2 * model + width]
    gain_key = gains[2 * model + width :]

    joined_pieces = joined_weight.astype(BF).transpose(1, 0, 2)
    output_pieces = output_weight.astype(BF).reshape(32, 4, 256).transpose(1, 0, 2)
    expand_pieces = (
        expand_weight.astype(BF).reshape(32, 2, 4, 1024).transpose(2, 0, 1, 3).reshape(4, 32, 2048)
    )
    reduce_pieces = reduce_weight.astype(BF).reshape(32, 4, 1024).transpose(1, 0, 2)
    rows = TEAM * 64
    first_row = team * rows
    query_index = first_row + jnp.arange(rows, dtype=jnp.int32)
    cosine, sine = tables(query_index, width)
    query_seg = lax.dynamic_slice_in_dim(segments, first_row, rows)
    main = (query_seg == segments[127]).astype(F32)
    seg_blocks = segments.reshape(TEAMS, rows)
    (
        attn_rows,
        grad_rows,
        joined_all,
        output_all,
        expand_all,
        reduce_all,
        projected,
        queries,
        every,
        attended,
        total,
        attn_out,
        middle,
        ffn_rows,
    ) = forward(
        block_in,
        cotangent,
        jnp.stack([gain_attn, gain_ffn]),
        jnp.stack([jnp.tile(gain_query, 2), jnp.tile(gain_key, 2)]),
        jnp.tile(cosine, (1, 2)),
        jnp.tile(sine, (1, 2)),
        query_seg[:, None],
        seg_blocks[:, None, :],
        main[:, None],
        [joined_pieces, output_pieces, expand_pieces, reduce_pieces],
        1,
    )
    attn_rows, grad_rows, ffn_rows = (v.reshape(rows, D) for v in (attn_rows, grad_rows, ffn_rows))
    joined_all, output_all, expand_all, reduce_all = (
        v.reshape(D, -1) for v in (joined_all, output_all, expand_all, reduce_all)
    )
    residual = block_in.astype(F32)
    _, norm_one_back = jax.vjp(rmsnorm, residual, gain_attn)
    _, norm_two_back = jax.vjp(rmsnorm, middle, gain_ffn)
    query_raw = projected[:, : GROUP_HEADS * width].reshape(rows, GROUP_HEADS, width)
    key_raw = projected[:, GROUP_HEADS * width : (GROUP_HEADS + 1) * width]

    def prepared(query_part, key_part, query_gain, key_gain):
        return prepare(query_part, key_part, query_gain, key_gain, cosine, sine)

    _, prep_back = jax.vjp(prepared, query_raw, key_raw, gain_query, gain_key)
    total = total[:, :, :1]
    attended = attended[:, :, width:]
    both = matmul(ffn_rows, expand_all, (1, 0))
    hidden, swiglu_back = jax.vjp(swiglu, both)
    hidden_low = hidden.astype(BF)
    branch_two = matmul(hidden_low, reduce_all, (1, 1), BF)
    grad_out = cotangent.astype(F32)
    grad_reduce = matmul(grad_rows, hidden_low, (0, 0), BF)
    grad_hidden = matmul(grad_rows, reduce_all, (1, 0))
    (grad_both,) = swiglu_back(grad_hidden)
    grad_both_low = grad_both.astype(BF)
    grad_expand = matmul(ffn_rows, grad_both_low, (0, 0), BF)
    grad_ffn_rows = team_reduce(matmul(grad_both_low, expand_all, (1, 1), BF), 5)
    block_out = (middle + team_reduce(branch_two, 5)).astype(BF)
    grad_middle_norm, grad_gain_ffn = norm_two_back(grad_ffn_rows)
    grad_middle = grad_out + grad_middle_norm
    grad_branch = team_gather(grad_middle.astype(BF), 3)
    grad_output = matmul(grad_branch, attn_out, (0, 0), BF)
    grad_attended = matmul(grad_branch, output_all, (1, 0))
    grad_attended = grad_attended.reshape(rows, GROUP_HEADS, width).transpose(1, 0, 2)
    scaled = (grad_attended / total).astype(BF)
    inner = jnp.sum(scaled.astype(F32) * attended, axis=-1)
    scaled = jnp.pad(scaled, ((0, 0), (0, 0), (128 - width, 0)))
    grad_queries, grad_blocks = attend_back(
        queries,
        scaled,
        inner[:, None, :],
        every,
        seg_blocks[:, :, None],
        query_seg[None, :],
        main[:, None],
        main[None, :],
    )
    own_grad = reduce_plane(grad_blocks, 6)
    grad_queries = grad_queries[:, :width].transpose(2, 0, 1) * factor
    grad_query_raw, grad_key_raw, grad_gain_query, grad_gain_key = prep_back(
        (grad_queries, own_grad[:, :width])
    )
    grad_projected = jnp.concatenate(
        [grad_query_raw.reshape(rows, GROUP_HEADS * width), grad_key_raw, own_grad[:, width:]],
        axis=-1,
    ).astype(BF)
    grad_joined = matmul(attn_rows, grad_projected, (0, 0), BF)
    grad_attn_rows = team_reduce(matmul(grad_projected, joined_all, (1, 1), BF), 5)
    grad_res_norm, grad_gain_attn = norm_one_back(grad_attn_rows)
    input_grad = (grad_middle + grad_res_norm).astype(BF)
    gain_grad = sum_all(
        jnp.concatenate([grad_gain_attn, grad_gain_ffn, grad_gain_query, grad_gain_key]), 7
    )

    def blocks(grad):
        return grad.reshape(TEAMS, 128, -1)

    shard_expand, shard_reduce = reduce_grads([blocks(grad_expand), blocks(grad_reduce)], 8)
    shard_joined, shard_output = reduce_grads([blocks(grad_joined), blocks(grad_output)], 9)
    shard_joined = shard_joined.transpose(1, 0, 2).astype(F32)
    shard_output = shard_output.transpose(1, 0, 2).reshape(32, 1024).astype(F32)
    shard_expand = (
        shard_expand.reshape(4, 32, 2, 1024).transpose(1, 2, 0, 3).reshape(32, 2, 4096).astype(F32)
    )
    shard_reduce = shard_reduce.transpose(1, 0, 2).reshape(32, 4096).astype(F32)
    joined = adamw(joined_weight, shard_joined, joined_first, joined_squares, D ** (-0.5))
    output = adamw(
        output_weight, shard_output, output_first, output_squares, max(1, H * HD // 128) ** (-0.5)
    )
    expand = adamw(expand_weight, shard_expand, expand_first, expand_squares, D ** (-0.5))
    reduce_new = adamw(reduce_weight, shard_reduce, reduce_first, reduce_squares, FF ** (-0.5))
    gain_new = adamw(gains, gain_grad, gains_first, gains_squares, GAIN_RATE)
    return (
        block_out,
        input_grad,
        joined[0],
        joined[1],
        joined[2],
        joined[2].astype(BF),
        output[0],
        output[1],
        output[2],
        output[2].astype(BF),
        expand[0],
        expand[1],
        expand[2],
        expand[2].astype(BF),
        reduce_new[0],
        reduce_new[1],
        reduce_new[2],
        reduce_new[2].astype(BF),
        gain_new[0],
        gain_new[1],
        gain_new[2],
    )


def solution(mesh):
    physical = Mesh(mesh.devices.reshape(SIDE, SIDE, 2, 2, 2), AXES)
    rows = P(AXES, None)
    joined = P(SEQ, "zh", None)
    plain = P(SEQ, "zh")
    expand = P(SEQ, None, "zh")
    placed = (
        (rows, rows, P(), P(), joined, plain, expand, plain, P(), P())
        + (joined,) * 2
        + (plain,) * 2
        + (expand,) * 2
        + (plain,) * 2
    )
    return jax.shard_map(
        on_device,
        mesh=physical,
        in_specs=placed,
        out_specs=(rows, rows)
        + (joined,) * 4
        + (plain,) * 4
        + (expand,) * 4
        + (plain,) * 4
        + (P(),) * 3,
        check_vma=False,
    )
```

```python
import functools

import jax
import jax.numpy as jnp
from jax import lax
from jax.experimental import pallas as pl
from jax.experimental.pallas import tpu as pltpu
from jax.sharding import Mesh
from jax.sharding import PartitionSpec as P

D = 2048
H = 32
HD = 64
FF = 8192
STEP = 10

EPS_NORM = 1e-05
THETA = 1000000.0
BETA_ONE = 0.5
BETA_TWO = 0.5
ADAM_EPS = 1e-08
DECAY = 0.1
GAIN_RATE = 0.2

AXES = ("y", "x", "zl", "c", "zh")
SEQ = ("y", "x", "zl", "c")
SIDE = 4
TEAMS = 16
TEAM = 8
GROUP_HEADS = 4
BF = jnp.bfloat16
F32 = jnp.float32
MESHID = pl.DeviceIdType.MESH
ANY = pl.BlockSpec(memory_space=pl.ANY)
VM = pl.BlockSpec(memory_space=pltpu.VMEM)
DMA = pltpu.SemaphoreType.DMA


def rmsnorm(values, weight):
    return values * lax.rsqrt(jnp.mean(values * values, axis=-1, keepdims=True) + EPS_NORM) * weight


def tables(positions, width):
    inverse = THETA ** (-(jnp.arange(0, width, 2).astype(jnp.float32) / width))
    angles = positions.astype(jnp.float32)[:, None] * inverse[None, :]
    angles = jnp.concatenate([angles, angles], axis=-1)
    return (jnp.cos(angles), jnp.sin(angles))


def rotate(values, cosine, sine):
    half = values.shape[-1] // 2
    turned = jnp.concatenate([-values[..., half:], values[..., :half]], axis=-1)
    return values * cosine + turned * sine


def prepare(query_raw, key_raw, gain_query, gain_key, cosine, sine):
    query_rot = rotate(rmsnorm(query_raw, gain_query), cosine[:, None, :], sine[:, None, :])
    key_rot = rotate(rmsnorm(key_raw, gain_key), cosine, sine)
    return (query_rot, key_rot)


def swiglu(both):
    half = both.shape[-1] // 2
    return jax.nn.silu(both[:, :half]) * both[:, half:]


def adamw(master, gradient, first, second, rate):
    moment = BETA_ONE * first + (1.0 - BETA_ONE) * gradient
    squares = BETA_TWO * second + (1.0 - BETA_TWO) * gradient * gradient
    scaled_one = moment / (1.0 - BETA_ONE**STEP)
    scaled_two = squares / (1.0 - BETA_TWO**STEP)
    updated = master - rate * (scaled_one / (jnp.sqrt(scaled_two) + ADAM_EPS) + DECAY * master)
    return (moment, squares, updated)


def here():
    return {a: lax.axis_index(a) for a in AXES}


def moved(at, axis, step=1):
    to = dict(at)
    if axis == "z":
        z = lax.rem(at["zh"] * 2 + at["zl"] + step + SIDE, SIDE)
        to["zh"] = z // 2
        to["zl"] = lax.rem(z, 2)
    elif axis == "quad":
        if step & 1:
            to["c"] = 1 - at["c"]
        if step & 2:
            to["zl"] = 1 - at["zl"]
    elif axis == "c":
        to["c"] = 1 - at["c"]
    else:
        to[axis] = lax.rem(at[axis] + step + SIDE, SIDE)
    return to


def ident(at):
    return tuple(at[a] for a in AXES)


def greet(at, moves):
    barrier = pltpu.get_barrier_semaphore()
    for axis, step in moves:
        pl.semaphore_signal(
            barrier, inc=1, device_id=ident(moved(at, axis, step)), device_id_type=MESHID
        )
    pl.semaphore_wait(barrier, len(moves))


def remote(src, dst, ssem, rsem, to):
    return pltpu.make_async_remote_copy(
        src_ref=src,
        dst_ref=dst,
        send_sem=ssem,
        recv_sem=rsem,
        device_id=ident(to),
        device_id_type=MESHID,
    )


def params(cid, vmem=48):
    return pltpu.CompilerParams(
        collective_id=cid, has_side_effects=True, vmem_limit_bytes=vmem << 20
    )


def place(z, c):
    return (lax.rem(z, 2) * 2 + c) * 2 + z // 2


QUAD = (("quad", 1), ("quad", 2), ("quad", 3))
NEAR = (("x", 1), ("x", -1), ("y", 1), ("y", -1))
FAR = tuple((axis, step) for axis in ("x", "y") for step in (1, 2, 3))
RING = (("z", 1), ("z", -1), ("z", 2), ("c", 1))


class Spread:
    def __init__(self, at, first, second, out, lo, rows, ssem, rsem):
        self.at, self.f, self.s, self.out = at, first, second, out
        self.lo, self.rows, self.ssem, self.rsem = lo, rows, ssem, rsem
        self.sent = []

    def slot(self, df, ds, part=None):
        f = lax.rem(self.at[self.f] + df + SIDE, SIDE)
        s = lax.rem(self.at[self.s] + ds + SIDE, SIDE)
        y, x = (f, s) if self.f == "y" else (s, f)
        lo, n = self.lo, self.rows
        if part is not None:
            n = n // 2
            lo = lo + part * n
        return self.out.at[y * SIDE + x, pl.ds(lo, n)]

    def send(self, block, k, axis, step):
        copy = remote(block, block, self.ssem.at[k], self.rsem.at[k], moved(self.at, axis, step))
        copy.start()
        self.sent.append(copy)

    def wait(self, block, k):
        to = moved(self.at, self.f, 1)
        remote(block, block, self.ssem.at[k], self.rsem.at[k], to).wait_recv()

    def one_a(self):
        self.send(self.slot(0, 0), 0, self.f, 1)
        self.send(self.slot(0, 0), 1, self.f, -1)

    def one_b(self, side):
        df = -1 if side == 0 else 1
        self.wait(self.slot(df, 0), side)
        self.send(self.slot(df, 0, side), 2 + side, self.f, -df)

    def one_c(self):
        self.wait(self.slot(2, 0, 0), 2)
        self.wait(self.slot(2, 0, 1), 3)

    STEPS = (0, -1, 1, 2)

    def two_a(self, j):
        block = self.slot(self.STEPS[j], 0)
        self.send(block, 4 + 4 * j, self.s, 1)
        self.send(block, 5 + 4 * j, self.s, -1)

    def two_b(self, j, side):
        ds = -1 if side == 0 else 1
        self.wait(self.slot(self.STEPS[j], ds), 4 + 4 * j + side)
        self.send(self.slot(self.STEPS[j], ds, side), 6 + 4 * j + side, self.s, -ds)

    def two_c(self, j):
        self.wait(self.slot(self.STEPS[j], 2, 0), 6 + 4 * j)
        self.wait(self.slot(self.STEPS[j], 2, 1), 7 + 4 * j)

    def done(self):
        for copy in self.sent:
            copy.wait_send()


def spread_rest(halves):
    for side in (0, 1):
        for h in halves:
            h.one_b(side)
            h.two_a(1 + side)
    yield
    for side in (0, 1):
        for h in halves:
            h.two_b(0, side)
    yield
    for h in halves:
        h.one_c()
        h.two_a(3)
    yield
    for j in (1, 2, 3):
        for side in (0, 1):
            for h in halves:
                h.two_b(j, side)
        yield
    for j in range(4):
        for h in halves:
            h.two_c(j)
    for h in halves:
        h.done()


class Weights:
    def __init__(self, at, pieces, outs, ssem, rsem, qs, qr, lsem):
        self.at, self.pieces, self.outs = at, pieces, outs
        self.ssem, self.rsem, self.qs, self.qr, self.lsem = ssem, rsem, qs, qr, lsem

    def steps(self):
        at = self.at
        mine = at["y"] * SIDE + at["x"]
        quad = at["zl"] * 2 + at["c"]
        near = pl.multiple_of(at["zl"] * 64, 64)
        far = pl.multiple_of(64 - at["zl"] * 64, 64)
        quads, owned = [], []
        for k, (piece, out) in enumerate(zip(self.pieces, self.outs)):
            rows = out.at[mine, pl.ds(pl.multiple_of(quad * 32, 32), 32)]
            local = pltpu.make_async_copy(piece.at[quad], rows, self.lsem.at[k])
            local.start()
            owned.append(local)
            for step in (1, 2, 3):
                to = moved(at, "quad", step)
                copy = remote(
                    piece.at[to["zl"] * 2 + to["c"]],
                    rows,
                    self.qs.at[k, step - 1],
                    self.qr.at[k, step - 1],
                    to,
                )
                copy.start()
                quads.append(copy)
        yield
        firsts, seconds = [], []
        for k, out in enumerate(self.outs):
            s, r = self.ssem, self.rsem
            firsts.append(Spread(at, "x", "y", out, near, 64, s.at[k, 0], r.at[k, 0]))
            seconds.append(Spread(at, "y", "x", out, far, 64, s.at[k, 1], r.at[k, 1]))
        for k, half in enumerate(firsts):
            owned[k].wait()
            quads[3 * k].wait_recv()
            half.one_a()
            half.two_a(0)
        yield
        for k, half in enumerate(seconds):
            quads[3 * k + 1].wait_recv()
            quads[3 * k + 2].wait_recv()
            half.one_a()
            half.two_a(0)
        yield
        yield from spread_rest(firsts + seconds)
        for copy in quads:
            copy.wait_send()

    @staticmethod
    def scratch(count):
        return [
            DMA((count, 2, 20)),
            DMA((count, 2, 20)),
            DMA((count, 3)),
            DMA((count, 3)),
            DMA((count,)),
        ]


def run(steps):
    for _ in steps:
        pass


class Gather:
    def __init__(self, at, first, second, src, lo, own, one, held, two, ssem, rsem, lsem):
        self.at, self.f, self.s, self.src, self.lo = at, first, second, src, lo
        self.own, self.one, self.held, self.two = own, one, held, two
        self.ssem, self.rsem, self.lsem = ssem, rsem, lsem
        self.rows = own.shape[1]

    def block(self, f, s):
        y, x = (f, s) if self.f == "y" else (s, f)
        return self.src.at[y * SIDE + x, pl.ds(self.lo, self.rows)]

    def start(self):
        self.sent, self.kept = [], []
        for d in (2, 1, 3):
            f = lax.rem(self.at[self.f] + d, SIDE)
            for s in range(SIDE):
                k = (d - 1) * 4 + s
                copy = remote(
                    self.block(f, s),
                    self.one.at[d - 1, s],
                    self.ssem.at[k],
                    self.rsem.at[k],
                    moved(self.at, self.f, d),
                )
                copy.start()
                self.sent.append((d, s, copy))
        for s in range(SIDE):
            copy = pltpu.make_async_copy(
                self.block(self.at[self.f], s), self.own.at[s], self.lsem.at[s]
            )
            copy.start()
            self.kept.append(copy)

    def middle(self):
        for copy in self.kept:
            copy.wait()
        for d, s, copy in self.sent:
            copy.wait_recv()

        def add(s, carry):
            total = self.own[s].astype(F32)
            for d in range(3):
                total = total + self.one[d, s].astype(F32)
            self.held[s] = total.astype(BF)
            return carry

        lax.fori_loop(0, SIDE, add, 0)
        for d in (2, 1, 3):
            copy = remote(
                self.held.at[lax.rem(self.at[self.s] + d, SIDE)],
                self.two.at[d - 1],
                self.ssem.at[11 + d],
                self.rsem.at[11 + d],
                moved(self.at, self.s, d),
            )
            copy.start()
            self.sent.append((d, 0, copy))

    def finish(self):
        for d, s, copy in self.sent[12:]:
            copy.wait_recv()
        total = self.held[self.at[self.s]].astype(F32)
        for d in range(3):
            total = total + self.two[d].astype(F32)
        return total

    def done(self):
        for d, s, copy in self.sent:
            copy.wait_send()


class Grads:
    def __init__(self, at, src, out, own, one, held, two, total, ssem, rsem, lsem, qs, qr):
        self.at, self.out, self.total, self.qs, self.qr = at, out, total, qs, qr
        self.halves = [
            Gather(
                at,
                f,
                s,
                src,
                64 * n,
                own.at[n],
                one.at[n],
                held.at[n],
                two.at[n],
                ssem.at[n],
                rsem.at[n],
                lsem.at[n],
            )
            for n, (f, s) in enumerate((("y", "x"), ("x", "y")))
        ]

    def start(self):
        for h in self.halves:
            h.start()

    def middle(self):
        for h in self.halves:
            h.middle()

    def finish(self):
        at, total = self.at, self.total
        quad = at["zl"] * 2 + at["c"]
        for n, h in enumerate(self.halves):
            total[n] = h.finish().astype(BF)
        self.quads = []
        for step in (3, 2, 1):
            to = moved(at, "quad", step)
            copy = remote(
                total.at[to["zl"], pl.ds(pl.multiple_of(to["c"] * 32, 32), 32)],
                self.out.at[quad],
                self.qs.at[step - 1],
                self.qr.at[step - 1],
                to,
            )
            copy.start()
            self.quads.append(copy)
        self.out[quad] = total[at["zl"], pl.ds(pl.multiple_of(at["c"] * 32, 32), 32)]

    def done(self):
        for copy in self.quads:
            copy.wait()
        for h in self.halves:
            h.done()

    @staticmethod
    def scratch(n):
        return [
            pltpu.VMEM((2, SIDE, 64, n), BF),
            pltpu.VMEM((2, 3, SIDE, 64, n), BF),
            pltpu.VMEM((2, SIDE, 64, n), BF),
            pltpu.VMEM((2, 3, 64, n), BF),
            pltpu.VMEM((2, 64, n), BF),
            DMA((2, 15)),
            DMA((2, 15)),
            DMA((2, 4)),
            DMA((3,)),
            DMA((3,)),
        ]


class TeamGather:
    def __init__(self, at, out, ssem, rsem):
        self.at, self.out, self.ssem, self.rsem = at, out, ssem, rsem

    def start(self, src=None):
        at, out = self.at, self.out
        c, z = at["c"], at["zh"] * 2 + at["zl"]
        mine = out.at[place(z, c)]
        src = mine if src is None else src
        self.ring = []
        for k, d in enumerate((2, 1, -1)):
            copy = remote(src, mine, self.ssem.at[k], self.rsem.at[k], moved(at, "z", d))
            copy.start()
            self.ring.append(copy)
        copy = remote(src, mine, self.ssem.at[6], self.rsem.at[6], moved(at, "c"))
        copy.start()
        self.pair = [copy]

    def forward(self):
        at, out = self.at, self.out
        c, z = at["c"], at["zh"] * 2 + at["zl"]
        for k, d in ((1, 1), (2, -1), (0, 2)):
            slot = out.at[place(lax.rem(z - d + SIDE, SIDE), c)]
            self.ring[k].wait_recv()
            copy = remote(slot, slot, self.ssem.at[3 + k], self.rsem.at[3 + k], moved(at, "c"))
            copy.start()
            self.pair.append(copy)

    def finish(self):
        for copy in self.pair:
            copy.wait_recv()

    def done(self):
        for copy in self.ring + self.pair:
            copy.wait_send()


class TeamReduce:
    ORDER = (2, 1, -1, 0)

    def __init__(self, at, part, one, held, two, ssem, rsem):
        self.at, self.part, self.one, self.held, self.two = at, part, one, held, two
        self.ssem, self.rsem = ssem, rsem

    def slot(self, d, c):
        return place(lax.rem(self.at["zh"] * 2 + self.at["zl"] + d + SIDE, SIDE), c)

    def start(self):
        self.first, self.second = [], []
        for k, d in enumerate(self.ORDER):
            copy = remote(
                self.part.at[self.slot(d, 1 - self.at["c"])],
                self.one.at[k],
                self.ssem.at[k],
                self.rsem.at[k],
                moved(self.at, "c"),
            )
            copy.start()
            self.first.append(copy)

    def middle(self):
        for k, d in enumerate(self.ORDER):
            self.first[k].wait_recv()
            if d == 0:
                continue
            mine = self.part[self.slot(d, self.at["c"])].astype(F32)
            self.held[k] = (mine + self.one[k].astype(F32)).astype(BF)
            copy = remote(
                self.held.at[k],
                self.two.at[k],
                self.ssem.at[4 + k],
                self.rsem.at[4 + k],
                moved(self.at, "z", d),
            )
            copy.start()
            self.second.append(copy)

    def finish(self):
        total = self.part[self.slot(0, self.at["c"])].astype(F32) + self.one[3].astype(F32)
        for k in (1, 2, 0):
            self.second[k].wait_recv()
            total = total + self.two[k].astype(F32)
        return total

    def done(self):
        for copy in self.first + self.second:
            copy.wait_send()

    @staticmethod
    def scratch(count, width):
        return [
            pltpu.VMEM((4, count, width), BF),
            pltpu.VMEM((3, count, width), BF),
            pltpu.VMEM((3, count, width), BF),
            DMA((7,)),
            DMA((7,)),
        ]


class Sum:
    def __init__(self, at, value, pair, ring, row, column, ssem, rsem):
        self.at, self.value, self.ssem, self.rsem = at, value, ssem, rsem
        self.axes = (
            ("c", pair, at["c"]),
            ("z", ring, at["zh"] * 2 + at["zl"]),
            ("x", row, at["x"]),
            ("y", column, at["y"]),
        )

    def steps(self):
        k = 0
        for axis, buffer, me in self.axes:
            buffer[me] = self.value[...]
            copies = []
            for step in range(1, buffer.shape[0]):
                copy = remote(
                    buffer.at[me],
                    buffer.at[me],
                    self.ssem.at[k],
                    self.rsem.at[k],
                    moved(self.at, axis, step),
                )
                copy.start()
                copies.append(copy)
                k += 1
            yield
            for copy in copies:
                copy.wait()
            total = buffer[0]
            for n in range(1, buffer.shape[0]):
                total = total + buffer[n]
            self.value[...] = total

    @staticmethod
    def scratch(shape):
        return [pltpu.VMEM((n,) + shape, F32) for n in (2, 4, 4, 4)] + [DMA((10,)), DMA((10,))]


def dot_plain(a, b):
    return jnp.dot(a, b, preferred_element_type=F32)


def dot_last(a, b):
    return lax.dot_general(a, b, (((1,), (1,)), ((), ())), preferred_element_type=F32)


def dot_first(a, b):
    return lax.dot_general(a, b, (((0,), (0,)), ((), ())), preferred_element_type=F32)


def lanes_of(value):
    return lax.broadcasted_iota(jnp.int32, value.shape, 1)


def turn(value):
    low = lax.rem(lanes_of(value), 64) < 32
    return jnp.where(low, -pltpu.roll(value, 96, 1), pltpu.roll(value, 32, 1))


def normalize(value):
    left = lanes_of(value) < 64
    square = value * value
    one = jnp.sum(jnp.where(left, square, 0.0), axis=-1, keepdims=True)
    two = jnp.sum(jnp.where(left, 0.0, square), axis=-1, keepdims=True)
    return value * lax.rsqrt(jnp.where(left, one, two) / HD + EPS_NORM)


def forward_kernel(*refs):
    (x_ref, ct_ref, gains_ref, heads_ref, cos_ref, sin_ref, segc_ref, segr_ref, main_ref) = refs[:9]
    pieces = refs[9:13]
    (rows_out, grads_out, joined_out, output_out, expand_out, reduce_out) = refs[13:19]
    (projected_out, queries_out, every_out, out_ref, attn_out, middle_out, ffn_out) = refs[19:26]
    sum_ref, part = refs[26:28]
    reduce_scratch = refs[28:33]
    small_scratch, large_scratch = refs[33:38], refs[38:43]
    ks, kr, gs, gr, lsem = refs[43:]
    at = here()
    team = at["y"] * SIDE + at["x"]
    me = place(at["zh"] * 2 + at["zl"], at["c"])
    rows = queries_out.shape[1]
    greet(at, RING + NEAR + QUAD[1:2] + QUAD[2:])

    small = Weights(at, pieces[:2], [joined_out, output_out], *small_scratch).steps()
    large = Weights(at, pieces[2:], [expand_out, reduce_out], *large_scratch).steps()
    next(small)

    residual = x_ref[...].astype(F32)
    scale = lax.rsqrt(jnp.mean(residual * residual, axis=-1, keepdims=True) + EPS_NORM)
    rows_out[me] = (residual * scale * gains_ref[0:1]).astype(BF)
    gather = TeamGather(at, rows_out, gs.at[0], gr.at[0])
    gather.start()
    run(small)
    gather.forward()
    next(large)
    gather.finish()
    local = pltpu.make_async_copy(ct_ref, grads_out.at[me], lsem)
    local.start()
    cotangents = TeamGather(at, grads_out, gs.at[1], gr.at[1])
    cotangents.start(ct_ref)

    projected_out[...] = jnp.dot(
        rows_out[...].reshape(rows, D),
        joined_out[...].reshape(D, 384),
        preferred_element_type=F32,
    )
    next(large)
    cosine, sine = cos_ref[...], sin_ref[...]
    left = lax.broadcasted_iota(jnp.int32, (rows, 128), 1) < 64
    raw = projected_out[:, 256:]
    key = normalize(raw) * heads_ref[1:2]
    key = key * cosine + turn(key) * sine
    every_out[team] = jnp.where(left, key, raw).astype(BF)
    halves = [
        Spread(at, "x", "y", every_out, 0, rows // 2, ks.at[0], kr.at[0]),
        Spread(at, "y", "x", every_out, rows // 2, rows // 2, ks.at[1], kr.at[1]),
    ]
    for h in halves:
        h.one_a()
        h.two_a(0)
    for n in range(2):
        query = normalize(projected_out[:, 128 * n : 128 * n + 128]) * heads_ref[0:1]
        query = query * cosine + turn(query) * sine
        query = query.astype(BF).astype(F32) * (HD**-0.5)
        queries_out[2 * n] = jnp.where(left, query, 0.0).astype(BF)
        queries_out[2 * n + 1] = jnp.where(left, pltpu.roll(query, 64, 1), 0.0).astype(BF)
    cotangents.forward()
    run(spread_rest(halves))
    next(large)

    out_ref[...] = jnp.zeros_like(out_ref)
    sum_ref[...] = jnp.zeros_like(sum_ref)

    def block(number, allowed):
        pairs = every_out[number]
        for h in range(GROUP_HEADS):
            weights = jnp.exp(dot_last(queries_out[h], pairs))
            if allowed is not None:
                weights = jnp.where(allowed, weights, 0.0)
            add = weights[:, :128]
            for lane in range(128, rows, 128):
                add = add + weights[:, lane : lane + 128]
            sum_ref[h] += add
            out_ref[h] += jnp.dot(weights.astype(BF), pairs, preferred_element_type=F32)

    def inner(number, carry):
        block(number, None)
        return carry

    lax.fori_loop(1, jnp.maximum(team - 6, 1), inner, 0)
    next(large)
    lax.fori_loop(jnp.maximum(team - 6, 1), team, inner, 0)
    next(large)
    for h in range(GROUP_HEADS):
        out_ref[h] *= main_ref[...]
        sum_ref[h] *= main_ref[...]

    def edge(step, carry):
        number = step * team
        ahead = (number - team) * rows
        row = lax.broadcasted_iota(jnp.int32, (rows, rows), 0)
        column = lax.broadcasted_iota(jnp.int32, (rows, rows), 1) + ahead
        block(number, (column <= row) & (segc_ref[...] == segr_ref[number]))
        return carry

    lax.fori_loop(jnp.where(team == 0, 1, 0), 2, edge, 0)
    for h in range(GROUP_HEADS):
        total = jnp.sum(sum_ref[h], axis=-1, keepdims=True)
        sum_ref[h] = jnp.broadcast_to(total, sum_ref.shape[1:])
        out_ref[h] = jnp.where(left, sum_ref[h], out_ref[h] / sum_ref[h])
    for n in range(2):
        one, two = out_ref[2 * n], out_ref[2 * n + 1]
        attn_out[:, 128 * n : 128 * n + 128] = jnp.where(left, pltpu.roll(one, 64, 1), two).astype(BF)

    def project(n, carry):
        columns = pl.ds(pl.multiple_of(n * 512, 512), 512)
        weight = output_out[pl.ds(n * 4, 4)].reshape(512, 256)
        branch = dot_last(attn_out[...], weight).astype(BF)
        part[:, :, columns] = branch.reshape(TEAM, 64, 512)
        return carry

    lax.fori_loop(0, 4, project, 0)
    branch = TeamReduce(at, part, *reduce_scratch)
    branch.start()
    branch.middle()
    next(large)
    middle = residual + branch.finish()
    middle_out[...] = middle
    scale = lax.rsqrt(jnp.mean(middle * middle, axis=-1, keepdims=True) + EPS_NORM)
    ffn_out[me] = (middle * scale * gains_ref[1:2]).astype(BF)
    second = TeamGather(at, ffn_out, gs.at[2], gr.at[2])
    second.start()
    next(large)
    second.forward()
    next(large)
    second.finish()
    run(large)
    cotangents.finish()
    local.wait()
    for transfer in (gather, cotangents, second, branch):
        transfer.done()


def forward(x, ct, gains, heads, cosine, sine, seg_columns, seg_rows, main, pieces, cid):
    rows = TEAM * 64

    def out(shape, kind=BF):
        return jax.ShapeDtypeStruct(shape, kind)

    return pl.pallas_call(
        forward_kernel,
        out_shape=[
            out((TEAM, 64, D)),
            out((TEAM, 64, D)),
            out((TEAMS, 128, 384)),
            out((TEAMS, 128, 256)),
            out((TEAMS, 128, 2048)),
            out((TEAMS, 128, 1024)),
            out((rows, 384), F32),
            out((GROUP_HEADS, rows, 128)),
            out((TEAMS, rows, 128)),
            out((GROUP_HEADS, rows, 128), F32),
            out((rows, 256)),
            out((64, D), F32),
            out((TEAM, 64, D)),
        ],
        in_specs=[VM, ANY] + [VM] * 7 + [ANY] * 4,
        out_specs=[VM, ANY, VM, VM, ANY, ANY] + [VM] * 7,
        scratch_shapes=[pltpu.VMEM((GROUP_HEADS, rows, 128), F32), pltpu.VMEM((TEAM, 64, D), BF)]
        + TeamReduce.scratch(64, D)
        + Weights.scratch(2)
        + Weights.scratch(2)
        + [DMA((2, 20)), DMA((2, 20)), DMA((3, 7)), DMA((3, 7)), DMA],
        compiler_params=params(cid, 56),
    )(x, ct, gains, heads, cosine, sine, seg_columns, seg_rows, main, *pieces)


def norm_back(value, gain, grad):
    scale = lax.rsqrt(jnp.mean(value * value, axis=-1, keepdims=True) + EPS_NORM)
    unit = value * scale
    inner = grad * gain
    back = scale * (inner - unit * jnp.mean(inner * unit, axis=-1, keepdims=True))
    return back, jnp.sum(grad * unit, axis=0, keepdims=True)


def feed_kernel(*refs):
    (rows_ref, grads_ref, middle_ref, ct_ref, gain_ref, expand_any, reduce_any) = refs[:7]
    (expand_out, shard_out, branch_out, grad_out, back_out, gain_out) = refs[7:13]
    expand_ref, reduce_ref, hidden_ref, both_ref, part = refs[13:18]
    reduce_scratch, grads_scratch = refs[18:23], refs[23:33]
    gs, gr, wsem, osem = refs[33:]
    at = here()
    me = place(at["zh"] * 2 + at["zl"], at["c"])
    rows = TEAM * 64

    def loads(n):
        low = pl.ds(pl.multiple_of(n * 256, 256), 256)
        high = pl.ds(pl.multiple_of(n * 256 + 1024, 256), 256)
        return [
            pltpu.make_async_copy(any_.at[:, :, part_], ref.at[:, :, part_], wsem.at[n, k])
            for k, (any_, ref, part_) in enumerate(
                (
                    (expand_any, expand_ref, low),
                    (expand_any, expand_ref, high),
                    (reduce_any, reduce_ref, low),
                )
            )
        ]

    for n in range(4):
        for copy in loads(n):
            copy.start()
    greet(at, RING + FAR + QUAD[1:])
    ffn_rows = rows_ref[...].reshape(rows, D)
    grad_rows = grads_ref[...].reshape(rows, D)

    def feed(n, carry):
        for copy in loads(n):
            copy.wait()
        low = pl.ds(pl.multiple_of(n * 256, 256), 256)
        high = pl.ds(pl.multiple_of(n * 256 + 1024, 256), 256)
        gate = dot_plain(ffn_rows, expand_ref[:, :, low].reshape(D, 256))
        up = dot_plain(ffn_rows, expand_ref[:, :, high].reshape(D, 256))
        grad = dot_plain(grad_rows, reduce_ref[:, :, low].reshape(D, 256))
        open_ = 1.0 / (1.0 + jnp.exp(-gate))
        silu = gate * open_
        hidden_ref[:, low] = (silu * up).astype(BF)
        both_ref[:, low] = (grad * up * (open_ + silu * (1.0 - open_))).astype(BF)
        both_ref[:, high] = (grad * silu).astype(BF)
        return carry

    lax.fori_loop(0, 4, feed, 0)

    def project(n, carry):
        columns = pl.ds(pl.multiple_of(n * 512, 512), 512)
        weight = expand_ref[pl.ds(n * 4, 4)].reshape(512, 2048)
        part[:, :, columns] = dot_last(both_ref[...], weight).astype(BF).reshape(TEAM, 64, 512)
        return carry

    lax.fori_loop(0, 4, project, 0)
    reduce = TeamReduce(at, part, *reduce_scratch)
    reduce.start()

    def branch(n, carry):
        columns = pl.ds(pl.multiple_of(n * 512, 512), 512)
        weight = reduce_ref[pl.ds(n * 4, 4)].reshape(512, 1024)
        value = dot_last(hidden_ref[...], weight).astype(BF)
        branch_out[:, :, columns] = value.reshape(TEAM, 64, 512)
        return carry

    reduce.middle()
    lax.fori_loop(0, 4, branch, 0)

    def grad_reduce(n, carry):
        columns = pl.ds(pl.multiple_of(n * 256, 256), 256)
        grad = dot_first(grads_ref[:, :, columns].reshape(rows, 256), hidden_ref[...])
        reduce_ref[pl.ds(n * 2, 2)] = grad.astype(BF).reshape(2, 128, 1024)
        return carry

    lax.fori_loop(0, 8, grad_reduce, 0)
    grads = Grads(at, reduce_ref, shard_out, *grads_scratch)
    grads.start()

    back, gain = norm_back(middle_ref[...], gain_ref[...], reduce.finish())
    gain_out[...] = gain
    grad_middle = ct_ref[...].astype(F32) + back
    grad_out[...] = grad_middle
    back_out[me] = grad_middle.astype(BF)
    gather = TeamGather(at, back_out, gs, gr)
    gather.start()

    def grad_expand(n, carry):
        columns = pl.ds(pl.multiple_of(n * 256, 256), 256)
        grad = dot_first(rows_ref[:, :, columns].reshape(rows, 256), both_ref[...])
        expand_ref[pl.ds(n * 2, 2)] = grad.astype(BF).reshape(2, 128, 2048)
        pltpu.make_async_copy(
            expand_ref.at[pl.ds(n * 2, 2)], expand_out.at[pl.ds(n * 2, 2)], osem.at[n]
        ).start()
        return carry

    lax.fori_loop(0, 8, grad_expand, 0)
    gather.forward()
    grads.middle()
    gather.finish()
    grads.finish()
    for n in range(8):
        pltpu.make_async_copy(
            expand_ref.at[pl.ds(n * 2, 2)], expand_out.at[pl.ds(n * 2, 2)], osem.at[n]
        ).wait()
    grads.done()
    gather.done()
    reduce.done()


def feed(ffn_rows, grad_rows, middle, ct, gain, expand_all, reduce_all, cid):
    rows = TEAM * 64

    def out(shape, kind=BF):
        return jax.ShapeDtypeStruct(shape, kind)

    return pl.pallas_call(
        feed_kernel,
        out_shape=[
            out((TEAMS, 128, 2048)),
            out((4, 32, 1024)),
            out((TEAM, 64, D)),
            out((64, D), F32),
            out((TEAM, 64, D)),
            out((1, D), F32),
        ],
        in_specs=[VM] * 5 + [ANY] * 2,
        out_specs=[ANY] + [VM] * 5,
        scratch_shapes=[
            pltpu.VMEM((TEAMS, 128, 2048), BF),
            pltpu.VMEM((TEAMS, 128, 1024), BF),
            pltpu.VMEM((rows, 1024), BF),
            pltpu.VMEM((rows, 2048), BF),
            pltpu.VMEM((TEAM, 64, D), BF),
        ]
        + TeamReduce.scratch(64, D)
        + Grads.scratch(1024)
        + [DMA((7,)), DMA((7,)), DMA((4, 3)), DMA((8,))],
        compiler_params=params(cid, 60),
    )(ffn_rows, grad_rows, middle, ct, gain, expand_all, reduce_all)


def backward_kernel(*refs):
    (
        back_ref,
        rows_ref,
        joined_ref,
        output_ref,
        q_ref,
        kv_ref,
        out_ref,
        attn_ref,
        projected_ref,
        branch_ref,
        middle_ref,
        grad_ref,
        x_ref,
        gains_ref,
        heads_ref,
        cos_ref,
        sin_ref,
        segc_ref,
        segr_ref,
        mainc_ref,
        mainr_ref,
        gain_ref,
        expand_any,
    ) = refs[:23]
    block_out, input_out, sum_out, expand_out, output_out, joined_out = refs[23:29]
    (do_ref, inner_ref, qm_ref, dom_ref, innerm_ref, dq_ref, dkv_ref) = refs[29:36]
    (gp_ref, part, output_grad, joined_grad) = refs[36:40]
    expand_scratch, output_scratch, joined_scratch = refs[40:50], refs[50:60], refs[60:70]
    first_scratch, second_scratch = refs[70:75], refs[75:80]
    own, one, held, two, ks, kr, kl = refs[80:87]
    sum_scratch = refs[87:]
    at = here()
    team = at["y"] * SIDE + at["x"]
    rows = TEAM * 64
    greet(at, RING + FAR + QUAD[1:])
    expand = Grads(at, expand_any, expand_out, *expand_scratch)
    expand.start()
    branch = TeamReduce(at, branch_ref, *first_scratch)
    branch.start()

    attended = dot_plain(back_ref[...].reshape(rows, D), output_ref[...].reshape(D, 256))
    left = lax.broadcasted_iota(jnp.int32, (rows, 128), 1) < 64
    ones = jnp.ones((8, 128), BF)
    low = mainc_ref[...].astype(BF)
    dq_ref[...] = jnp.zeros_like(dq_ref)
    for h in range(GROUP_HEADS):
        grad = attended[:, 128 * (h // 2) : 128 * (h // 2) + 128]
        if h % 2 == 0:
            grad = pltpu.roll(grad, 64, 1)
        value = out_ref[h]
        scaled = jnp.where(left, 0.0, grad / value[:, :1]).astype(BF)
        do_ref[h] = scaled
        inner = jnp.where(left, 0.0, scaled.astype(F32) * value)
        high = inner.astype(BF)
        rest = (inner - high.astype(F32)).astype(BF)
        inner_ref[h] = (dot_last(ones, high) + dot_last(ones, rest))[0:1]
        qm_ref[h] = q_ref[h] * low
        dom_ref[h] = scaled * low
        innerm_ref[h] = inner_ref[h] * mainr_ref[...]

    def grad_output(n, carry):
        columns = pl.ds(pl.multiple_of(n * 256, 256), 256)
        grad = dot_first(back_ref[:, :, columns].reshape(rows, 256), attn_ref[...])
        output_grad[pl.ds(n * 2, 2)] = grad.astype(BF).reshape(2, 128, 256)
        return carry

    lax.fori_loop(0, 8, grad_output, 0)
    output = Grads(at, output_grad, output_out, *output_scratch)
    output.start()
    branch.middle()

    def block(number, allowed, q, do, inner):
        pairs = kv_ref[number]
        total = jnp.zeros(pairs.shape, F32)
        for h in range(GROUP_HEADS):
            weights = jnp.exp(dot_last(pairs, q[h]))
            if allowed is not None:
                weights = jnp.where(allowed, weights, 0.0)
            grad = (weights * (dot_last(pairs, do[h]) - inner[h])).astype(BF)
            total = total + jnp.dot(grad, q[h], preferred_element_type=F32)
            total = total + jnp.dot(weights.astype(BF), do[h], preferred_element_type=F32)
            dq_ref[h] += dot_first(pairs, grad)
        dkv_ref[number] = total.astype(BF)

    def interior(number, carry):
        block(number, None, qm_ref, dom_ref, innerm_ref)
        return carry

    lax.fori_loop(1, team, interior, 0)

    def edge(step, carry):
        number = step * team
        ahead = (number - team) * rows
        row = lax.broadcasted_iota(jnp.int32, (rows, rows), 1)
        column = lax.broadcasted_iota(jnp.int32, (rows, rows), 0) + ahead
        allowed = (column <= row) & (segc_ref[number] == segr_ref[...])
        block(number, allowed, q_ref, do_ref, inner_ref)
        return carry

    lax.fori_loop(jnp.where(team == 0, 1, 0), 2, edge, 0)

    def rest_of(number, carry):
        dkv_ref[number] = jnp.zeros(dkv_ref.shape[1:], BF)
        return carry

    lax.fori_loop(team + 1, TEAMS, rest_of, 0)
    half = rows // 2
    pairs = [
        Gather(
            at,
            f,
            s,
            dkv_ref,
            half * n,
            own.at[n],
            one.at[n],
            held.at[n],
            two.at[n],
            ks.at[n],
            kr.at[n],
            kl.at[n],
        )
        for n, (f, s) in enumerate((("y", "x"), ("x", "y")))
    ]
    for h in pairs:
        h.start()
    block_out[...] = (middle_ref[...] + branch.finish()).astype(BF)

    cosine, sine = cos_ref[...], sin_ref[...]

    def prepare_back(raw, gain, grad):
        unit = normalize(raw)
        square = raw * raw
        across = jnp.sum(jnp.where(left, square, 0.0), axis=-1, keepdims=True)
        along = jnp.sum(jnp.where(left, 0.0, square), axis=-1, keepdims=True)
        scale = lax.rsqrt(jnp.where(left, across, along) / HD + EPS_NORM)
        grad = grad * cosine - turn(grad * sine)
        gain_grad = jnp.sum(grad * unit, axis=0, keepdims=True)
        grad = grad * gain
        inner = grad * unit
        across = jnp.sum(jnp.where(left, inner, 0.0), axis=-1, keepdims=True)
        along = jnp.sum(jnp.where(left, 0.0, inner), axis=-1, keepdims=True)
        return scale * (grad - unit * (jnp.where(left, across, along) / HD)), gain_grad

    query_gain = jnp.zeros((1, 128), F32)
    for n in range(2):
        both = jnp.concatenate([dq_ref[2 * n, :64], dq_ref[2 * n + 1, :64]], axis=0)
        columns = slice(128 * n, 128 * n + 128)
        grad, gain = prepare_back(
            projected_ref[:, columns], heads_ref[0:1], both.T * (HD**-0.5)
        )
        query_gain = query_gain + gain
        gp_ref[:, columns] = grad.astype(BF)
    for h in pairs:
        h.middle()
    expand.middle()
    output.middle()
    pair_grad = jnp.concatenate([h.finish() for h in pairs], axis=0)
    grad, key_gain = prepare_back(projected_ref[:, 256:], heads_ref[1:2], pair_grad)
    gp_ref[:, 256:] = jnp.where(left, grad, pair_grad).astype(BF)

    def project(n, carry):
        columns = pl.ds(pl.multiple_of(n * 512, 512), 512)
        weight = joined_ref[pl.ds(n * 4, 4)].reshape(512, 384)
        part[:, :, columns] = dot_last(gp_ref[...], weight).astype(BF).reshape(TEAM, 64, 512)
        return carry

    lax.fori_loop(0, 4, project, 0)
    reduce = TeamReduce(at, part, *second_scratch)
    reduce.start()

    def grad_joined(n, carry):
        columns = pl.ds(pl.multiple_of(n * 256, 256), 256)
        grad = dot_first(rows_ref[:, :, columns].reshape(rows, 256), gp_ref[...])
        joined_grad[pl.ds(n * 2, 2)] = grad.astype(BF).reshape(2, 128, 384)
        return carry

    reduce.middle()
    lax.fori_loop(0, 8, grad_joined, 0)
    joined = Grads(at, joined_grad, joined_out, *joined_scratch)
    joined.start()
    expand.finish()
    output.finish()
    back, gain = norm_back(x_ref[...].astype(F32), gains_ref[0:1], reduce.finish())
    input_out[...] = (grad_ref[...] + back).astype(BF)
    for n in range(16):
        columns = slice(128 * n, 128 * n + 128)
        sum_out[n : n + 1, :] = gain[:, columns]
        sum_out[16 + n : 17 + n, :] = gain_ref[:, columns]
    query_gain = query_gain + pltpu.roll(query_gain, 64, 1)
    lane = lax.broadcasted_iota(jnp.int32, (1, 128), 1)
    sum_out[32:33, :] = jnp.where(lane < 64, query_gain, pltpu.roll(key_gain, 64, 1))
    sums = Sum(at, sum_out, *sum_scratch).steps()
    next(sums)
    next(sums)
    joined.middle()
    next(sums)
    next(sums)
    joined.finish()
    run(sums)
    for transfer in (expand, output, joined, branch, reduce):
        transfer.done()
    for h in pairs:
        h.done()


def backward(arrays, cid):
    rows = TEAM * 64
    half = rows // 2

    def out(shape, kind=BF):
        return jax.ShapeDtypeStruct(shape, kind)

    heads = (GROUP_HEADS, rows, 128)
    return pl.pallas_call(
        backward_kernel,
        out_shape=[
            out((64, D)),
            out((64, D)),
            out((33, 128), F32),
            out((4, 32, 2048)),
            out((4, 32, 256)),
            out((4, 32, 384)),
        ],
        in_specs=[VM] * (len(arrays) - 1) + [ANY],
        out_specs=[VM] * 6,
        scratch_shapes=[
            pltpu.VMEM(heads, BF),
            pltpu.VMEM((GROUP_HEADS, 1, rows), F32),
            pltpu.VMEM(heads, BF),
            pltpu.VMEM(heads, BF),
            pltpu.VMEM((GROUP_HEADS, 1, rows), F32),
            pltpu.VMEM((GROUP_HEADS, 128, rows), F32),
            pltpu.VMEM((TEAMS, rows, 128), BF),
            pltpu.VMEM((rows, 384), BF),
            pltpu.VMEM((TEAM, 64, D), BF),
            pltpu.VMEM((TEAMS, 128, 256), BF),
            pltpu.VMEM((TEAMS, 128, 384), BF),
        ]
        + Grads.scratch(2048)
        + Grads.scratch(256)
        + Grads.scratch(384)
        + TeamReduce.scratch(64, D)
        + TeamReduce.scratch(64, D)
        + [
            pltpu.VMEM((2, SIDE, half, 128), BF),
            pltpu.VMEM((2, 3, SIDE, half, 128), BF),
            pltpu.VMEM((2, SIDE, half, 128), BF),
            pltpu.VMEM((2, 3, half, 128), BF),
            DMA((2, 15)),
            DMA((2, 15)),
            DMA((2, 4)),
        ]
        + Sum.scratch((33, 128)),
        compiler_params=params(cid, 60),
    )(*arrays)


def on_device(
    block_in,
    cotangent,
    segments,
    gains,
    joined_weight,
    output_weight,
    expand_weight,
    reduce_weight,
    gains_first,
    gains_squares,
    joined_first,
    joined_squares,
    output_first,
    output_squares,
    expand_first,
    expand_squares,
    reduce_first,
    reduce_squares,
):
    model, width = D, HD
    team = lax.axis_index("y") * SIDE + lax.axis_index("x")
    gain_attn = gains[:model]
    gain_ffn = gains[model : 2 * model]
    gain_query = gains[2 * model : 2 * model + width]
    gain_key = gains[2 * model + width :]

    joined_pieces = joined_weight.astype(BF).transpose(1, 0, 2)
    output_pieces = output_weight.astype(BF).reshape(32, 4, 256).transpose(1, 0, 2)
    expand_pieces = (
        expand_weight.astype(BF).reshape(32, 2, 4, 1024).transpose(2, 0, 1, 3).reshape(4, 32, 2048)
    )
    reduce_pieces = reduce_weight.astype(BF).reshape(32, 4, 1024).transpose(1, 0, 2)
    rows = TEAM * 64
    first_row = team * rows
    query_index = first_row + jnp.arange(rows, dtype=jnp.int32)
    cosine, sine = tables(query_index, width)
    query_seg = lax.dynamic_slice_in_dim(segments, first_row, rows)
    main = (query_seg == segments[127]).astype(F32)
    seg_blocks = segments.reshape(TEAMS, rows)
    norms = jnp.stack([gain_attn, gain_ffn])
    heads = jnp.stack([jnp.tile(gain_query, 2), jnp.tile(gain_key, 2)])
    cosine, sine = jnp.tile(cosine, (1, 2)), jnp.tile(sine, (1, 2))
    (
        attn_rows,
        grad_rows,
        joined_all,
        output_all,
        expand_all,
        reduce_all,
        projected,
        queries,
        every,
        attended,
        attn_out,
        middle,
        ffn_rows,
    ) = forward(
        block_in,
        cotangent,
        norms,
        heads,
        cosine,
        sine,
        query_seg[:, None],
        seg_blocks[:, None, :],
        main[:, None],
        [joined_pieces, output_pieces, expand_pieces, reduce_pieces],
        1,
    )
    grad_expand, shard_reduce, branch, grad_middle, back_rows, gain_grad = feed(
        ffn_rows, grad_rows, middle, cotangent, norms[1:], expand_all, reduce_all, 2
    )
    block_out, input_grad, gain_grad, shard_expand, shard_output, shard_joined = backward(
        [
            back_rows,
            attn_rows,
            joined_all,
            output_all,
            queries,
            every,
            attended,
            attn_out,
            projected,
            branch,
            middle,
            grad_middle,
            block_in,
            norms,
            heads,
            cosine,
            sine,
            seg_blocks[:, :, None],
            query_seg[None, :],
            main[:, None],
            main[None, :],
            gain_grad,
            grad_expand,
        ],
        3,
    )
    gain_grad = gain_grad.reshape(-1)
    shard_joined = shard_joined.transpose(1, 0, 2).astype(F32)
    shard_output = shard_output.transpose(1, 0, 2).reshape(32, 1024).astype(F32)
    shard_expand = (
        shard_expand.reshape(4, 32, 2, 1024).transpose(1, 2, 0, 3).reshape(32, 2, 4096).astype(F32)
    )
    shard_reduce = shard_reduce.transpose(1, 0, 2).reshape(32, 4096).astype(F32)
    joined = adamw(joined_weight, shard_joined, joined_first, joined_squares, D ** (-0.5))
    output = adamw(
        output_weight, shard_output, output_first, output_squares, max(1, H * HD // 128) ** (-0.5)
    )
    expand = adamw(expand_weight, shard_expand, expand_first, expand_squares, D ** (-0.5))
    reduce_new = adamw(reduce_weight, shard_reduce, reduce_first, reduce_squares, FF ** (-0.5))
    gain_new = adamw(gains, gain_grad, gains_first, gains_squares, GAIN_RATE)
    return (
        block_out,
        input_grad,
        joined[0],
        joined[1],
        joined[2],
        joined[2].astype(BF),
        output[0],
        output[1],
        output[2],
        output[2].astype(BF),
        expand[0],
        expand[1],
        expand[2],
        expand[2].astype(BF),
        reduce_new[0],
        reduce_new[1],
        reduce_new[2],
        reduce_new[2].astype(BF),
        gain_new[0],
        gain_new[1],
        gain_new[2],
    )


def solution(mesh):
    physical = Mesh(mesh.devices.reshape(SIDE, SIDE, 2, 2, 2), AXES)
    rows = P(AXES, None)
    joined = P(SEQ, "zh", None)
    plain = P(SEQ, "zh")
    expand = P(SEQ, None, "zh")
    placed = (
        (rows, rows, P(), P(), joined, plain, expand, plain, P(), P())
        + (joined,) * 2
        + (plain,) * 2
        + (expand,) * 2
        + (plain,) * 2
    )
    return jax.shard_map(
        on_device,
        mesh=physical,
        in_specs=placed,
        out_specs=(rows, rows)
        + (joined,) * 4
        + (plain,) * 4
        + (expand,) * 4
        + (plain,) * 4
        + (P(),) * 3,
        check_vma=False,
    )
```

```python
import functools

import jax
import jax.numpy as jnp
from jax import lax
from jax.experimental import pallas as pl
from jax.experimental.pallas import tpu as pltpu
from jax.sharding import Mesh
from jax.sharding import PartitionSpec as P

D = 2048
H = 32
HD = 64
FF = 8192
STEP = 10

EPS_NORM = 1e-05
THETA = 1000000.0
BETA_ONE = 0.5
BETA_TWO = 0.5
ADAM_EPS = 1e-08
DECAY = 0.1
GAIN_RATE = 0.2

AXES = ("y", "x", "zl", "c", "zh")
SEQ = ("y", "x", "zl", "c")
SIDE = 4
TEAMS = 16
TEAM = 8
GROUP_HEADS = 4
BF = jnp.bfloat16
F32 = jnp.float32
MESHID = pl.DeviceIdType.MESH
ANY = pl.BlockSpec(memory_space=pl.ANY)
VM = pl.BlockSpec(memory_space=pltpu.VMEM)
DMA = pltpu.SemaphoreType.DMA


def rmsnorm(values, weight):
    return values * lax.rsqrt(jnp.mean(values * values, axis=-1, keepdims=True) + EPS_NORM) * weight


def tables(positions, width):
    inverse = THETA ** (-(jnp.arange(0, width, 2).astype(jnp.float32) / width))
    angles = positions.astype(jnp.float32)[:, None] * inverse[None, :]
    angles = jnp.concatenate([angles, angles], axis=-1)
    return (jnp.cos(angles), jnp.sin(angles))


def rotate(values, cosine, sine):
    half = values.shape[-1] // 2
    turned = jnp.concatenate([-values[..., half:], values[..., :half]], axis=-1)
    return values * cosine + turned * sine


def prepare(query_raw, key_raw, gain_query, gain_key, cosine, sine):
    query_rot = rotate(rmsnorm(query_raw, gain_query), cosine[:, None, :], sine[:, None, :])
    key_rot = rotate(rmsnorm(key_raw, gain_key), cosine, sine)
    return (query_rot, key_rot)


def swiglu(both):
    half = both.shape[-1] // 2
    return jax.nn.silu(both[:, :half]) * both[:, half:]


def adamw(master, gradient, first, second, rate):
    moment = BETA_ONE * first + (1.0 - BETA_ONE) * gradient
    squares = BETA_TWO * second + (1.0 - BETA_TWO) * gradient * gradient
    scaled_one = moment / (1.0 - BETA_ONE**STEP)
    scaled_two = squares / (1.0 - BETA_TWO**STEP)
    updated = master - rate * (scaled_one / (jnp.sqrt(scaled_two) + ADAM_EPS) + DECAY * master)
    return (moment, squares, updated)


def here():
    return {a: lax.axis_index(a) for a in AXES}


def moved(at, axis, step=1):
    to = dict(at)
    if axis == "z":
        z = lax.rem(at["zh"] * 2 + at["zl"] + step + SIDE, SIDE)
        to["zh"] = z // 2
        to["zl"] = lax.rem(z, 2)
    elif axis == "quad":
        if step & 1:
            to["c"] = 1 - at["c"]
        if step & 2:
            to["zl"] = 1 - at["zl"]
    elif axis == "c":
        to["c"] = 1 - at["c"]
    else:
        to[axis] = lax.rem(at[axis] + step + SIDE, SIDE)
    return to


def ident(at):
    return tuple(at[a] for a in AXES)


def greet(at, moves):
    barrier = pltpu.get_barrier_semaphore()
    for axis, step in moves:
        pl.semaphore_signal(
            barrier, inc=1, device_id=ident(moved(at, axis, step)), device_id_type=MESHID
        )
    pl.semaphore_wait(barrier, len(moves))


def remote(src, dst, ssem, rsem, to):
    return pltpu.make_async_remote_copy(
        src_ref=src,
        dst_ref=dst,
        send_sem=ssem,
        recv_sem=rsem,
        device_id=ident(to),
        device_id_type=MESHID,
    )


def params(cid, vmem=48):
    return pltpu.CompilerParams(
        collective_id=cid, has_side_effects=True, vmem_limit_bytes=vmem << 20
    )


def place(z, c):
    return (lax.rem(z, 2) * 2 + c) * 2 + z // 2


QUAD = (("quad", 1), ("quad", 2), ("quad", 3))
NEAR = (("x", 1), ("x", -1), ("y", 1), ("y", -1))
FAR = tuple((axis, step) for axis in ("x", "y") for step in (1, 2, 3))
RING = (("z", 1), ("z", -1), ("z", 2), ("c", 1))


class Spread:
    def __init__(self, at, first, second, out, lo, rows, ssem, rsem):
        self.at, self.f, self.s, self.out = at, first, second, out
        self.lo, self.rows, self.ssem, self.rsem = lo, rows, ssem, rsem
        self.sent = []

    def slot(self, df, ds, part=None):
        f = lax.rem(self.at[self.f] + df + SIDE, SIDE)
        s = lax.rem(self.at[self.s] + ds + SIDE, SIDE)
        y, x = (f, s) if self.f == "y" else (s, f)
        lo, n = self.lo, self.rows
        if part is not None:
            n = n // 2
            lo = lo + part * n
        return self.out.at[y * SIDE + x, pl.ds(lo, n)]

    def send(self, block, k, axis, step):
        copy = remote(block, block, self.ssem.at[k], self.rsem.at[k], moved(self.at, axis, step))
        copy.start()
        self.sent.append(copy)

    def wait(self, block, k):
        to = moved(self.at, self.f, 1)
        remote(block, block, self.ssem.at[k], self.rsem.at[k], to).wait_recv()

    def one_a(self):
        self.send(self.slot(0, 0), 0, self.f, 1)
        self.send(self.slot(0, 0), 1, self.f, -1)

    def one_b(self, side):
        df = -1 if side == 0 else 1
        self.wait(self.slot(df, 0), side)
        self.send(self.slot(df, 0, side), 2 + side, self.f, -df)

    def one_c(self):
        self.wait(self.slot(2, 0, 0), 2)
        self.wait(self.slot(2, 0, 1), 3)

    STEPS = (0, -1, 1, 2)

    def two_a(self, j):
        block = self.slot(self.STEPS[j], 0)
        self.send(block, 4 + 4 * j, self.s, 1)
        self.send(block, 5 + 4 * j, self.s, -1)

    def two_b(self, j, side):
        ds = -1 if side == 0 else 1
        self.wait(self.slot(self.STEPS[j], ds), 4 + 4 * j + side)
        self.send(self.slot(self.STEPS[j], ds, side), 6 + 4 * j + side, self.s, -ds)

    def two_c(self, j):
        self.wait(self.slot(self.STEPS[j], 2, 0), 6 + 4 * j)
        self.wait(self.slot(self.STEPS[j], 2, 1), 7 + 4 * j)

    def done(self):
        for copy in self.sent:
            copy.wait_send()


def spread_rest(halves):
    for side in (0, 1):
        for h in halves:
            h.one_b(side)
            h.two_a(1 + side)
    yield
    for side in (0, 1):
        for h in halves:
            h.two_b(0, side)
    yield
    for h in halves:
        h.one_c()
        h.two_a(3)
    yield
    for j in (1, 2, 3):
        for side in (0, 1):
            for h in halves:
                h.two_b(j, side)
        yield
    for j in range(4):
        for h in halves:
            h.two_c(j)
    for h in halves:
        h.done()


class Weights:
    def __init__(self, at, pieces, outs, ssem, rsem, qs, qr, lsem):
        self.at, self.pieces, self.outs = at, pieces, outs
        self.ssem, self.rsem, self.qs, self.qr, self.lsem = ssem, rsem, qs, qr, lsem

    def steps(self):
        at = self.at
        mine = at["y"] * SIDE + at["x"]
        quad = at["zl"] * 2 + at["c"]
        near = pl.multiple_of(at["zl"] * 64, 64)
        far = pl.multiple_of(64 - at["zl"] * 64, 64)
        quads, owned = [], []
        for k, (piece, out) in enumerate(zip(self.pieces, self.outs)):
            rows = out.at[mine, pl.ds(pl.multiple_of(quad * 32, 32), 32)]
            local = pltpu.make_async_copy(piece.at[quad], rows, self.lsem.at[k])
            local.start()
            owned.append(local)
            for step in (1, 2, 3):
                to = moved(at, "quad", step)
                copy = remote(
                    piece.at[to["zl"] * 2 + to["c"]],
                    rows,
                    self.qs.at[k, step - 1],
                    self.qr.at[k, step - 1],
                    to,
                )
                copy.start()
                quads.append(copy)
        yield
        firsts, seconds = [], []
        for k, out in enumerate(self.outs):
            s, r = self.ssem, self.rsem
            firsts.append(Spread(at, "x", "y", out, near, 64, s.at[k, 0], r.at[k, 0]))
            seconds.append(Spread(at, "y", "x", out, far, 64, s.at[k, 1], r.at[k, 1]))
        for k, half in enumerate(firsts):
            owned[k].wait()
            quads[3 * k].wait_recv()
            half.one_a()
            half.two_a(0)
        yield
        for k, half in enumerate(seconds):
            quads[3 * k + 1].wait_recv()
            quads[3 * k + 2].wait_recv()
            half.one_a()
            half.two_a(0)
        yield
        yield from spread_rest(firsts + seconds)
        for copy in quads:
            copy.wait_send()

    @staticmethod
    def scratch(count):
        return [
            DMA((count, 2, 20)),
            DMA((count, 2, 20)),
            DMA((count, 3)),
            DMA((count, 3)),
            DMA((count,)),
        ]


def run(steps):
    for _ in steps:
        pass


class Gather:
    def __init__(self, at, first, second, src, lo, rows, one, two, ssem, rsem):
        self.at, self.f, self.s, self.src, self.lo, self.rows = at, first, second, src, lo, rows
        self.one, self.two, self.ssem, self.rsem = one, two, ssem, rsem

    def block(self, f, s):
        y, x = (f, s) if self.f == "y" else (s, f)
        return self.src.at[y * SIDE + x, pl.ds(self.lo, self.rows)]

    def start(self):
        self.sent = []
        for d in (2, 1, 3):
            f = lax.rem(self.at[self.f] + d, SIDE)
            for s in range(SIDE):
                k = (d - 1) * 4 + s
                copy = remote(
                    self.block(f, s),
                    self.one.at[d - 1, s],
                    self.ssem.at[k],
                    self.rsem.at[k],
                    moved(self.at, self.f, d),
                )
                copy.start()
                self.sent.append((d, s, copy))

    def arrived(self):
        for d, s, copy in self.sent:
            copy.wait_recv()

    def add(self, s, one):
        own = self.block(self.at[self.f], s)
        total = own[...].astype(F32)
        for d in range(3):
            total = total + one[d].astype(F32)
        own[...] = total.astype(BF)

    def onward(self):
        for d in (2, 1, 3):
            s = lax.rem(self.at[self.s] + d, SIDE)
            copy = remote(
                self.block(self.at[self.f], s),
                self.two.at[d - 1],
                self.ssem.at[11 + d],
                self.rsem.at[11 + d],
                moved(self.at, self.s, d),
            )
            copy.start()
            self.sent.append((d, 0, copy))

    def finish(self):
        for d, s, copy in self.sent[12:]:
            copy.wait_recv()
        total = self.block(self.at[self.f], self.at[self.s])[...].astype(F32)
        for d in range(3):
            total = total + self.two[d].astype(F32)
        return total

    def done(self):
        for d, s, copy in self.sent:
            copy.wait_send()


def middle_held(halves):
    for h in halves:
        h.arrived()

        def add(s, carry, h=h):
            h.add(s, h.one.at[:, s])
            return carry

        lax.fori_loop(0, SIDE, add, 0)
        h.onward()


def middle_staged(halves, stage, sems):
    def load(k):
        h, s = halves[k // SIDE], k % SIDE
        return pltpu.make_async_copy(h.one.at[:, s], stage.at[k % 2], sems.at[k % 2])

    for k in range(SIDE * len(halves)):
        h, s = halves[k // SIDE], k % SIDE
        if s == 0:
            h.arrived()
        load(k).start()
        if k > 0:
            before = halves[(k - 1) // SIDE]
            load(k - 1).wait()
            before.add((k - 1) % SIDE, stage.at[(k - 1) % 2])
            if s == 0:
                before.onward()
    load(k).wait()
    h.add(s, stage.at[k % 2])
    h.onward()


class Grads:
    def __init__(self, at, src, out, one, two, total, ssem, rsem, qs, qr):
        self.at, self.out, self.total, self.qs, self.qr = at, out, total, qs, qr
        self.halves = [
            Gather(at, f, s, src, 64 * n, 64, one.at[n], two.at[n], ssem.at[n], rsem.at[n])
            for n, (f, s) in enumerate((("y", "x"), ("x", "y")))
        ]

    def start(self):
        for h in self.halves:
            h.start()

    def finish(self):
        at, total = self.at, self.total
        quad = at["zl"] * 2 + at["c"]
        for n, h in enumerate(self.halves):
            total[n] = h.finish().astype(BF)
        self.quads = []
        for step in (3, 2, 1):
            to = moved(at, "quad", step)
            copy = remote(
                total.at[to["zl"], pl.ds(pl.multiple_of(to["c"] * 32, 32), 32)],
                self.out.at[quad],
                self.qs.at[step - 1],
                self.qr.at[step - 1],
                to,
            )
            copy.start()
            self.quads.append(copy)
        self.out[quad] = total[at["zl"], pl.ds(pl.multiple_of(at["c"] * 32, 32), 32)]

    def done(self):
        for copy in self.quads:
            copy.wait()
        for h in self.halves:
            h.done()

    @staticmethod
    def shape(n):
        return (2, 3, SIDE, 64, n)

    @staticmethod
    def scratch(n):
        return [
            pltpu.VMEM((2, 3, 64, n), BF),
            pltpu.VMEM((2, 64, n), BF),
            DMA((2, 15)),
            DMA((2, 15)),
            DMA((3,)),
            DMA((3,)),
        ]


class TeamGather:
    def __init__(self, at, out, ssem, rsem):
        self.at, self.out, self.ssem, self.rsem = at, out, ssem, rsem

    def start(self, src=None):
        at, out = self.at, self.out
        c, z = at["c"], at["zh"] * 2 + at["zl"]
        mine = out.at[place(z, c)]
        src = mine if src is None else src
        self.ring = []
        for k, d in enumerate((2, 1, -1)):
            copy = remote(src, mine, self.ssem.at[k], self.rsem.at[k], moved(at, "z", d))
            copy.start()
            self.ring.append(copy)
        copy = remote(src, mine, self.ssem.at[6], self.rsem.at[6], moved(at, "c"))
        copy.start()
        self.pair = [copy]

    def forward(self):
        at, out = self.at, self.out
        c, z = at["c"], at["zh"] * 2 + at["zl"]
        for k, d in ((1, 1), (2, -1), (0, 2)):
            slot = out.at[place(lax.rem(z - d + SIDE, SIDE), c)]
            self.ring[k].wait_recv()
            copy = remote(slot, slot, self.ssem.at[3 + k], self.rsem.at[3 + k], moved(at, "c"))
            copy.start()
            self.pair.append(copy)

    def finish(self):
        for copy in self.pair:
            copy.wait_recv()

    def done(self):
        for copy in self.ring + self.pair:
            copy.wait_send()


class TeamReduce:
    ORDER = (2, 1, -1, 0)

    def __init__(self, at, part, one, held, two, ssem, rsem):
        self.at, self.part, self.one, self.held, self.two = at, part, one, held, two
        self.ssem, self.rsem = ssem, rsem

    def slot(self, d, c):
        return place(lax.rem(self.at["zh"] * 2 + self.at["zl"] + d + SIDE, SIDE), c)

    def start(self):
        self.first, self.second = [], []
        for k, d in enumerate(self.ORDER):
            copy = remote(
                self.part.at[self.slot(d, 1 - self.at["c"])],
                self.one.at[k],
                self.ssem.at[k],
                self.rsem.at[k],
                moved(self.at, "c"),
            )
            copy.start()
            self.first.append(copy)

    def middle(self):
        for k, d in enumerate(self.ORDER):
            self.first[k].wait_recv()
            if d == 0:
                continue
            mine = self.part[self.slot(d, self.at["c"])].astype(F32)
            self.held[k] = (mine + self.one[k].astype(F32)).astype(BF)
            copy = remote(
                self.held.at[k],
                self.two.at[k],
                self.ssem.at[4 + k],
                self.rsem.at[4 + k],
                moved(self.at, "z", d),
            )
            copy.start()
            self.second.append(copy)

    def finish(self):
        total = self.part[self.slot(0, self.at["c"])].astype(F32) + self.one[3].astype(F32)
        for k in (1, 2, 0):
            self.second[k].wait_recv()
            total = total + self.two[k].astype(F32)
        return total

    def done(self):
        for copy in self.first + self.second:
            copy.wait_send()

    @staticmethod
    def scratch(count, width):
        return [
            pltpu.VMEM((4, count, width), BF),
            pltpu.VMEM((3, count, width), BF),
            pltpu.VMEM((3, count, width), BF),
            DMA((7,)),
            DMA((7,)),
        ]


class Sum:
    def __init__(self, at, value, pair, ring, row, column, ssem, rsem):
        self.at, self.value, self.ssem, self.rsem = at, value, ssem, rsem
        self.axes = (
            ("c", pair, at["c"]),
            ("z", ring, at["zh"] * 2 + at["zl"]),
            ("x", row, at["x"]),
            ("y", column, at["y"]),
        )

    def steps(self):
        k = 0
        for axis, buffer, me in self.axes:
            buffer[me] = self.value[...]
            copies = []
            for step in range(1, buffer.shape[0]):
                copy = remote(
                    buffer.at[me],
                    buffer.at[me],
                    self.ssem.at[k],
                    self.rsem.at[k],
                    moved(self.at, axis, step),
                )
                copy.start()
                copies.append(copy)
                k += 1
            yield
            for copy in copies:
                copy.wait()
            total = buffer[0]
            for n in range(1, buffer.shape[0]):
                total = total + buffer[n]
            self.value[...] = total

    @staticmethod
    def scratch(shape):
        return [pltpu.VMEM((n,) + shape, F32) for n in (2, 4, 4, 4)] + [DMA((10,)), DMA((10,))]


def dot_plain(a, b):
    return jnp.dot(a, b, preferred_element_type=F32)


def dot_last(a, b):
    return lax.dot_general(a, b, (((1,), (1,)), ((), ())), preferred_element_type=F32)


def dot_first(a, b):
    return lax.dot_general(a, b, (((0,), (0,)), ((), ())), preferred_element_type=F32)


def lanes_of(value):
    return lax.broadcasted_iota(jnp.int32, value.shape, 1)


def turn(value):
    low = lax.rem(lanes_of(value), 64) < 32
    return jnp.where(low, -pltpu.roll(value, 96, 1), pltpu.roll(value, 32, 1))


def head_gains(gains_ref):
    both = gains_ref[32:33]
    other = pltpu.roll(both, 64, 1)
    left = lanes_of(both) < 64
    return jnp.where(left, both, other), jnp.where(left, other, both)


def wide_gain(gains_ref, first):
    return jnp.concatenate([gains_ref[n : n + 1] for n in range(first, first + 16)], axis=1)


def upright(row):
    return jnp.broadcast_to(row, (8, row.shape[1])).T[:, :1]


def normalize(value):
    left = lanes_of(value) < 64
    square = value * value
    one = jnp.sum(jnp.where(left, square, 0.0), axis=-1, keepdims=True)
    two = jnp.sum(jnp.where(left, 0.0, square), axis=-1, keepdims=True)
    return value * lax.rsqrt(jnp.where(left, one, two) / HD + EPS_NORM)


def forward_kernel(*refs):
    (x_ref, ct_ref, gains_ref, cos_ref, sin_ref, seg_ref) = refs[:6]
    weights = refs[6:11]
    (rows_out, grads_out, joined_out, output_out, expand_out, reduce_out) = refs[11:17]
    (projected_out, queries_out, every_out, out_ref, attn_out, middle_out, ffn_out) = refs[17:24]
    sum_ref, part = refs[24:26]
    reduce_scratch = refs[26:31]
    small_scratch, large_scratch = refs[31:36], refs[36:41]
    ks, kr, gs, gr, lsem = refs[41:46]
    pieces = refs[46:50]
    at = here()
    team = at["y"] * SIDE + at["x"]
    me = place(at["zh"] * 2 + at["zl"], at["c"])
    rows = queries_out.shape[1]
    sources = ((0, 0, 0, 384), (1, 1, 0, 256), (2, 2, 0, 1024), (3, 2, 1024, 1024), (4, 3, 0, 1024))
    for source, piece, to, n in sources:
        for t in range(4):
            value = weights[source][:, n * t : n * t + n]
            pieces[piece][t, :, to : to + n] = value.astype(BF)
    greet(at, RING + NEAR + QUAD[1:])

    small = Weights(at, pieces[:2], [joined_out, output_out], *small_scratch).steps()
    large = Weights(at, pieces[2:], [expand_out, reduce_out], *large_scratch).steps()
    next(small)

    residual = x_ref[...].astype(F32)
    scale = lax.rsqrt(jnp.mean(residual * residual, axis=-1, keepdims=True) + EPS_NORM)
    rows_out[me] = (residual * scale * wide_gain(gains_ref, 0)).astype(BF)
    gather = TeamGather(at, rows_out, gs.at[0], gr.at[0])
    gather.start()
    run(small)
    gather.forward()
    next(large)
    gather.finish()
    local = pltpu.make_async_copy(ct_ref, grads_out.at[me], lsem)
    local.start()
    cotangents = TeamGather(at, grads_out, gs.at[1], gr.at[1])
    cotangents.start(ct_ref)

    projected_out[...] = jnp.dot(
        rows_out[...].reshape(rows, D),
        joined_out[...].reshape(D, 384),
        preferred_element_type=F32,
    )
    next(large)
    query_gain, key_gain = head_gains(gains_ref)
    cosine, sine = cos_ref[...], sin_ref[...]
    left = lax.broadcasted_iota(jnp.int32, (rows, 128), 1) < 64
    raw = projected_out[:, 256:]
    key = normalize(raw) * key_gain
    key = key * cosine + turn(key) * sine
    every_out[team] = jnp.where(left, key, raw).astype(BF)
    halves = [
        Spread(at, "x", "y", every_out, 0, rows // 2, ks.at[0], kr.at[0]),
        Spread(at, "y", "x", every_out, rows // 2, rows // 2, ks.at[1], kr.at[1]),
    ]
    for h in halves:
        h.one_a()
        h.two_a(0)
    for n in range(2):
        query = normalize(projected_out[:, 128 * n : 128 * n + 128]) * query_gain
        query = query * cosine + turn(query) * sine
        query = query.astype(BF).astype(F32) * (HD**-0.5)
        queries_out[2 * n] = jnp.where(left, query, 0.0).astype(BF)
        queries_out[2 * n + 1] = jnp.where(left, pltpu.roll(query, 64, 1), 0.0).astype(BF)
    run(spread_rest(halves))
    next(large)

    out_ref[...] = jnp.zeros_like(out_ref)
    sum_ref[...] = jnp.zeros_like(sum_ref)

    def block(number, allowed):
        pairs = every_out[number]
        for h in range(GROUP_HEADS):
            weights = jnp.exp(dot_last(queries_out[h], pairs))
            if allowed is not None:
                weights = jnp.where(allowed, weights, 0.0)
            add = weights[:, :128]
            for lane in range(128, rows, 128):
                add = add + weights[:, lane : lane + 128]
            sum_ref[h] += add
            out_ref[h] += jnp.dot(weights.astype(BF), pairs, preferred_element_type=F32)

    def inner(number, carry):
        block(number, None)
        return carry

    lax.fori_loop(1, jnp.maximum(team - 6, 1), inner, 0)
    next(large)
    lax.fori_loop(jnp.maximum(team - 6, 1), team, inner, 0)
    next(large)
    own = upright(seg_ref[pl.ds(team, 1)].astype(F32))
    main = (own == seg_ref[0:1, 127:128].astype(F32)).astype(F32)
    for h in range(GROUP_HEADS):
        out_ref[h] *= main
        sum_ref[h] *= main

    def edge(step, carry):
        number = step * team
        ahead = (number - team) * rows
        row = lax.broadcasted_iota(jnp.int32, (rows, rows), 0)
        column = lax.broadcasted_iota(jnp.int32, (rows, rows), 1) + ahead
        block(number, (column <= row) & (own == seg_ref[pl.ds(number, 1)].astype(F32)))
        return carry

    lax.fori_loop(jnp.where(team == 0, 1, 0), 2, edge, 0)
    cotangents.forward()
    for h in range(GROUP_HEADS):
        total = jnp.sum(sum_ref[h], axis=-1, keepdims=True)
        sum_ref[h] = jnp.broadcast_to(total, sum_ref.shape[1:])
        out_ref[h] = jnp.where(left, sum_ref[h], out_ref[h] / sum_ref[h])
    for n in range(2):
        one, two = out_ref[2 * n], out_ref[2 * n + 1]
        attn_out[:, 128 * n : 128 * n + 128] = jnp.where(left, pltpu.roll(one, 64, 1), two).astype(BF)

    def project(n, carry):
        columns = pl.ds(pl.multiple_of(n * 512, 512), 512)
        weight = output_out[pl.ds(n * 4, 4)].reshape(512, 256)
        branch = dot_last(attn_out[...], weight).astype(BF)
        part[:, :, columns] = branch.reshape(TEAM, 64, 512)
        return carry

    lax.fori_loop(0, 4, project, 0)
    branch = TeamReduce(at, part, *reduce_scratch)
    branch.start()
    branch.middle()
    next(large)
    middle = residual + branch.finish()
    middle_out[...] = middle
    scale = lax.rsqrt(jnp.mean(middle * middle, axis=-1, keepdims=True) + EPS_NORM)
    ffn_out[me] = (middle * scale * wide_gain(gains_ref, 16)).astype(BF)
    second = TeamGather(at, ffn_out, gs.at[2], gr.at[2])
    second.start()
    next(large)
    second.forward()
    next(large)
    second.finish()
    run(large)
    cotangents.finish()
    local.wait()
    for transfer in (gather, cotangents, second, branch):
        transfer.done()


def forward(x, ct, gains, cosine, sine, segs, weights, cid):
    rows = TEAM * 64

    def out(shape, kind=BF):
        return jax.ShapeDtypeStruct(shape, kind)

    return pl.pallas_call(
        forward_kernel,
        out_shape=[
            out((TEAM, 64, D)),
            out((TEAM, 64, D)),
            out((TEAMS, 128, 384)),
            out((TEAMS, 128, 256)),
            out((TEAMS, 128, 2048)),
            out((TEAMS, 128, 1024)),
            out((rows, 384), F32),
            out((GROUP_HEADS, rows, 128)),
            out((TEAMS, rows, 128)),
            out((GROUP_HEADS, rows, 128), F32),
            out((rows, 256)),
            out((64, D), F32),
            out((TEAM, 64, D)),
        ],
        in_specs=[VM, ANY] + [VM] * 9,
        out_specs=[VM, ANY, VM, VM, ANY, ANY] + [VM] * 7,
        scratch_shapes=[pltpu.VMEM((GROUP_HEADS, rows, 128), F32), pltpu.VMEM((TEAM, 64, D), BF)]
        + TeamReduce.scratch(64, D)
        + Weights.scratch(2)
        + Weights.scratch(2)
        + [DMA((2, 20)), DMA((2, 20)), DMA((3, 7)), DMA((3, 7)), DMA]
        + [pltpu.VMEM((4, 32, n), BF) for n in (384, 256, 2048, 1024)],
        compiler_params=params(cid, 56),
    )(x, ct, gains, cosine, sine, segs, *weights)


def norm_back(value, gain, grad):
    scale = lax.rsqrt(jnp.mean(value * value, axis=-1, keepdims=True) + EPS_NORM)
    unit = value * scale
    inner = grad * gain
    back = scale * (inner - unit * jnp.mean(inner * unit, axis=-1, keepdims=True))
    return back, jnp.sum(grad * unit, axis=0, keepdims=True)


def back_kernel(*refs):
    (rows_any, grads_any, middle_ref, ct_ref, x_ref, gains_ref, cos_ref, sin_ref, seg_ref) = refs[:9]
    refs = refs[:7] + (None,) * 4 + refs[7:]
    expand_any, reduce_any = refs[13:15]
    late_any = refs[15:23]
    block_out, input_out, sum_out, expand_out, reduce_out, output_out, joined_out = refs[23:30]
    expand_one, reduce_one = refs[30:32]
    expand_ref, reduce_ref, hidden_ref, both_ref, part, branch_ref, back_ref, grad_ref = refs[32:40]
    (joined_ref, output_ref, q_ref, kv_ref, out_ref, attn_ref, projected_ref) = refs[40:47]
    inner_ref, innerm_ref, dq_ref, dkv_ref = refs[47:51]
    output_grad, joined_grad, output_one, joined_one = refs[51:55]
    expand_sems, reduce_sems, output_sems, joined_sems = (
        refs[55:61],
        refs[61:67],
        refs[67:73],
        refs[73:79],
    )
    first_scratch, second_scratch = refs[79:84], refs[84:89]
    kv_one, kv_two, ks, kr, stage, stage_sem, gs, gr, wsem, lsem = refs[89:99]
    rows_ref, grads_ref, isem = refs[99:102]
    sum_scratch = refs[102:]
    late_refs = refs[40:47] + (rows_ref,)
    slabs = [both_ref.at[:, pl.ds(128 * n, 128)] for n in range(3 * GROUP_HEADS)]
    do_refs, qm_refs, dom_refs = (slabs[n : n + GROUP_HEADS] for n in (0, 4, 8))
    q_refs = [q_ref.at[h] for h in range(GROUP_HEADS)]
    gp_ref = hidden_ref.at[:, pl.ds(0, 384)]
    at = here()
    me = place(at["zh"] * 2 + at["zl"], at["c"])
    team = at["y"] * SIDE + at["x"]
    rows = TEAM * 64
    late = [
        pltpu.make_async_copy(src, dst, lsem.at[n])
        for n, (src, dst) in enumerate(zip(late_any, late_refs))
    ]

    def loads(n):
        low = pl.ds(pl.multiple_of(n * 256, 256), 256)
        high = pl.ds(pl.multiple_of(n * 256 + 1024, 256), 256)
        return [
            pltpu.make_async_copy(any_.at[:, :, part_], ref.at[:, :, part_], wsem.at[n, k])
            for k, (any_, ref, part_) in enumerate(
                (
                    (expand_any, expand_ref, low),
                    (expand_any, expand_ref, high),
                    (reduce_any, reduce_ref, low),
                )
            )
        ]

    inputs = [
        pltpu.make_async_copy(rows_any, rows_ref, isem.at[0]),
        pltpu.make_async_copy(grads_any, grads_ref, isem.at[1]),
    ]
    for copy in inputs:
        copy.start()
    for n in range(4):
        for copy in loads(n):
            copy.start()
    greet(at, RING + FAR + QUAD[1:])
    for copy in late[:-1]:
        copy.start()
    for copy in inputs:
        copy.wait()
    ffn_values = rows_ref[...].reshape(rows, D)
    grad_values = grads_ref[...].reshape(rows, D)

    def feed(n, carry):
        for copy in loads(n):
            copy.wait()
        low = pl.ds(pl.multiple_of(n * 256, 256), 256)
        high = pl.ds(pl.multiple_of(n * 256 + 1024, 256), 256)
        gate = dot_plain(ffn_values, expand_ref[:, :, low].reshape(D, 256))
        up = dot_plain(ffn_values, expand_ref[:, :, high].reshape(D, 256))
        grad = dot_plain(grad_values, reduce_ref[:, :, low].reshape(D, 256))
        open_ = 1.0 / (1.0 + jnp.exp(-gate))
        silu = gate * open_
        hidden_ref[:, low] = (silu * up).astype(BF)
        both_ref[:, low] = (grad * up * (open_ + silu * (1.0 - open_))).astype(BF)
        both_ref[:, high] = (grad * silu).astype(BF)
        return carry

    lax.fori_loop(0, 4, feed, 0)

    def project(n, carry):
        columns = pl.ds(pl.multiple_of(n * 512, 512), 512)
        weight = expand_ref[pl.ds(n * 4, 4)].reshape(512, 2048)
        part[:, :, columns] = dot_last(both_ref[...], weight).astype(BF).reshape(TEAM, 64, 512)
        return carry

    lax.fori_loop(0, 4, project, 0)
    first = TeamReduce(at, part, *first_scratch)
    first.start()

    def branch(n, carry):
        columns = pl.ds(pl.multiple_of(n * 512, 512), 512)
        weight = reduce_ref[pl.ds(n * 4, 4)].reshape(512, 1024)
        value = dot_last(hidden_ref[...], weight).astype(BF)
        branch_ref[:, :, columns] = value.reshape(TEAM, 64, 512)
        return carry

    first.middle()
    lax.fori_loop(0, 4, branch, 0)

    def grad_reduce(n, carry):
        columns = pl.ds(pl.multiple_of(n * 256, 256), 256)
        grad = dot_first(grads_ref[:, :, columns].reshape(rows, 256), hidden_ref[...])
        reduce_ref[pl.ds(n * 2, 2)] = grad.astype(BF).reshape(2, 128, 1024)
        return carry

    lax.fori_loop(0, 8, grad_reduce, 0)
    reduced = Grads(at, reduce_ref, reduce_out, reduce_one, *reduce_sems)
    reduced.start()

    back, gain = norm_back(middle_ref[...], wide_gain(gains_ref, 16), first.finish())
    ffn_gain = gain
    grad_middle = ct_ref[...].astype(F32) + back
    grad_ref[...] = grad_middle
    back_ref[me] = grad_middle.astype(BF)
    gather = TeamGather(at, back_ref, gs, gr)
    gather.start()

    def grad_expand(n, carry):
        columns = pl.ds(pl.multiple_of(n * 256, 256), 256)
        grad = dot_first(rows_ref[:, :, columns].reshape(rows, 256), both_ref[...])
        expand_ref[pl.ds(n * 2, 2)] = grad.astype(BF).reshape(2, 128, 2048)
        return carry

    lax.fori_loop(0, 8, grad_expand, 0)
    late[-1].start()
    expanded = Grads(at, expand_ref, expand_out, expand_one, *expand_sems)
    expanded.start()
    gather.forward()
    gather.finish()
    for copy in late[:-1]:
        copy.wait()
    branch = TeamReduce(at, branch_ref, *second_scratch)
    branch.start()

    attended = dot_plain(back_ref[...].reshape(rows, D), output_ref[...].reshape(D, 256))
    left = lax.broadcasted_iota(jnp.int32, (rows, 128), 1) < 64
    ones = jnp.ones((8, 128), BF)
    own = seg_ref[pl.ds(team, 1)].astype(F32)
    main = (own == seg_ref[0:1, 127:128].astype(F32)).astype(F32)
    low = upright(main).astype(BF)
    dq_ref[...] = jnp.zeros_like(dq_ref)
    for h in range(GROUP_HEADS):
        grad = attended[:, 128 * (h // 2) : 128 * (h // 2) + 128]
        if h % 2 == 0:
            grad = pltpu.roll(grad, 64, 1)
        value = out_ref[h]
        scaled = jnp.where(left, 0.0, grad / value[:, :1]).astype(BF)
        do_refs[h][...] = scaled
        inner = jnp.where(left, 0.0, scaled.astype(F32) * value)
        high = inner.astype(BF)
        rest = (inner - high.astype(F32)).astype(BF)
        inner_ref[h] = (dot_last(ones, high) + dot_last(ones, rest))[0:1]
        qm_refs[h][...] = q_ref[h] * low
        dom_refs[h][...] = scaled * low
        innerm_ref[h] = inner_ref[h] * main

    def grad_output(n, carry):
        columns = pl.ds(pl.multiple_of(n * 256, 256), 256)
        grad = dot_first(back_ref[:, :, columns].reshape(rows, 256), attn_ref[...])
        output_grad[pl.ds(n * 2, 2)] = grad.astype(BF).reshape(2, 128, 256)
        return carry

    lax.fori_loop(0, 8, grad_output, 0)
    output = Grads(at, output_grad, output_out, output_one, *output_sems)
    output.start()
    branch.middle()

    def block(number, allowed, q, do, inner):
        pairs = kv_ref[number]
        total = jnp.zeros(pairs.shape, F32)
        for h in range(GROUP_HEADS):
            query, above = q[h][...], do[h][...]
            weights = jnp.exp(dot_last(pairs, query))
            if allowed is not None:
                weights = jnp.where(allowed, weights, 0.0)
            grad = (weights * (dot_last(pairs, above) - inner[h])).astype(BF)
            total = total + dot_plain(grad, query)
            total = total + dot_plain(weights.astype(BF), above)
            dq_ref[h] += dot_first(pairs, grad)
        dkv_ref[number] = total.astype(BF)

    def interior(number, carry):
        block(number, None, qm_refs, dom_refs, innerm_ref)
        return carry

    part_way = jnp.maximum(team - 8, 1)
    lax.fori_loop(1, part_way, interior, 0)
    middle_staged(reduced.halves, stage.at[:, :, :, pl.ds(0, 1024)], stage_sem)
    lax.fori_loop(part_way, team, interior, 0)

    def edge(step, carry):
        number = step * team
        ahead = (number - team) * rows
        row = lax.broadcasted_iota(jnp.int32, (rows, rows), 1)
        column = lax.broadcasted_iota(jnp.int32, (rows, rows), 0) + ahead
        allowed = (column <= row) & (upright(seg_ref[pl.ds(number, 1)].astype(F32)) == own)
        block(number, allowed, q_refs, do_refs, inner_ref)
        return carry

    lax.fori_loop(jnp.where(team == 0, 1, 0), 2, edge, 0)

    def rest_of(number, carry):
        dkv_ref[number] = jnp.zeros(dkv_ref.shape[1:], BF)
        return carry

    lax.fori_loop(team + 1, TEAMS, rest_of, 0)
    half = rows // 2
    pairs = [
        Gather(at, f, s, dkv_ref, half * n, half, kv_one.at[n], kv_two.at[n], ks.at[n], kr.at[n])
        for n, (f, s) in enumerate((("y", "x"), ("x", "y")))
    ]
    for h in pairs:
        h.start()
    block_out[...] = (middle_ref[...] + branch.finish()).astype(BF)

    cosine, sine = cos_ref[...], sin_ref[...]
    head_gain = head_gains(gains_ref)

    def prepare_back(raw, gain, grad):
        unit = normalize(raw)
        square = raw * raw
        across = jnp.sum(jnp.where(left, square, 0.0), axis=-1, keepdims=True)
        along = jnp.sum(jnp.where(left, 0.0, square), axis=-1, keepdims=True)
        scale = lax.rsqrt(jnp.where(left, across, along) / HD + EPS_NORM)
        grad = grad * cosine - turn(grad * sine)
        gain_grad = jnp.sum(grad * unit, axis=0, keepdims=True)
        grad = grad * gain
        inner = grad * unit
        across = jnp.sum(jnp.where(left, inner, 0.0), axis=-1, keepdims=True)
        along = jnp.sum(jnp.where(left, 0.0, inner), axis=-1, keepdims=True)
        return scale * (grad - unit * (jnp.where(left, across, along) / HD)), gain_grad

    query_gain = jnp.zeros((1, 128), F32)
    for n in range(2):
        both = jnp.concatenate([dq_ref[2 * n, :64], dq_ref[2 * n + 1, :64]], axis=0)
        columns = slice(128 * n, 128 * n + 128)
        grad, gain = prepare_back(
            projected_ref[:, columns], head_gain[0], both.T * (HD**-0.5)
        )
        query_gain = query_gain + gain
        gp_ref[:, columns] = grad.astype(BF)
    middle_held(pairs)
    middle_staged(expanded.halves, stage, stage_sem)
    middle_held(output.halves)
    pair_grad = jnp.concatenate([h.finish() for h in pairs], axis=0)
    grad, key_gain = prepare_back(projected_ref[:, 256:], head_gain[1], pair_grad)
    gp_ref[:, 256:] = jnp.where(left, grad, pair_grad).astype(BF)

    first.done()

    def project(n, carry):
        columns = pl.ds(pl.multiple_of(n * 512, 512), 512)
        weight = joined_ref[pl.ds(n * 4, 4)].reshape(512, 384)
        part[:, :, columns] = dot_last(gp_ref[...], weight).astype(BF).reshape(TEAM, 64, 512)
        return carry

    lax.fori_loop(0, 4, project, 0)
    last = TeamReduce(at, part, *first_scratch)
    last.start()
    late[-1].wait()

    def grad_joined(n, carry):
        columns = pl.ds(pl.multiple_of(n * 256, 256), 256)
        grad = dot_first(rows_ref[:, :, columns].reshape(rows, 256), gp_ref[...])
        joined_grad[pl.ds(n * 2, 2)] = grad.astype(BF).reshape(2, 128, 384)
        return carry

    last.middle()
    lax.fori_loop(0, 8, grad_joined, 0)
    joined = Grads(at, joined_grad, joined_out, joined_one, *joined_sems)
    joined.start()
    reduced.finish()
    expanded.finish()
    output.finish()
    back, gain = norm_back(x_ref[...].astype(F32), wide_gain(gains_ref, 0), last.finish())
    input_out[...] = (grad_ref[...] + back).astype(BF)
    for n in range(16):
        columns = slice(128 * n, 128 * n + 128)
        sum_out[n : n + 1, :] = gain[:, columns]
        sum_out[16 + n : 17 + n, :] = ffn_gain[:, columns]
    query_gain = query_gain + pltpu.roll(query_gain, 64, 1)
    lane = lax.broadcasted_iota(jnp.int32, (1, 128), 1)
    sum_out[32:33, :] = jnp.where(lane < 64, query_gain, pltpu.roll(key_gain, 64, 1))
    sums = Sum(at, sum_out, *sum_scratch).steps()
    next(sums)
    next(sums)
    middle_held(joined.halves)
    next(sums)
    next(sums)
    joined.finish()
    run(sums)
    for transfer in (reduced, expanded, output, joined, branch, last, gather):
        transfer.done()
    for h in pairs:
        h.done()


def backward(arrays, expand_all, reduce_all, late, cid):
    rows = TEAM * 64

    def out(shape, kind=BF):
        return jax.ShapeDtypeStruct(shape, kind)

    return pl.pallas_call(
        back_kernel,
        out_shape=[
            out((64, D)),
            out((64, D)),
            out((33, 128), F32),
            out((4, 32, 2048)),
            out((4, 32, 1024)),
            out((4, 32, 256)),
            out((4, 32, 384)),
            out(Grads.shape(2048)),
            out(Grads.shape(1024)),
        ],
        in_specs=[ANY] * 2 + [VM] * (len(arrays) - 2) + [ANY] * (2 + len(late)),
        out_specs=[VM] * 7 + [ANY] * 2,
        scratch_shapes=[
            pltpu.VMEM((TEAMS, 128, 2048), BF),
            pltpu.VMEM((TEAMS, 128, 1024), BF),
            pltpu.VMEM((rows, 1024), BF),
            pltpu.VMEM((rows, 2048), BF),
            pltpu.VMEM((TEAM, 64, D), BF),
            pltpu.VMEM((TEAM, 64, D), BF),
            pltpu.VMEM((TEAM, 64, D), BF),
            pltpu.VMEM((64, D), F32),
        ]
        + [pltpu.VMEM(v.shape, v.dtype) for v in late[:-1]]
        + [
            pltpu.VMEM((GROUP_HEADS, 1, rows), F32),
            pltpu.VMEM((GROUP_HEADS, 1, rows), F32),
            pltpu.VMEM((GROUP_HEADS, 128, rows), F32),
            pltpu.VMEM((TEAMS, rows, 128), BF),
            pltpu.VMEM((TEAMS, 128, 256), BF),
            pltpu.VMEM((TEAMS, 128, 384), BF),
            pltpu.VMEM(Grads.shape(256), BF),
            pltpu.VMEM(Grads.shape(384), BF),
        ]
        + Grads.scratch(2048)
        + Grads.scratch(1024)
        + Grads.scratch(256)
        + Grads.scratch(384)
        + TeamReduce.scratch(64, D)
        + TeamReduce.scratch(64, D)
        + [
            pltpu.VMEM((2, 3, SIDE, rows // 2, 128), BF),
            pltpu.VMEM((2, 3, rows // 2, 128), BF),
            DMA((2, 15)),
            DMA((2, 15)),
            pltpu.VMEM((2, 3, 64, 2048), BF),
            DMA((2,)),
            DMA((7,)),
            DMA((7,)),
            DMA((4, 3)),
            DMA((len(late),)),
            pltpu.VMEM((TEAM, 64, D), BF),
            pltpu.VMEM((TEAM, 64, D), BF),
            DMA((2,)),
        ]
        + Sum.scratch((33, 128)),
        compiler_params=params(cid, 63),
    )(*arrays, expand_all, reduce_all, *late)[:7]


def on_device(
    block_in,
    cotangent,
    segments,
    gains,
    joined_weight,
    output_weight,
    expand_weight,
    reduce_weight,
    gains_first,
    gains_squares,
    joined_first,
    joined_squares,
    output_first,
    output_squares,
    expand_first,
    expand_squares,
    reduce_first,
    reduce_squares,
):
    team = lax.axis_index("y") * SIDE + lax.axis_index("x")
    rows = TEAM * 64
    positions = lax.broadcasted_iota(jnp.int32, (rows, 128), 0) + team * rows
    entry = lax.rem(lax.broadcasted_iota(jnp.int32, (rows, 128), 1), HD // 2)
    inverse = THETA ** (-(entry.astype(F32) * 2 / HD))
    angles = positions.astype(F32) * inverse
    cosine, sine = jnp.cos(angles), jnp.sin(angles)
    lines = gains.reshape(33, 128)
    segs = segments.reshape(TEAMS, rows)
    (
        attn_rows,
        grad_rows,
        joined_all,
        output_all,
        expand_all,
        reduce_all,
        projected,
        queries,
        every,
        attended,
        attn_out,
        middle,
        ffn_rows,
    ) = forward(
        block_in,
        cotangent,
        lines,
        cosine,
        sine,
        segs,
        [
            joined_weight.reshape(32, 1536),
            output_weight,
            expand_weight[:, 0],
            expand_weight[:, 1],
            reduce_weight,
        ],
        1,
    )
    (
        block_out,
        input_grad,
        gain_grad,
        shard_expand,
        shard_reduce,
        shard_output,
        shard_joined,
    ) = backward(
        [
            ffn_rows,
            grad_rows,
            middle,
            cotangent,
            block_in,
            lines,
            cosine,
            sine,
            segs,
        ],
        expand_all,
        reduce_all,
        [joined_all, output_all, queries, every, attended, attn_out, projected, attn_rows],
        2,
    )
    gain_grad = gain_grad.reshape(-1)
    shard_joined = shard_joined.transpose(1, 0, 2).astype(F32)
    shard_output = shard_output.transpose(1, 0, 2).reshape(32, 1024).astype(F32)
    shard_expand = (
        shard_expand.reshape(4, 32, 2, 1024).transpose(1, 2, 0, 3).reshape(32, 2, 4096).astype(F32)
    )
    shard_reduce = shard_reduce.transpose(1, 0, 2).reshape(32, 4096).astype(F32)
    joined = adamw(joined_weight, shard_joined, joined_first, joined_squares, D ** (-0.5))
    output = adamw(
        output_weight, shard_output, output_first, output_squares, max(1, H * HD // 128) ** (-0.5)
    )
    expand = adamw(expand_weight, shard_expand, expand_first, expand_squares, D ** (-0.5))
    reduce_new = adamw(reduce_weight, shard_reduce, reduce_first, reduce_squares, FF ** (-0.5))
    gain_new = adamw(gains, gain_grad, gains_first, gains_squares, GAIN_RATE)
    return (
        block_out,
        input_grad,
        joined[0],
        joined[1],
        joined[2],
        joined[2].astype(BF),
        output[0],
        output[1],
        output[2],
        output[2].astype(BF),
        expand[0],
        expand[1],
        expand[2],
        expand[2].astype(BF),
        reduce_new[0],
        reduce_new[1],
        reduce_new[2],
        reduce_new[2].astype(BF),
        gain_new[0],
        gain_new[1],
        gain_new[2],
    )


def solution(mesh):
    physical = Mesh(mesh.devices.reshape(SIDE, SIDE, 2, 2, 2), AXES)
    rows = P(AXES, None)
    joined = P(SEQ, "zh", None)
    plain = P(SEQ, "zh")
    expand = P(SEQ, None, "zh")
    placed = (
        (rows, rows, P(), P(), joined, plain, expand, plain, P(), P())
        + (joined,) * 2
        + (plain,) * 2
        + (expand,) * 2
        + (plain,) * 2
    )
    return jax.shard_map(
        on_device,
        mesh=physical,
        in_specs=placed,
        out_specs=(rows, rows)
        + (joined,) * 4
        + (plain,) * 4
        + (expand,) * 4
        + (plain,) * 4
        + (P(),) * 3,
        check_vma=False,
    )
```

```python
import functools

import jax
import jax.numpy as jnp
from jax import lax
from jax.experimental import pallas as pl
from jax.experimental.layout import Layout, with_layout_constraint
from jax.experimental.pallas import tpu as pltpu
from jax.sharding import Mesh
from jax.sharding import PartitionSpec as P

D = 2048
H = 32
HD = 64
FF = 8192
STEP = 10

EPS_NORM = 1e-05
THETA = 1000000.0
BETA_ONE = 0.5
BETA_TWO = 0.5
ADAM_EPS = 1e-08
DECAY = 0.1
GAIN_RATE = 0.2

AXES = ("y", "x", "zl", "c", "zh")
SEQ = ("y", "x", "zl", "c")
SIDE = 4
TEAMS = 16
TEAM = 8
GROUP_HEADS = 4
BF = jnp.bfloat16
F32 = jnp.float32
MESHID = pl.DeviceIdType.MESH
ANY = pl.BlockSpec(memory_space=pl.ANY)
VM = pl.BlockSpec(memory_space=pltpu.VMEM)
DMA = pltpu.SemaphoreType.DMA


def adamw(master, gradient, first, second, rate):
    moment = BETA_ONE * first + (1.0 - BETA_ONE) * gradient
    squares = BETA_TWO * second + (1.0 - BETA_TWO) * gradient * gradient
    scaled_one = moment / (1.0 - BETA_ONE**STEP)
    scaled_two = squares / (1.0 - BETA_TWO**STEP)
    updated = master - rate * (scaled_one / (jnp.sqrt(scaled_two) + ADAM_EPS) + DECAY * master)
    return (moment, squares, updated)


def here():
    return {a: lax.axis_index(a) for a in AXES}


def moved(at, axis, step=1):
    to = dict(at)
    if axis == "z":
        z = lax.rem(at["zh"] * 2 + at["zl"] + step + SIDE, SIDE)
        to["zh"] = z // 2
        to["zl"] = lax.rem(z, 2)
    elif axis == "quad":
        if step & 1:
            to["c"] = 1 - at["c"]
        if step & 2:
            to["zl"] = 1 - at["zl"]
    elif axis == "c":
        to["c"] = 1 - at["c"]
    else:
        to[axis] = lax.rem(at[axis] + step + SIDE, SIDE)
    return to


def ident(at):
    return tuple(at[a] for a in AXES)


def greet(at, moves):
    barrier = pltpu.get_barrier_semaphore()
    for axis, step in moves:
        pl.semaphore_signal(
            barrier, inc=1, device_id=ident(moved(at, axis, step)), device_id_type=MESHID
        )
    pl.semaphore_wait(barrier, len(moves))


def remote(src, dst, ssem, rsem, to):
    return pltpu.make_async_remote_copy(
        src_ref=src,
        dst_ref=dst,
        send_sem=ssem,
        recv_sem=rsem,
        device_id=ident(to),
        device_id_type=MESHID,
    )


def params(cid, vmem=48):
    return pltpu.CompilerParams(
        collective_id=cid, has_side_effects=True, vmem_limit_bytes=vmem << 20
    )


def place(z, c):
    return (lax.rem(z, 2) * 2 + c) * 2 + z // 2


QUAD = (("quad", 1), ("quad", 2), ("quad", 3))
NEAR = (("x", 1), ("x", -1), ("y", 1), ("y", -1))
FAR = tuple((axis, step) for axis in ("x", "y") for step in (1, 2, 3))
RING = (("z", 1), ("z", -1), ("z", 2), ("c", 1))


class Spread:
    def __init__(self, at, first, second, out, lo, rows, ssem, rsem):
        self.at, self.f, self.s, self.out = at, first, second, out
        self.lo, self.rows, self.ssem, self.rsem = lo, rows, ssem, rsem
        self.sent = []

    def slot(self, df, ds, part=None):
        f = lax.rem(self.at[self.f] + df + SIDE, SIDE)
        s = lax.rem(self.at[self.s] + ds + SIDE, SIDE)
        y, x = (f, s) if self.f == "y" else (s, f)
        lo, n = self.lo, self.rows
        if part is not None:
            n = n // 2
            lo = lo + part * n
        return self.out.at[y * SIDE + x, pl.ds(lo, n)]

    def send(self, block, k, axis, step):
        copy = remote(block, block, self.ssem.at[k], self.rsem.at[k], moved(self.at, axis, step))
        copy.start()
        self.sent.append(copy)

    def wait(self, block, k):
        to = moved(self.at, self.f, 1)
        remote(block, block, self.ssem.at[k], self.rsem.at[k], to).wait_recv()

    def one_a(self):
        self.send(self.slot(0, 0), 0, self.f, 1)
        self.send(self.slot(0, 0), 1, self.f, -1)

    def one_b(self, side):
        df = -1 if side == 0 else 1
        self.wait(self.slot(df, 0), side)
        self.send(self.slot(df, 0, side), 2 + side, self.f, -df)

    def one_c(self):
        self.wait(self.slot(2, 0, 0), 2)
        self.wait(self.slot(2, 0, 1), 3)

    STEPS = (0, -1, 1, 2)

    def two_a(self, j):
        block = self.slot(self.STEPS[j], 0)
        self.send(block, 4 + 4 * j, self.s, 1)
        self.send(block, 5 + 4 * j, self.s, -1)

    def two_b(self, j, side):
        ds = -1 if side == 0 else 1
        self.wait(self.slot(self.STEPS[j], ds), 4 + 4 * j + side)
        self.send(self.slot(self.STEPS[j], ds, side), 6 + 4 * j + side, self.s, -ds)

    def two_c(self, j):
        self.wait(self.slot(self.STEPS[j], 2, 0), 6 + 4 * j)
        self.wait(self.slot(self.STEPS[j], 2, 1), 7 + 4 * j)

    def done(self):
        for copy in self.sent:
            copy.wait_send()


def spread_rest(halves):
    for side in (0, 1):
        for h in halves:
            h.one_b(side)
            h.two_a(1 + side)
    yield
    for side in (0, 1):
        for h in halves:
            h.two_b(0, side)
    yield
    for h in halves:
        h.one_c()
        h.two_a(3)
    yield
    for j in (1, 2, 3):
        for side in (0, 1):
            for h in halves:
                h.two_b(j, side)
        yield
    for j in range(4):
        for h in halves:
            h.two_c(j)
    for h in halves:
        h.done()


class Weights:
    def __init__(self, at, pieces, outs, ssem, rsem, qs, qr, lsem):
        self.at, self.pieces, self.outs = at, pieces, outs
        self.ssem, self.rsem, self.qs, self.qr, self.lsem = ssem, rsem, qs, qr, lsem

    def steps(self):
        at = self.at
        mine = at["y"] * SIDE + at["x"]
        quad = at["zl"] * 2 + at["c"]
        near = pl.multiple_of(at["zl"] * 64, 64)
        far = pl.multiple_of(64 - at["zl"] * 64, 64)
        quads, owned = [], []
        for k, (piece, out) in enumerate(zip(self.pieces, self.outs)):
            rows = out.at[mine, pl.ds(pl.multiple_of(quad * 32, 32), 32)]
            local = pltpu.make_async_copy(piece.at[quad], rows, self.lsem.at[k])
            local.start()
            owned.append(local)
            for step in (1, 2, 3):
                to = moved(at, "quad", step)
                copy = remote(
                    piece.at[to["zl"] * 2 + to["c"]],
                    rows,
                    self.qs.at[k, step - 1],
                    self.qr.at[k, step - 1],
                    to,
                )
                copy.start()
                quads.append(copy)
        yield
        firsts, seconds = [], []
        for k, out in enumerate(self.outs):
            s, r = self.ssem, self.rsem
            firsts.append(Spread(at, "x", "y", out, near, 64, s.at[k, 0], r.at[k, 0]))
            seconds.append(Spread(at, "y", "x", out, far, 64, s.at[k, 1], r.at[k, 1]))
        for k, half in enumerate(firsts):
            owned[k].wait()
            quads[3 * k].wait_recv()
            half.one_a()
            half.two_a(0)
        yield
        for k, half in enumerate(seconds):
            quads[3 * k + 1].wait_recv()
            quads[3 * k + 2].wait_recv()
            half.one_a()
            half.two_a(0)
        yield
        yield from spread_rest(firsts + seconds)
        for copy in quads:
            copy.wait_send()

    @staticmethod
    def scratch(count):
        return [
            DMA((count, 2, 20)),
            DMA((count, 2, 20)),
            DMA((count, 3)),
            DMA((count, 3)),
            DMA((count,)),
        ]


def run(steps):
    for _ in steps:
        pass


class Gather:
    def __init__(self, at, first, second, src, lo, rows, one, two, ssem, rsem):
        self.at, self.f, self.s, self.src, self.lo, self.rows = at, first, second, src, lo, rows
        self.one, self.two, self.ssem, self.rsem = one, two, ssem, rsem

    def block(self, f, s):
        y, x = (f, s) if self.f == "y" else (s, f)
        return self.src.at[y * SIDE + x, pl.ds(self.lo, self.rows)]

    def start(self):
        self.sent = []
        for d in (2, 1, 3):
            f = lax.rem(self.at[self.f] + d, SIDE)
            for s in range(SIDE):
                k = (d - 1) * 4 + s
                copy = remote(
                    self.block(f, s),
                    self.one.at[d - 1, s],
                    self.ssem.at[k],
                    self.rsem.at[k],
                    moved(self.at, self.f, d),
                )
                copy.start()
                self.sent.append((d, s, copy))

    def arrived(self):
        for d, s, copy in self.sent:
            copy.wait_recv()

    def add(self, s, one):
        own = self.block(self.at[self.f], s)
        total = own[...].astype(F32)
        for d in range(3):
            total = total + one[d].astype(F32)
        own[...] = total.astype(BF)

    def onward(self):
        for d in (2, 1, 3):
            s = lax.rem(self.at[self.s] + d, SIDE)
            copy = remote(
                self.block(self.at[self.f], s),
                self.two.at[d - 1],
                self.ssem.at[11 + d],
                self.rsem.at[11 + d],
                moved(self.at, self.s, d),
            )
            copy.start()
            self.sent.append((d, 0, copy))

    def finish(self):
        for d, s, copy in self.sent[12:]:
            copy.wait_recv()
        total = self.block(self.at[self.f], self.at[self.s])[...].astype(F32)
        for d in range(3):
            total = total + self.two[d].astype(F32)
        return total

    def done(self):
        for d, s, copy in self.sent:
            copy.wait_send()


def middle_held(halves):
    for h in halves:
        h.arrived()

        def add(s, carry, h=h):
            h.add(s, h.one.at[:, s])
            return carry

        lax.fori_loop(0, SIDE, add, 0)
        h.onward()


def middle_staged(halves, stage, sems):
    def load(k):
        h, s = halves[k // SIDE], k % SIDE
        return pltpu.make_async_copy(h.one.at[:, s], stage.at[k % 2], sems.at[k % 2])

    for k in range(SIDE * len(halves)):
        h, s = halves[k // SIDE], k % SIDE
        if s == 0:
            h.arrived()
        load(k).start()
        if k > 0:
            before = halves[(k - 1) // SIDE]
            load(k - 1).wait()
            before.add((k - 1) % SIDE, stage.at[(k - 1) % 2])
            if s == 0:
                before.onward()
    load(k).wait()
    h.add(s, stage.at[k % 2])
    h.onward()


class Grads:
    def __init__(self, at, src, out, one, two, total, ssem, rsem, qs, qr):
        self.at, self.out, self.total, self.qs, self.qr = at, out, total, qs, qr
        self.halves = [
            Gather(at, f, s, src, 64 * n, 64, one.at[n], two.at[n], ssem.at[n], rsem.at[n])
            for n, (f, s) in enumerate((("y", "x"), ("x", "y")))
        ]

    def start(self):
        for h in self.halves:
            h.start()

    def cut(self, quad):
        n = self.total.shape[2]
        if len(self.out.shape) == 2:
            return [(pl.ds(0, n), self.out.at[:, pl.ds(pl.multiple_of(quad * n, 128), n)])]
        n = n // 2
        columns = pl.ds(pl.multiple_of(quad * n, 128), n)
        return [(pl.ds(k * n, n), self.out.at[k, :, columns]) for k in (0, 1)]

    def finish(self):
        at, total = self.at, self.total
        quad = at["zl"] * 2 + at["c"]
        for n, h in enumerate(self.halves):
            total[n] = h.finish().astype(BF)
        self.quads = []
        for step in (3, 2, 1):
            to = moved(at, "quad", step)
            rows = pl.ds(pl.multiple_of(to["c"] * 32, 32), 32)
            for k, (columns, place_) in enumerate(self.cut(quad)):
                copy = remote(
                    total.at[to["zl"], rows, columns],
                    place_,
                    self.qs.at[step - 1, k],
                    self.qr.at[step - 1, k],
                    to,
                )
                copy.start()
                self.quads.append(copy)
        rows = pl.ds(pl.multiple_of(at["c"] * 32, 32), 32)
        for columns, place_ in self.cut(quad):
            place_[...] = total[at["zl"], rows, columns]

    def done(self):
        for copy in self.quads:
            copy.wait()
        for h in self.halves:
            h.done()

    @staticmethod
    def shape(n):
        return (2, 3, SIDE, 64, n)

    @staticmethod
    def scratch(n):
        return [
            pltpu.VMEM((2, 3, 64, n), BF),
            pltpu.VMEM((2, 64, n), BF),
            DMA((2, 15)),
            DMA((2, 15)),
            DMA((3, 2)),
            DMA((3, 2)),
        ]


class TeamGather:
    def __init__(self, at, out, ssem, rsem):
        self.at, self.out, self.ssem, self.rsem = at, out, ssem, rsem

    def start(self, src=None):
        at, out = self.at, self.out
        c, z = at["c"], at["zh"] * 2 + at["zl"]
        mine = out.at[place(z, c)]
        src = mine if src is None else src
        self.ring = []
        for k, d in enumerate((2, 1, -1)):
            copy = remote(src, mine, self.ssem.at[k], self.rsem.at[k], moved(at, "z", d))
            copy.start()
            self.ring.append(copy)
        copy = remote(src, mine, self.ssem.at[6], self.rsem.at[6], moved(at, "c"))
        copy.start()
        self.pair = [copy]

    def forward(self):
        at, out = self.at, self.out
        c, z = at["c"], at["zh"] * 2 + at["zl"]
        for k, d in ((1, 1), (2, -1), (0, 2)):
            slot = out.at[place(lax.rem(z - d + SIDE, SIDE), c)]
            self.ring[k].wait_recv()
            copy = remote(slot, slot, self.ssem.at[3 + k], self.rsem.at[3 + k], moved(at, "c"))
            copy.start()
            self.pair.append(copy)

    def finish(self):
        for copy in self.pair:
            copy.wait_recv()

    def done(self):
        for copy in self.ring + self.pair:
            copy.wait_send()


class TeamReduce:
    ORDER = (2, 1, -1, 0)

    def __init__(self, at, part, one, held, two, ssem, rsem):
        self.at, self.part, self.one, self.held, self.two = at, part, one, held, two
        self.ssem, self.rsem = ssem, rsem

    def slot(self, d, c):
        return place(lax.rem(self.at["zh"] * 2 + self.at["zl"] + d + SIDE, SIDE), c)

    def start(self):
        self.first, self.second = [], []
        for k, d in enumerate(self.ORDER):
            copy = remote(
                self.part.at[self.slot(d, 1 - self.at["c"])],
                self.one.at[k],
                self.ssem.at[k],
                self.rsem.at[k],
                moved(self.at, "c"),
            )
            copy.start()
            self.first.append(copy)

    def middle(self):
        for k, d in enumerate(self.ORDER):
            self.first[k].wait_recv()
            if d == 0:
                continue
            mine = self.part[self.slot(d, self.at["c"])].astype(F32)
            self.held[k] = (mine + self.one[k].astype(F32)).astype(BF)
            copy = remote(
                self.held.at[k],
                self.two.at[k],
                self.ssem.at[4 + k],
                self.rsem.at[4 + k],
                moved(self.at, "z", d),
            )
            copy.start()
            self.second.append(copy)

    def finish(self):
        total = self.part[self.slot(0, self.at["c"])].astype(F32) + self.one[3].astype(F32)
        for k in (1, 2, 0):
            self.second[k].wait_recv()
            total = total + self.two[k].astype(F32)
        return total

    def done(self):
        for copy in self.first + self.second:
            copy.wait_send()

    @staticmethod
    def scratch(count, width):
        return [
            pltpu.VMEM((4, count, width), BF),
            pltpu.VMEM((3, count, width), BF),
            pltpu.VMEM((3, count, width), BF),
            DMA((7,)),
            DMA((7,)),
        ]


class Sum:
    def __init__(self, at, value, pair, ring, row, column, ssem, rsem):
        self.at, self.value, self.ssem, self.rsem = at, value, ssem, rsem
        self.axes = (
            ("c", pair, at["c"]),
            ("z", ring, at["zh"] * 2 + at["zl"]),
            ("x", row, at["x"]),
            ("y", column, at["y"]),
        )

    def steps(self):
        k = 0
        for axis, buffer, me in self.axes:
            buffer[me] = self.value[...]
            copies = []
            for step in range(1, buffer.shape[0]):
                copy = remote(
                    buffer.at[me],
                    buffer.at[me],
                    self.ssem.at[k],
                    self.rsem.at[k],
                    moved(self.at, axis, step),
                )
                copy.start()
                copies.append(copy)
                k += 1
            yield
            for copy in copies:
                copy.wait()
            total = buffer[0]
            for n in range(1, buffer.shape[0]):
                total = total + buffer[n]
            self.value[...] = total

    @staticmethod
    def scratch(shape):
        return [pltpu.VMEM((n,) + shape, F32) for n in (2, 4, 4, 4)] + [DMA((10,)), DMA((10,))]


def dot_plain(a, b):
    return jnp.dot(a, b, preferred_element_type=F32)


def dot_last(a, b):
    return lax.dot_general(a, b, (((1,), (1,)), ((), ())), preferred_element_type=F32)


def dot_first(a, b):
    return lax.dot_general(a, b, (((0,), (0,)), ((), ())), preferred_element_type=F32)


def lanes_of(value):
    return lax.broadcasted_iota(jnp.int32, value.shape, 1)


def turn(value):
    low = lax.rem(lanes_of(value), 64) < 32
    return jnp.where(low, -pltpu.roll(value, 96, 1), pltpu.roll(value, 32, 1))


def head_gains(gains_ref):
    both = gains_ref[32:33]
    other = pltpu.roll(both, 64, 1)
    left = lanes_of(both) < 64
    return jnp.where(left, both, other), jnp.where(left, other, both)


def wide_gain(gains_ref, first):
    return jnp.concatenate([gains_ref[n : n + 1] for n in range(first, first + 16)], axis=1)


def upright(row):
    return jnp.broadcast_to(row, (8, row.shape[1])).T[:, :1]


def normalize(value):
    left = lanes_of(value) < 64
    square = value * value
    one = jnp.sum(jnp.where(left, square, 0.0), axis=-1, keepdims=True)
    two = jnp.sum(jnp.where(left, 0.0, square), axis=-1, keepdims=True)
    return value * lax.rsqrt(jnp.where(left, one, two) / HD + EPS_NORM)


def forward_kernel(*refs):
    (x_ref, ct_ref, gains_ref, cos_ref, sin_ref, seg_ref) = refs[:6]
    weights = refs[6:11]
    (rows_out, grads_out, joined_out, output_out, expand_out, reduce_out) = refs[11:17]
    (projected_out, queries_out, every_out, out_ref, attn_out, middle_out, ffn_out) = refs[17:24]
    sum_ref, part = refs[24:26]
    reduce_scratch = refs[26:31]
    small_scratch, large_scratch = refs[31:36], refs[36:41]
    ks, kr, gs, gr, lsem = refs[41:46]
    pieces = refs[46:50]
    at = here()
    team = at["y"] * SIDE + at["x"]
    me = place(at["zh"] * 2 + at["zl"], at["c"])
    rows = queries_out.shape[1]
    sources = ((0, 0, 0, 384), (1, 1, 0, 256), (2, 2, 0, 1024), (3, 2, 1024, 1024), (4, 3, 0, 1024))
    for source, piece, to, n in sources:
        for t in range(4):
            value = weights[source][:, n * t : n * t + n]
            pieces[piece][t, :, to : to + n] = value.astype(BF)
    greet(at, RING + NEAR + QUAD[1:])

    small = Weights(at, pieces[:2], [joined_out, output_out], *small_scratch).steps()
    large = Weights(at, pieces[2:], [expand_out, reduce_out], *large_scratch).steps()
    next(small)

    residual = x_ref[...].astype(F32)
    scale = lax.rsqrt(jnp.mean(residual * residual, axis=-1, keepdims=True) + EPS_NORM)
    rows_out[me] = (residual * scale * wide_gain(gains_ref, 0)).astype(BF)
    gather = TeamGather(at, rows_out, gs.at[0], gr.at[0])
    gather.start()
    run(small)
    gather.forward()
    next(large)
    gather.finish()

    projected_out[...] = jnp.dot(
        rows_out[...].reshape(rows, D),
        joined_out[...].reshape(D, 384),
        preferred_element_type=F32,
    )
    next(large)
    query_gain, key_gain = head_gains(gains_ref)
    cosine, sine = cos_ref[...], sin_ref[...]
    left = lax.broadcasted_iota(jnp.int32, (rows, 128), 1) < 64
    raw = projected_out[:, 256:]
    key = normalize(raw) * key_gain
    key = key * cosine + turn(key) * sine
    every_out[team] = jnp.where(left, key, raw).astype(BF)
    halves = [
        Spread(at, "x", "y", every_out, 0, rows // 2, ks.at[0], kr.at[0]),
        Spread(at, "y", "x", every_out, rows // 2, rows // 2, ks.at[1], kr.at[1]),
    ]
    for h in halves:
        h.one_a()
        h.two_a(0)
    for n in range(2):
        query = normalize(projected_out[:, 128 * n : 128 * n + 128]) * query_gain
        query = query * cosine + turn(query) * sine
        query = query.astype(BF).astype(F32) * (HD**-0.5)
        queries_out[2 * n] = jnp.where(left, query, 0.0).astype(BF)
        queries_out[2 * n + 1] = jnp.where(left, pltpu.roll(query, 64, 1), 0.0).astype(BF)
    run(spread_rest(halves))
    local = pltpu.make_async_copy(ct_ref, grads_out.at[me], lsem)
    local.start()
    cotangents = TeamGather(at, grads_out, gs.at[1], gr.at[1])
    cotangents.start(ct_ref)
    next(large)

    out_ref[...] = jnp.zeros_like(out_ref)
    sum_ref[...] = jnp.zeros_like(sum_ref)

    def block(number, allowed):
        pairs = every_out[number]
        for h in range(GROUP_HEADS):
            weights = jnp.exp(dot_last(queries_out[h], pairs))
            if allowed is not None:
                weights = jnp.where(allowed, weights, 0.0)
            add = weights[:, :128]
            for lane in range(128, rows, 128):
                add = add + weights[:, lane : lane + 128]
            sum_ref[h] += add
            out_ref[h] += jnp.dot(weights.astype(BF), pairs, preferred_element_type=F32)

    def inner(number, carry):
        block(number, None)
        return carry

    lax.fori_loop(1, jnp.maximum(team - 6, 1), inner, 0)
    next(large)
    lax.fori_loop(jnp.maximum(team - 6, 1), team, inner, 0)
    next(large)
    own = upright(seg_ref[pl.ds(team, 1)].astype(F32))
    main = (own == seg_ref[0:1, 127:128].astype(F32)).astype(F32)
    for h in range(GROUP_HEADS):
        out_ref[h] *= main
        sum_ref[h] *= main

    def edge(step, carry):
        number = step * team
        ahead = (number - team) * rows
        row = lax.broadcasted_iota(jnp.int32, (rows, rows), 0)
        column = lax.broadcasted_iota(jnp.int32, (rows, rows), 1) + ahead
        block(number, (column <= row) & (own == seg_ref[pl.ds(number, 1)].astype(F32)))
        return carry

    lax.fori_loop(jnp.where(team == 0, 1, 0), 2, edge, 0)
    cotangents.forward()
    for h in range(GROUP_HEADS):
        total = jnp.sum(sum_ref[h], axis=-1, keepdims=True)
        sum_ref[h] = jnp.broadcast_to(total, sum_ref.shape[1:])
        out_ref[h] = jnp.where(left, sum_ref[h], out_ref[h] / sum_ref[h])
    for n in range(2):
        one, two = out_ref[2 * n], out_ref[2 * n + 1]
        attn_out[:, 128 * n : 128 * n + 128] = jnp.where(left, pltpu.roll(one, 64, 1), two).astype(BF)

    def project(n, carry):
        columns = pl.ds(pl.multiple_of(n * 512, 512), 512)
        weight = output_out[pl.ds(n * 4, 4)].reshape(512, 256)
        branch = dot_last(attn_out[...], weight).astype(BF)
        part[:, :, columns] = branch.reshape(TEAM, 64, 512)
        return carry

    lax.fori_loop(0, 4, project, 0)
    branch = TeamReduce(at, part, *reduce_scratch)
    branch.start()
    branch.middle()
    next(large)
    middle = residual + branch.finish()
    middle_out[...] = middle
    scale = lax.rsqrt(jnp.mean(middle * middle, axis=-1, keepdims=True) + EPS_NORM)
    ffn_out[me] = (middle * scale * wide_gain(gains_ref, 16)).astype(BF)
    second = TeamGather(at, ffn_out, gs.at[2], gr.at[2])
    second.start()
    next(large)
    second.forward()
    next(large)
    second.finish()
    run(large)
    cotangents.finish()
    local.wait()
    for transfer in (gather, cotangents, second, branch):
        transfer.done()


def forward(x, ct, gains, cosine, sine, segs, weights, cid):
    rows = TEAM * 64

    def out(shape, kind=BF):
        return jax.ShapeDtypeStruct(shape, kind)

    return pl.pallas_call(
        forward_kernel,
        out_shape=[
            out((TEAM, 64, D)),
            out((TEAM, 64, D)),
            out((TEAMS, 128, 384)),
            out((TEAMS, 128, 256)),
            out((TEAMS, 128, 2048)),
            out((TEAMS, 128, 1024)),
            out((rows, 384), F32),
            out((GROUP_HEADS, rows, 128)),
            out((TEAMS, rows, 128)),
            out((GROUP_HEADS, rows, 128), F32),
            out((rows, 256)),
            out((64, D), F32),
            out((TEAM, 64, D)),
        ],
        in_specs=[VM, ANY] + [VM] * 9,
        out_specs=[VM, ANY, VM, VM, ANY, ANY] + [VM] * 7,
        scratch_shapes=[pltpu.VMEM((GROUP_HEADS, rows, 128), F32), pltpu.VMEM((TEAM, 64, D), BF)]
        + TeamReduce.scratch(64, D)
        + Weights.scratch(2)
        + Weights.scratch(2)
        + [DMA((2, 20)), DMA((2, 20)), DMA((3, 7)), DMA((3, 7)), DMA]
        + [pltpu.VMEM((4, 32, n), BF) for n in (384, 256, 2048, 1024)],
        compiler_params=params(cid, 56),
    )(x, ct, gains, cosine, sine, segs, *weights)


def norm_back(value, gain, grad):
    scale = lax.rsqrt(jnp.mean(value * value, axis=-1, keepdims=True) + EPS_NORM)
    unit = value * scale
    inner = grad * gain
    back = scale * (inner - unit * jnp.mean(inner * unit, axis=-1, keepdims=True))
    return back, jnp.sum(grad * unit, axis=0, keepdims=True)


def back_kernel(*refs):
    (rows_any, grads_any, middle_ref, ct_ref, x_ref, gains_ref, cos_ref, sin_ref, seg_ref) = refs[:9]
    refs = refs[:7] + (None,) * 4 + refs[7:]
    expand_any, reduce_any = refs[13:15]
    late_any = refs[15:23]
    block_out, input_out, sum_out, expand_out, reduce_out, output_out, joined_out = refs[23:30]
    expand_one, reduce_one = refs[30:32]
    expand_ref, reduce_ref, hidden_ref, both_ref, part, branch_ref, back_ref, grad_ref = refs[32:40]
    (joined_ref, output_ref, q_ref, kv_ref, out_ref, attn_ref, projected_ref) = refs[40:47]
    inner_ref, innerm_ref, dq_ref, dkv_ref = refs[47:51]
    output_grad, joined_grad, output_one, joined_one = refs[51:55]
    expand_sems, reduce_sems, output_sems, joined_sems = (
        refs[55:61],
        refs[61:67],
        refs[67:73],
        refs[73:79],
    )
    first_scratch, second_scratch = refs[79:84], refs[84:89]
    kv_one, kv_two, ks, kr, stage, stage_sem, gs, gr, wsem, lsem = refs[89:99]
    rows_ref, grads_ref, isem = refs[99:102]
    sum_scratch = refs[102:]
    late_refs = refs[40:47] + (rows_ref,)
    slabs = [both_ref.at[:, pl.ds(128 * n, 128)] for n in range(3 * GROUP_HEADS)]
    do_refs, qm_refs, dom_refs = (slabs[n : n + GROUP_HEADS] for n in (0, 4, 8))
    q_refs = [q_ref.at[h] for h in range(GROUP_HEADS)]
    gp_ref = hidden_ref.at[:, pl.ds(0, 384)]
    at = here()
    me = place(at["zh"] * 2 + at["zl"], at["c"])
    team = at["y"] * SIDE + at["x"]
    rows = TEAM * 64
    late = [
        pltpu.make_async_copy(src, dst, lsem.at[n])
        for n, (src, dst) in enumerate(zip(late_any, late_refs))
    ]

    def loads(n):
        low = pl.ds(pl.multiple_of(n * 256, 256), 256)
        high = pl.ds(pl.multiple_of(n * 256 + 1024, 256), 256)
        return [
            pltpu.make_async_copy(any_.at[:, :, part_], ref.at[:, :, part_], wsem.at[n, k])
            for k, (any_, ref, part_) in enumerate(
                (
                    (expand_any, expand_ref, low),
                    (expand_any, expand_ref, high),
                    (reduce_any, reduce_ref, low),
                )
            )
        ]

    inputs = [
        pltpu.make_async_copy(rows_any, rows_ref, isem.at[0]),
        pltpu.make_async_copy(grads_any, grads_ref, isem.at[1]),
    ]
    for copy in inputs:
        copy.start()
    for n in range(4):
        for copy in loads(n):
            copy.start()
    greet(at, RING + FAR + QUAD[1:])
    for copy in late[:-1]:
        copy.start()
    for copy in inputs:
        copy.wait()
    ffn_values = rows_ref[...].reshape(rows, D)
    grad_values = grads_ref[...].reshape(rows, D)

    def feed(n, carry):
        for copy in loads(n):
            copy.wait()
        low = pl.ds(pl.multiple_of(n * 256, 256), 256)
        high = pl.ds(pl.multiple_of(n * 256 + 1024, 256), 256)
        gate = dot_plain(ffn_values, expand_ref[:, :, low].reshape(D, 256))
        up = dot_plain(ffn_values, expand_ref[:, :, high].reshape(D, 256))
        grad = dot_plain(grad_values, reduce_ref[:, :, low].reshape(D, 256))
        open_ = 1.0 / (1.0 + jnp.exp(-gate))
        silu = gate * open_
        hidden_ref[:, low] = (silu * up).astype(BF)
        both_ref[:, low] = (grad * up * (open_ + silu * (1.0 - open_))).astype(BF)
        both_ref[:, high] = (grad * silu).astype(BF)
        return carry

    lax.fori_loop(0, 4, feed, 0)

    def project(n, carry):
        columns = pl.ds(pl.multiple_of(n * 512, 512), 512)
        weight = expand_ref[pl.ds(n * 4, 4)].reshape(512, 2048)
        part[:, :, columns] = dot_last(both_ref[...], weight).astype(BF).reshape(TEAM, 64, 512)
        return carry

    lax.fori_loop(0, 4, project, 0)
    first = TeamReduce(at, part, *first_scratch)
    first.start()

    def branch(n, carry):
        columns = pl.ds(pl.multiple_of(n * 512, 512), 512)
        weight = reduce_ref[pl.ds(n * 4, 4)].reshape(512, 1024)
        value = dot_last(hidden_ref[...], weight).astype(BF)
        branch_ref[:, :, columns] = value.reshape(TEAM, 64, 512)
        return carry

    first.middle()
    lax.fori_loop(0, 4, branch, 0)

    def grad_reduce(n, carry):
        columns = pl.ds(pl.multiple_of(n * 256, 256), 256)
        grad = dot_first(grads_ref[:, :, columns].reshape(rows, 256), hidden_ref[...])
        reduce_ref[pl.ds(n * 2, 2)] = grad.astype(BF).reshape(2, 128, 1024)
        return carry

    lax.fori_loop(0, 8, grad_reduce, 0)
    reduced = Grads(at, reduce_ref, reduce_out, reduce_one, *reduce_sems)
    reduced.start()

    back, gain = norm_back(middle_ref[...], wide_gain(gains_ref, 16), first.finish())
    ffn_gain = gain
    grad_middle = ct_ref[...].astype(F32) + back
    grad_ref[...] = grad_middle
    back_ref[me] = grad_middle.astype(BF)
    gather = TeamGather(at, back_ref, gs, gr)
    gather.start()

    def grad_expand(n, carry):
        columns = pl.ds(pl.multiple_of(n * 256, 256), 256)
        grad = dot_first(rows_ref[:, :, columns].reshape(rows, 256), both_ref[...])
        expand_ref[pl.ds(n * 2, 2)] = grad.astype(BF).reshape(2, 128, 2048)
        return carry

    lax.fori_loop(0, 8, grad_expand, 0)
    late[-1].start()
    expanded = Grads(at, expand_ref, expand_out, expand_one, *expand_sems)
    expanded.start()
    gather.forward()
    gather.finish()
    for copy in late[:-1]:
        copy.wait()
    branch = TeamReduce(at, branch_ref, *second_scratch)
    branch.start()

    attended = dot_plain(back_ref[...].reshape(rows, D), output_ref[...].reshape(D, 256))
    left = lax.broadcasted_iota(jnp.int32, (rows, 128), 1) < 64
    ones = jnp.ones((8, 128), BF)
    own = seg_ref[pl.ds(team, 1)].astype(F32)
    main = (own == seg_ref[0:1, 127:128].astype(F32)).astype(F32)
    low = upright(main).astype(BF)
    dq_ref[...] = jnp.zeros_like(dq_ref)
    for h in range(GROUP_HEADS):
        grad = attended[:, 128 * (h // 2) : 128 * (h // 2) + 128]
        if h % 2 == 0:
            grad = pltpu.roll(grad, 64, 1)
        value = out_ref[h]
        scaled = jnp.where(left, 0.0, grad / value[:, :1]).astype(BF)
        do_refs[h][...] = scaled
        inner = jnp.where(left, 0.0, scaled.astype(F32) * value)
        high = inner.astype(BF)
        rest = (inner - high.astype(F32)).astype(BF)
        inner_ref[h] = (dot_last(ones, high) + dot_last(ones, rest))[0:1]
        qm_refs[h][...] = q_ref[h] * low
        dom_refs[h][...] = scaled * low
        innerm_ref[h] = inner_ref[h] * main

    def grad_output(n, carry):
        columns = pl.ds(pl.multiple_of(n * 256, 256), 256)
        grad = dot_first(back_ref[:, :, columns].reshape(rows, 256), attn_ref[...])
        output_grad[pl.ds(n * 2, 2)] = grad.astype(BF).reshape(2, 128, 256)
        return carry

    lax.fori_loop(0, 8, grad_output, 0)
    output = Grads(at, output_grad, output_out, output_one, *output_sems)
    output.start()
    branch.middle()

    def block(number, allowed, q, do, inner):
        pairs = kv_ref[number]
        total = jnp.zeros(pairs.shape, F32)
        for h in range(GROUP_HEADS):
            query, above = q[h][...], do[h][...]
            weights = jnp.exp(dot_last(pairs, query))
            if allowed is not None:
                weights = jnp.where(allowed, weights, 0.0)
            grad = (weights * (dot_last(pairs, above) - inner[h])).astype(BF)
            total = total + dot_plain(grad, query)
            total = total + dot_plain(weights.astype(BF), above)
            dq_ref[h] += dot_first(pairs, grad)
        dkv_ref[number] = total.astype(BF)

    def interior(number, carry):
        block(number, None, qm_refs, dom_refs, innerm_ref)
        return carry

    part_way = jnp.maximum(team - 8, 1)
    lax.fori_loop(1, part_way, interior, 0)
    lax.fori_loop(part_way, team, interior, 0)

    def edge(step, carry):
        number = step * team
        ahead = (number - team) * rows
        row = lax.broadcasted_iota(jnp.int32, (rows, rows), 1)
        column = lax.broadcasted_iota(jnp.int32, (rows, rows), 0) + ahead
        allowed = (column <= row) & (upright(seg_ref[pl.ds(number, 1)].astype(F32)) == own)
        block(number, allowed, q_refs, do_refs, inner_ref)
        return carry

    lax.fori_loop(jnp.where(team == 0, 1, 0), 2, edge, 0)

    def rest_of(number, carry):
        dkv_ref[number] = jnp.zeros(dkv_ref.shape[1:], BF)
        return carry

    lax.fori_loop(team + 1, TEAMS, rest_of, 0)
    half = rows // 2
    pairs = [
        Gather(at, f, s, dkv_ref, half * n, half, kv_one.at[n], kv_two.at[n], ks.at[n], kr.at[n])
        for n, (f, s) in enumerate((("y", "x"), ("x", "y")))
    ]
    for h in pairs:
        h.start()
    block_out[...] = (middle_ref[...] + branch.finish()).astype(BF)

    cosine, sine = cos_ref[...], sin_ref[...]
    head_gain = head_gains(gains_ref)

    def prepare_back(raw, gain, grad):
        unit = normalize(raw)
        square = raw * raw
        across = jnp.sum(jnp.where(left, square, 0.0), axis=-1, keepdims=True)
        along = jnp.sum(jnp.where(left, 0.0, square), axis=-1, keepdims=True)
        scale = lax.rsqrt(jnp.where(left, across, along) / HD + EPS_NORM)
        grad = grad * cosine - turn(grad * sine)
        gain_grad = jnp.sum(grad * unit, axis=0, keepdims=True)
        grad = grad * gain
        inner = grad * unit
        across = jnp.sum(jnp.where(left, inner, 0.0), axis=-1, keepdims=True)
        along = jnp.sum(jnp.where(left, 0.0, inner), axis=-1, keepdims=True)
        return scale * (grad - unit * (jnp.where(left, across, along) / HD)), gain_grad

    query_gain = jnp.zeros((1, 128), F32)
    for n in range(2):
        both = jnp.concatenate([dq_ref[2 * n, :64], dq_ref[2 * n + 1, :64]], axis=0)
        columns = slice(128 * n, 128 * n + 128)
        grad, gain = prepare_back(
            projected_ref[:, columns], head_gain[0], both.T * (HD**-0.5)
        )
        query_gain = query_gain + gain
        gp_ref[:, columns] = grad.astype(BF)
    middle_staged(reduced.halves, stage.at[:, :, :, pl.ds(0, 1024)], stage_sem)
    middle_held(pairs)
    middle_staged(expanded.halves, stage, stage_sem)
    middle_held(output.halves)
    pair_grad = jnp.concatenate([h.finish() for h in pairs], axis=0)
    grad, key_gain = prepare_back(projected_ref[:, 256:], head_gain[1], pair_grad)
    gp_ref[:, 256:] = jnp.where(left, grad, pair_grad).astype(BF)

    first.done()

    def project(n, carry):
        columns = pl.ds(pl.multiple_of(n * 512, 512), 512)
        weight = joined_ref[pl.ds(n * 4, 4)].reshape(512, 384)
        part[:, :, columns] = dot_last(gp_ref[...], weight).astype(BF).reshape(TEAM, 64, 512)
        return carry

    lax.fori_loop(0, 4, project, 0)
    last = TeamReduce(at, part, *first_scratch)
    last.start()
    late[-1].wait()

    def grad_joined(n, carry):
        columns = pl.ds(pl.multiple_of(n * 256, 256), 256)
        grad = dot_first(rows_ref[:, :, columns].reshape(rows, 256), gp_ref[...])
        joined_grad[pl.ds(n * 2, 2)] = grad.astype(BF).reshape(2, 128, 384)
        return carry

    last.middle()
    lax.fori_loop(0, 8, grad_joined, 0)
    joined = Grads(at, joined_grad, joined_out, joined_one, *joined_sems)
    joined.start()
    reduced.finish()
    expanded.finish()
    output.finish()
    back, gain = norm_back(x_ref[...].astype(F32), wide_gain(gains_ref, 0), last.finish())
    input_out[...] = (grad_ref[...] + back).astype(BF)
    for n in range(16):
        columns = slice(128 * n, 128 * n + 128)
        sum_out[n : n + 1, :] = gain[:, columns]
        sum_out[16 + n : 17 + n, :] = ffn_gain[:, columns]
    query_gain = query_gain + pltpu.roll(query_gain, 64, 1)
    lane = lax.broadcasted_iota(jnp.int32, (1, 128), 1)
    sum_out[32:33, :] = jnp.where(lane < 64, query_gain, pltpu.roll(key_gain, 64, 1))
    sums = Sum(at, sum_out, *sum_scratch).steps()
    next(sums)
    next(sums)
    middle_held(joined.halves)
    next(sums)
    next(sums)
    joined.finish()
    run(sums)
    for transfer in (reduced, expanded, output, joined, branch, last, gather):
        transfer.done()
    for h in pairs:
        h.done()


def backward(arrays, expand_all, reduce_all, late, cid):
    rows = TEAM * 64

    def out(shape, kind=BF):
        return jax.ShapeDtypeStruct(shape, kind)

    return pl.pallas_call(
        back_kernel,
        out_shape=[
            out((64, D)),
            out((64, D)),
            out((33, 128), F32),
            out((2, 32, 4096)),
            out((32, 4096)),
            out((32, 1024)),
            out((32, 1536)),
            out(Grads.shape(2048)),
            out(Grads.shape(1024)),
        ],
        in_specs=[ANY] * 2 + [VM] * (len(arrays) - 2) + [ANY] * (2 + len(late)),
        out_specs=[VM] * 7 + [ANY] * 2,
        scratch_shapes=[
            pltpu.VMEM((TEAMS, 128, 2048), BF),
            pltpu.VMEM((TEAMS, 128, 1024), BF),
            pltpu.VMEM((rows, 1024), BF),
            pltpu.VMEM((rows, 2048), BF),
            pltpu.VMEM((TEAM, 64, D), BF),
            pltpu.VMEM((TEAM, 64, D), BF),
            pltpu.VMEM((TEAM, 64, D), BF),
            pltpu.VMEM((64, D), F32),
        ]
        + [pltpu.VMEM(v.shape, v.dtype) for v in late[:-1]]
        + [
            pltpu.VMEM((GROUP_HEADS, 1, rows), F32),
            pltpu.VMEM((GROUP_HEADS, 1, rows), F32),
            pltpu.VMEM((GROUP_HEADS, 128, rows), F32),
            pltpu.VMEM((TEAMS, rows, 128), BF),
            pltpu.VMEM((TEAMS, 128, 256), BF),
            pltpu.VMEM((TEAMS, 128, 384), BF),
            pltpu.VMEM(Grads.shape(256), BF),
            pltpu.VMEM(Grads.shape(384), BF),
        ]
        + Grads.scratch(2048)
        + Grads.scratch(1024)
        + Grads.scratch(256)
        + Grads.scratch(384)
        + TeamReduce.scratch(64, D)
        + TeamReduce.scratch(64, D)
        + [
            pltpu.VMEM((2, 3, SIDE, rows // 2, 128), BF),
            pltpu.VMEM((2, 3, rows // 2, 128), BF),
            DMA((2, 15)),
            DMA((2, 15)),
            pltpu.VMEM((2, 3, 64, 2048), BF),
            DMA((2,)),
            DMA((7,)),
            DMA((7,)),
            DMA((4, 3)),
            DMA((len(late),)),
            pltpu.VMEM((TEAM, 64, D), BF),
            pltpu.VMEM((TEAM, 64, D), BF),
            DMA((2,)),
        ]
        + Sum.scratch((33, 128)),
        compiler_params=params(cid, 63),
    )(*arrays, expand_all, reduce_all, *late)[:7]


def on_device(
    block_in,
    cotangent,
    segments,
    gains,
    joined_weight,
    output_weight,
    expand_weight,
    reduce_weight,
    gains_first,
    gains_squares,
    joined_first,
    joined_squares,
    output_first,
    output_squares,
    expand_first,
    expand_squares,
    reduce_first,
    reduce_squares,
):
    team = lax.axis_index("y") * SIDE + lax.axis_index("x")
    rows = TEAM * 64
    positions = jnp.arange(rows, dtype=jnp.int32) + team * rows
    inverse = THETA ** (-(jnp.arange(0, HD, 2).astype(F32) / HD))
    angles = positions.astype(F32)[:, None] * inverse[None, :]
    cosine, sine = jnp.tile(jnp.cos(angles), (1, 4)), jnp.tile(jnp.sin(angles), (1, 4))
    lines = gains.reshape(33, 128)
    segs = segments.reshape(TEAMS, rows)
    (
        attn_rows,
        grad_rows,
        joined_all,
        output_all,
        expand_all,
        reduce_all,
        projected,
        queries,
        every,
        attended,
        attn_out,
        middle,
        ffn_rows,
    ) = forward(
        block_in,
        cotangent,
        lines,
        cosine,
        sine,
        segs,
        [
            joined_weight.reshape(32, 1536),
            output_weight,
            expand_weight[:, 0],
            expand_weight[:, 1],
            reduce_weight,
        ],
        1,
    )
    (
        block_out,
        input_grad,
        gain_grad,
        shard_expand,
        shard_reduce,
        shard_output,
        shard_joined,
    ) = backward(
        [
            ffn_rows,
            grad_rows,
            middle,
            cotangent,
            block_in,
            lines,
            cosine,
            sine,
            segs,
        ],
        expand_all,
        reduce_all,
        [joined_all, output_all, queries, every, attended, attn_out, projected, attn_rows],
        2,
    )
    gain_grad = gain_grad.reshape(-1)
    shard_joined = shard_joined.reshape(32, 4, 384).astype(F32)
    shard_output = shard_output.astype(F32)
    shard_expand = shard_expand.transpose(1, 0, 2).astype(F32)
    shard_expand = with_layout_constraint(shard_expand, Layout(major_to_minor=(0, 1, 2)))
    shard_reduce = shard_reduce.astype(F32)
    joined = adamw(joined_weight, shard_joined, joined_first, joined_squares, D ** (-0.5))
    output = adamw(
        output_weight, shard_output, output_first, output_squares, max(1, H * HD // 128) ** (-0.5)
    )
    expand = adamw(expand_weight, shard_expand, expand_first, expand_squares, D ** (-0.5))
    reduce_new = adamw(reduce_weight, shard_reduce, reduce_first, reduce_squares, FF ** (-0.5))
    gain_new = adamw(gains, gain_grad, gains_first, gains_squares, GAIN_RATE)
    return (
        block_out,
        input_grad,
        joined[0],
        joined[1],
        joined[2],
        joined[2].astype(BF),
        output[0],
        output[1],
        output[2],
        output[2].astype(BF),
        expand[0],
        expand[1],
        expand[2],
        expand[2].astype(BF),
        reduce_new[0],
        reduce_new[1],
        reduce_new[2],
        reduce_new[2].astype(BF),
        gain_new[0],
        gain_new[1],
        gain_new[2],
    )


def solution(mesh):
    physical = Mesh(mesh.devices.reshape(SIDE, SIDE, 2, 2, 2), AXES)
    rows = P(AXES, None)
    joined = P(SEQ, "zh", None)
    plain = P(SEQ, "zh")
    expand = P(SEQ, None, "zh")
    placed = (
        (rows, rows, P(), P(), joined, plain, expand, plain, P(), P())
        + (joined,) * 2
        + (plain,) * 2
        + (expand,) * 2
        + (plain,) * 2
    )
    return jax.shard_map(
        on_device,
        mesh=physical,
        in_specs=placed,
        out_specs=(rows, rows)
        + (joined,) * 4
        + (plain,) * 4
        + (expand,) * 4
        + (plain,) * 4
        + (P(),) * 3,
        check_vma=False,
    )
```

```python
import functools

import jax
import jax.numpy as jnp
from jax import lax
from jax.experimental import pallas as pl
from jax.experimental.layout import Layout, with_layout_constraint
from jax.experimental.pallas import tpu as pltpu
from jax.sharding import Mesh
from jax.sharding import PartitionSpec as P

D = 2048
H = 32
HD = 64
FF = 8192
STEP = 10

EPS_NORM = 1e-05
THETA = 1000000.0
BETA_ONE = 0.5
BETA_TWO = 0.5
ADAM_EPS = 1e-08
DECAY = 0.1
GAIN_RATE = 0.2

AXES = ("y", "x", "zl", "c", "zh")
SEQ = ("y", "x", "zl", "c")
SIDE = 4
TEAMS = 16
TEAM = 8
GROUP_HEADS = 4
BF = jnp.bfloat16
F32 = jnp.float32
MESHID = pl.DeviceIdType.MESH
ANY = pl.BlockSpec(memory_space=pl.ANY)
VM = pl.BlockSpec(memory_space=pltpu.VMEM)
DMA = pltpu.SemaphoreType.DMA


def adamw(master, gradient, first, second, rate):
    moment = BETA_ONE * first + (1.0 - BETA_ONE) * gradient
    squares = BETA_TWO * second + (1.0 - BETA_TWO) * gradient * gradient
    scaled_one = moment / (1.0 - BETA_ONE**STEP)
    scaled_two = squares / (1.0 - BETA_TWO**STEP)
    updated = master - rate * (scaled_one / (jnp.sqrt(scaled_two) + ADAM_EPS) + DECAY * master)
    return (moment, squares, updated)


def here():
    return {a: lax.axis_index(a) for a in AXES}


def moved(at, axis, step=1):
    to = dict(at)
    if axis == "z":
        z = lax.rem(at["zh"] * 2 + at["zl"] + step + SIDE, SIDE)
        to["zh"] = z // 2
        to["zl"] = lax.rem(z, 2)
    elif axis == "quad":
        if step & 1:
            to["c"] = 1 - at["c"]
        if step & 2:
            to["zl"] = 1 - at["zl"]
    elif axis == "c":
        to["c"] = 1 - at["c"]
    else:
        to[axis] = lax.rem(at[axis] + step + SIDE, SIDE)
    return to


def ident(at):
    return tuple(at[a] for a in AXES)


def greet(at, moves):
    barrier = pltpu.get_barrier_semaphore()
    for axis, step in moves:
        pl.semaphore_signal(
            barrier, inc=1, device_id=ident(moved(at, axis, step)), device_id_type=MESHID
        )
    pl.semaphore_wait(barrier, len(moves))


def remote(src, dst, ssem, rsem, to):
    return pltpu.make_async_remote_copy(
        src_ref=src,
        dst_ref=dst,
        send_sem=ssem,
        recv_sem=rsem,
        device_id=ident(to),
        device_id_type=MESHID,
    )


def params(cid, vmem=48):
    return pltpu.CompilerParams(
        collective_id=cid, has_side_effects=True, vmem_limit_bytes=vmem << 20
    )


def place(z, c):
    return (lax.rem(z, 2) * 2 + c) * 2 + z // 2


QUAD = (("quad", 1), ("quad", 2), ("quad", 3))
NEAR = (("x", 1), ("x", -1), ("y", 1), ("y", -1))
FAR = tuple((axis, step) for axis in ("x", "y") for step in (1, 2, 3))
RING = (("z", 1), ("z", -1), ("z", 2), ("c", 1))


class Spread:
    def __init__(self, at, first, second, out, lo, rows, ssem, rsem):
        self.at, self.f, self.s, self.out = at, first, second, out
        self.lo, self.rows, self.ssem, self.rsem = lo, rows, ssem, rsem
        self.sent = []

    def slot(self, df, ds, part=None):
        f = lax.rem(self.at[self.f] + df + SIDE, SIDE)
        s = lax.rem(self.at[self.s] + ds + SIDE, SIDE)
        y, x = (f, s) if self.f == "y" else (s, f)
        lo, n = self.lo, self.rows
        if part is not None:
            n = n // 2
            lo = lo + part * n
        return self.out.at[y * SIDE + x, pl.ds(lo, n)]

    def send(self, block, k, axis, step):
        copy = remote(block, block, self.ssem.at[k], self.rsem.at[k], moved(self.at, axis, step))
        copy.start()
        self.sent.append(copy)

    def wait(self, block, k):
        to = moved(self.at, self.f, 1)
        remote(block, block, self.ssem.at[k], self.rsem.at[k], to).wait_recv()

    def one_a(self):
        self.send(self.slot(0, 0), 0, self.f, 1)
        self.send(self.slot(0, 0), 1, self.f, -1)

    def one_b(self, side):
        df = -1 if side == 0 else 1
        self.wait(self.slot(df, 0), side)
        self.send(self.slot(df, 0, side), 2 + side, self.f, -df)

    def one_c(self):
        self.wait(self.slot(2, 0, 0), 2)
        self.wait(self.slot(2, 0, 1), 3)

    STEPS = (0, -1, 1, 2)

    def two_a(self, j):
        block = self.slot(self.STEPS[j], 0)
        self.send(block, 4 + 4 * j, self.s, 1)
        self.send(block, 5 + 4 * j, self.s, -1)

    def two_b(self, j, side):
        ds = -1 if side == 0 else 1
        self.wait(self.slot(self.STEPS[j], ds), 4 + 4 * j + side)
        self.send(self.slot(self.STEPS[j], ds, side), 6 + 4 * j + side, self.s, -ds)

    def two_c(self, j):
        self.wait(self.slot(self.STEPS[j], 2, 0), 6 + 4 * j)
        self.wait(self.slot(self.STEPS[j], 2, 1), 7 + 4 * j)

    def done(self):
        for copy in self.sent:
            copy.wait_send()


def spread_rest(halves):
    for side in (0, 1):
        for h in halves:
            h.one_b(side)
            h.two_a(1 + side)
    yield
    for side in (0, 1):
        for h in halves:
            h.two_b(0, side)
    yield
    for h in halves:
        h.one_c()
        h.two_a(3)
    yield
    for j in (1, 2, 3):
        for side in (0, 1):
            for h in halves:
                h.two_b(j, side)
        yield
    for j in range(4):
        for h in halves:
            h.two_c(j)
    for h in halves:
        h.done()


class Weights:
    def __init__(self, at, pieces, outs, ssem, rsem, qs, qr, lsem):
        self.at, self.pieces, self.outs = at, pieces, outs
        self.ssem, self.rsem, self.qs, self.qr, self.lsem = ssem, rsem, qs, qr, lsem

    def steps(self):
        at = self.at
        mine = at["y"] * SIDE + at["x"]
        quad = at["zl"] * 2 + at["c"]
        near = pl.multiple_of(at["zl"] * 64, 64)
        far = pl.multiple_of(64 - at["zl"] * 64, 64)
        quads, owned = [], []
        for k, (piece, out) in enumerate(zip(self.pieces, self.outs)):
            rows = out.at[mine, pl.ds(pl.multiple_of(quad * 32, 32), 32)]
            local = pltpu.make_async_copy(piece.at[quad], rows, self.lsem.at[k])
            local.start()
            owned.append(local)
            for step in (1, 2, 3):
                to = moved(at, "quad", step)
                copy = remote(
                    piece.at[to["zl"] * 2 + to["c"]],
                    rows,
                    self.qs.at[k, step - 1],
                    self.qr.at[k, step - 1],
                    to,
                )
                copy.start()
                quads.append(copy)
        yield
        firsts, seconds = [], []
        for k, out in enumerate(self.outs):
            s, r = self.ssem, self.rsem
            firsts.append(Spread(at, "x", "y", out, near, 64, s.at[k, 0], r.at[k, 0]))
            seconds.append(Spread(at, "y", "x", out, far, 64, s.at[k, 1], r.at[k, 1]))
        for k, half in enumerate(firsts):
            owned[k].wait()
            quads[3 * k].wait_recv()
            half.one_a()
            half.two_a(0)
        yield
        for k, half in enumerate(seconds):
            quads[3 * k + 1].wait_recv()
            quads[3 * k + 2].wait_recv()
            half.one_a()
            half.two_a(0)
        yield
        yield from spread_rest(firsts + seconds)
        for copy in quads:
            copy.wait_send()

    @staticmethod
    def scratch(count):
        return [
            DMA((count, 2, 20)),
            DMA((count, 2, 20)),
            DMA((count, 3)),
            DMA((count, 3)),
            DMA((count,)),
        ]


def run(steps):
    for _ in steps:
        pass


class Gather:
    def __init__(self, at, first, second, src, lo, rows, one, two, ssem, rsem):
        self.at, self.f, self.s, self.src, self.lo, self.rows = at, first, second, src, lo, rows
        self.one, self.two, self.ssem, self.rsem = one, two, ssem, rsem

    def block(self, f, s):
        y, x = (f, s) if self.f == "y" else (s, f)
        return self.src.at[y * SIDE + x, pl.ds(self.lo, self.rows)]

    def start(self):
        self.sent = []
        for d in (2, 1, 3):
            f = lax.rem(self.at[self.f] + d, SIDE)
            for s in range(SIDE):
                k = (d - 1) * 4 + s
                copy = remote(
                    self.block(f, s),
                    self.one.at[d - 1, s],
                    self.ssem.at[k],
                    self.rsem.at[k],
                    moved(self.at, self.f, d),
                )
                copy.start()
                self.sent.append((d, s, copy))

    def arrived(self):
        for d, s, copy in self.sent:
            copy.wait_recv()

    def add(self, s, one):
        own = self.block(self.at[self.f], s)
        total = own[...].astype(F32)
        for d in range(3):
            total = total + one[d].astype(F32)
        own[...] = total.astype(BF)

    def onward(self):
        for d in (2, 1, 3):
            s = lax.rem(self.at[self.s] + d, SIDE)
            copy = remote(
                self.block(self.at[self.f], s),
                self.two.at[d - 1],
                self.ssem.at[11 + d],
                self.rsem.at[11 + d],
                moved(self.at, self.s, d),
            )
            copy.start()
            self.sent.append((d, 0, copy))

    def finish(self):
        for d, s, copy in self.sent[12:]:
            copy.wait_recv()
        total = self.block(self.at[self.f], self.at[self.s])[...].astype(F32)
        for d in range(3):
            total = total + self.two[d].astype(F32)
        return total

    def done(self):
        for d, s, copy in self.sent:
            copy.wait_send()


def middle_held(halves):
    for h in halves:
        h.arrived()

        def add(s, carry, h=h):
            h.add(s, h.one.at[:, s])
            return carry

        lax.fori_loop(0, SIDE, add, 0)
        h.onward()


def middle_staged(halves, stage, sems, onward=True):
    def load(k):
        h, s = halves[k // SIDE], k % SIDE
        return pltpu.make_async_copy(h.one.at[:, s], stage.at[k % 2], sems.at[k % 2])

    for k in range(SIDE * len(halves)):
        h, s = halves[k // SIDE], k % SIDE
        if s == 0:
            h.arrived()
        load(k).start()
        if k > 0:
            before = halves[(k - 1) // SIDE]
            load(k - 1).wait()
            before.add((k - 1) % SIDE, stage.at[(k - 1) % 2])
            if s == 0 and onward:
                before.onward()
    load(k).wait()
    h.add(s, stage.at[k % 2])
    if onward:
        h.onward()


class Grads:
    def __init__(self, at, src, out, one, two, total, ssem, rsem, qs, qr):
        self.at, self.out, self.total, self.qs, self.qr = at, out, total, qs, qr
        self.halves = [
            Gather(at, f, s, src, 64 * n, 64, one.at[n], two.at[n], ssem.at[n], rsem.at[n])
            for n, (f, s) in enumerate((("y", "x"), ("x", "y")))
        ]

    def start(self):
        for h in self.halves:
            h.start()

    def cut(self, quad):
        n = self.total.shape[2]
        if len(self.out.shape) == 2:
            return [(pl.ds(0, n), self.out.at[:, pl.ds(pl.multiple_of(quad * n, 128), n)])]
        n = n // 2
        columns = pl.ds(pl.multiple_of(quad * n, 128), n)
        return [(pl.ds(k * n, n), self.out.at[k, :, columns]) for k in (0, 1)]

    def finish(self):
        at, total = self.at, self.total
        quad = at["zl"] * 2 + at["c"]
        for n, h in enumerate(self.halves):
            total[n] = h.finish().astype(BF)
        self.quads = []
        for step in (3, 2, 1):
            to = moved(at, "quad", step)
            rows = pl.ds(pl.multiple_of(to["c"] * 32, 32), 32)
            for k, (columns, place_) in enumerate(self.cut(quad)):
                copy = remote(
                    total.at[to["zl"], rows, columns],
                    place_,
                    self.qs.at[step - 1, k],
                    self.qr.at[step - 1, k],
                    to,
                )
                copy.start()
                self.quads.append(copy)
        rows = pl.ds(pl.multiple_of(at["c"] * 32, 32), 32)
        for columns, place_ in self.cut(quad):
            place_[...] = total[at["zl"], rows, columns]

    def done(self):
        for copy in self.quads:
            copy.wait()
        for h in self.halves:
            h.done()

    @staticmethod
    def shape(n):
        return (2, 3, SIDE, 64, n)

    @staticmethod
    def scratch(n):
        return [
            pltpu.VMEM((2, 3, 64, n), BF),
            pltpu.VMEM((2, 64, n), BF),
            DMA((2, 15)),
            DMA((2, 15)),
            DMA((3, 2)),
            DMA((3, 2)),
        ]


class TeamGather:
    def __init__(self, at, out, ssem, rsem):
        self.at, self.out, self.ssem, self.rsem = at, out, ssem, rsem

    def start(self, src=None):
        at, out = self.at, self.out
        c, z = at["c"], at["zh"] * 2 + at["zl"]
        mine = out.at[place(z, c)]
        src = mine if src is None else src
        self.ring = []
        for k, d in enumerate((2, 1, -1)):
            copy = remote(src, mine, self.ssem.at[k], self.rsem.at[k], moved(at, "z", d))
            copy.start()
            self.ring.append(copy)
        copy = remote(src, mine, self.ssem.at[6], self.rsem.at[6], moved(at, "c"))
        copy.start()
        self.pair = [copy]

    def forward(self):
        at, out = self.at, self.out
        c, z = at["c"], at["zh"] * 2 + at["zl"]
        for k, d in ((1, 1), (2, -1), (0, 2)):
            slot = out.at[place(lax.rem(z - d + SIDE, SIDE), c)]
            self.ring[k].wait_recv()
            copy = remote(slot, slot, self.ssem.at[3 + k], self.rsem.at[3 + k], moved(at, "c"))
            copy.start()
            self.pair.append(copy)

    def finish(self):
        for copy in self.pair:
            copy.wait_recv()

    def done(self):
        for copy in self.ring + self.pair:
            copy.wait_send()


class TeamReduce:
    ORDER = (2, 1, -1, 0)

    def __init__(self, at, part, one, held, two, ssem, rsem):
        self.at, self.part, self.one, self.held, self.two = at, part, one, held, two
        self.ssem, self.rsem = ssem, rsem

    def slot(self, d, c):
        return place(lax.rem(self.at["zh"] * 2 + self.at["zl"] + d + SIDE, SIDE), c)

    def start(self):
        self.first, self.second = [], []
        for k, d in enumerate(self.ORDER):
            copy = remote(
                self.part.at[self.slot(d, 1 - self.at["c"])],
                self.one.at[k],
                self.ssem.at[k],
                self.rsem.at[k],
                moved(self.at, "c"),
            )
            copy.start()
            self.first.append(copy)

    def middle(self):
        for k, d in enumerate(self.ORDER):
            self.first[k].wait_recv()
            if d == 0:
                continue
            mine = self.part[self.slot(d, self.at["c"])].astype(F32)
            self.held[k] = (mine + self.one[k].astype(F32)).astype(BF)
            copy = remote(
                self.held.at[k],
                self.two.at[k],
                self.ssem.at[4 + k],
                self.rsem.at[4 + k],
                moved(self.at, "z", d),
            )
            copy.start()
            self.second.append(copy)

    def finish(self):
        total = self.part[self.slot(0, self.at["c"])].astype(F32) + self.one[3].astype(F32)
        for k in (1, 2, 0):
            self.second[k].wait_recv()
            total = total + self.two[k].astype(F32)
        return total

    def done(self):
        for copy in self.first + self.second:
            copy.wait_send()

    @staticmethod
    def scratch(count, width):
        return [
            pltpu.VMEM((4, count, width), BF),
            pltpu.VMEM((3, count, width), BF),
            pltpu.VMEM((3, count, width), BF),
            DMA((7,)),
            DMA((7,)),
        ]


class Sum:
    def __init__(self, at, value, pair, ring, row, column, ssem, rsem):
        self.at, self.value, self.ssem, self.rsem = at, value, ssem, rsem
        self.axes = (
            ("c", pair, at["c"]),
            ("z", ring, at["zh"] * 2 + at["zl"]),
            ("x", row, at["x"]),
            ("y", column, at["y"]),
        )

    def steps(self):
        k = 0
        for axis, buffer, me in self.axes:
            buffer[me] = self.value[...]
            copies = []
            for step in range(1, buffer.shape[0]):
                copy = remote(
                    buffer.at[me],
                    buffer.at[me],
                    self.ssem.at[k],
                    self.rsem.at[k],
                    moved(self.at, axis, step),
                )
                copy.start()
                copies.append(copy)
                k += 1
            yield
            for copy in copies:
                copy.wait()
            total = buffer[0]
            for n in range(1, buffer.shape[0]):
                total = total + buffer[n]
            self.value[...] = total

    @staticmethod
    def scratch(shape):
        return [pltpu.VMEM((n,) + shape, F32) for n in (2, 4, 4, 4)] + [DMA((10,)), DMA((10,))]


def dot_plain(a, b):
    return jnp.dot(a, b, preferred_element_type=F32)


def dot_last(a, b):
    return lax.dot_general(a, b, (((1,), (1,)), ((), ())), preferred_element_type=F32)


def dot_first(a, b):
    return lax.dot_general(a, b, (((0,), (0,)), ((), ())), preferred_element_type=F32)


def sweep(start, stop, body):
    pairs = jnp.maximum(stop - start, 0) // 2

    def two(n, carry):
        body(start + 2 * n)
        body(start + 2 * n + 1)
        return carry

    def one(n, carry):
        body(n)
        return carry

    lax.fori_loop(0, pairs, two, 0)
    lax.fori_loop(start + 2 * pairs, stop, one, 0)


def lanes_of(value):
    return lax.broadcasted_iota(jnp.int32, value.shape, 1)


def turn(value):
    low = lax.rem(lanes_of(value), 64) < 32
    return jnp.where(low, -pltpu.roll(value, 96, 1), pltpu.roll(value, 32, 1))


def head_gains(gains_ref):
    both = gains_ref[32:33]
    other = pltpu.roll(both, 64, 1)
    left = lanes_of(both) < 64
    return jnp.where(left, both, other), jnp.where(left, other, both)


def wide_gain(gains_ref, first):
    return jnp.concatenate([gains_ref[n : n + 1] for n in range(first, first + 16)], axis=1)


def numbers(seg_ref, block):
    parts = [seg_ref[pl.ds(block * 4 + n, 1)].astype(F32) for n in range(4)]
    return jnp.concatenate(parts, axis=1)


def upright(row):
    return jnp.broadcast_to(row, (8, row.shape[1])).T[:, :1]


def normalize(value):
    left = lanes_of(value) < 64
    square = value * value
    one = jnp.sum(jnp.where(left, square, 0.0), axis=-1, keepdims=True)
    two = jnp.sum(jnp.where(left, 0.0, square), axis=-1, keepdims=True)
    return value * lax.rsqrt(jnp.where(left, one, two) / HD + EPS_NORM)


def forward_kernel(*refs):
    (x_ref, ct_ref, gains_ref, cos_ref, sin_ref, seg_ref) = refs[:6]
    weights = refs[6:11]
    (rows_out, grads_out, joined_out, output_out, expand_out, reduce_out) = refs[11:17]
    (projected_out, queries_out, every_out, out_ref, attn_out, middle_out, ffn_out) = refs[17:24]
    sum_ref, part = refs[24:26]
    reduce_scratch = refs[26:31]
    small_scratch, large_scratch = refs[31:36], refs[36:41]
    ks, kr, gs, gr, lsem = refs[41:46]
    pieces = refs[46:50]
    results = (rows_out, joined_out, output_out, every_out)
    rows_out, joined_out, output_out, every_out = refs[50:54]
    buffers, psem = refs[50:54], refs[54]

    def park(n):
        copy = pltpu.make_async_copy(buffers[n], results[n], psem.at[n])
        copy.start()
        return copy

    at = here()
    team = at["y"] * SIDE + at["x"]
    me = place(at["zh"] * 2 + at["zl"], at["c"])
    rows = queries_out.shape[1]
    sources = ((0, 0, 0, 384), (1, 1, 0, 256), (2, 2, 0, 1024), (3, 2, 1024, 1024), (4, 3, 0, 1024))
    for source, piece, to, n in sources:
        for t in range(4):
            value = weights[source][:, n * t : n * t + n]
            pieces[piece][t, :, to : to + n] = value.astype(BF)
    greet(at, RING + NEAR + QUAD[1:])

    small = Weights(at, pieces[:2], [joined_out, output_out], *small_scratch).steps()
    large = Weights(at, pieces[2:], [expand_out, reduce_out], *large_scratch).steps()
    next(small)

    residual = x_ref[...].astype(F32)
    scale = lax.rsqrt(jnp.mean(residual * residual, axis=-1, keepdims=True) + EPS_NORM)
    rows_out[me] = (residual * scale * wide_gain(gains_ref, 0)).astype(BF)
    gather = TeamGather(at, rows_out, gs.at[0], gr.at[0])
    gather.start()
    run(small)
    gather.forward()
    next(large)
    gather.finish()

    projected_out[...] = jnp.dot(
        rows_out[...].reshape(rows, D),
        joined_out[...].reshape(D, 384),
        preferred_element_type=F32,
    )
    next(large)
    parked = [park(0), park(1), park(2)]
    query_gain, key_gain = head_gains(gains_ref)
    cosine, sine = cos_ref[...], sin_ref[...]
    left = lax.broadcasted_iota(jnp.int32, (rows, 128), 1) < 64
    raw = projected_out[:, 256:]
    key = normalize(raw) * key_gain
    key = key * cosine + turn(key) * sine
    every_out[team] = jnp.where(left, key, raw).astype(BF)
    halves = [
        Spread(at, "x", "y", every_out, 0, rows // 2, ks.at[0], kr.at[0]),
        Spread(at, "y", "x", every_out, rows // 2, rows // 2, ks.at[1], kr.at[1]),
    ]
    for h in halves:
        h.one_a()
        h.two_a(0)
    for n in range(2):
        query = normalize(projected_out[:, 128 * n : 128 * n + 128]) * query_gain
        query = query * cosine + turn(query) * sine
        query = query.astype(BF).astype(F32) * (HD**-0.5)
        queries_out[2 * n] = jnp.where(left, query, 0.0).astype(BF)
        queries_out[2 * n + 1] = jnp.where(left, pltpu.roll(query, 64, 1), 0.0).astype(BF)
    run(spread_rest(halves))
    parked.append(park(3))
    local = pltpu.make_async_copy(ct_ref, grads_out.at[me], lsem)
    local.start()
    cotangents = TeamGather(at, grads_out, gs.at[1], gr.at[1])
    cotangents.start(ct_ref)
    next(large)

    out_ref[...] = jnp.zeros_like(out_ref)
    sum_ref[...] = jnp.zeros_like(sum_ref)

    def block(number, allowed):
        pairs = every_out[number]
        for h in range(GROUP_HEADS):
            weights = jnp.exp(dot_last(queries_out[h], pairs))
            if allowed is not None:
                weights = jnp.where(allowed, weights, 0.0)
            add = weights[:, :128]
            for lane in range(128, rows, 128):
                add = add + weights[:, lane : lane + 128]
            sum_ref[h] += add
            out_ref[h] += jnp.dot(weights.astype(BF), pairs, preferred_element_type=F32)

    def inner(number):
        block(number, None)

    sweep(1, jnp.maximum(team - 6, 1), inner)
    next(large)
    sweep(jnp.maximum(team - 6, 1), team, inner)
    next(large)
    own = upright(numbers(seg_ref, team))
    main = (own == seg_ref[0:1, 127:128].astype(F32)).astype(F32)
    for h in range(GROUP_HEADS):
        out_ref[h] *= main
        sum_ref[h] *= main

    def edge(step, carry):
        number = step * team
        ahead = (number - team) * rows
        row = lax.broadcasted_iota(jnp.int32, (rows, rows), 0)
        column = lax.broadcasted_iota(jnp.int32, (rows, rows), 1) + ahead
        block(number, (column <= row) & (own == numbers(seg_ref, number)))
        return carry

    lax.fori_loop(jnp.where(team == 0, 1, 0), 2, edge, 0)
    cotangents.forward()
    for h in range(GROUP_HEADS):
        total = jnp.sum(sum_ref[h], axis=-1, keepdims=True)
        sum_ref[h] = jnp.broadcast_to(total, sum_ref.shape[1:])
        out_ref[h] = jnp.where(left, sum_ref[h], out_ref[h] / sum_ref[h])
    for n in range(2):
        one, two = out_ref[2 * n], out_ref[2 * n + 1]
        attn_out[:, 128 * n : 128 * n + 128] = jnp.where(left, pltpu.roll(one, 64, 1), two).astype(BF)

    def project(n, carry):
        columns = pl.ds(pl.multiple_of(n * 512, 512), 512)
        weight = output_out[pl.ds(n * 4, 4)].reshape(512, 256)
        branch = dot_last(attn_out[...], weight).astype(BF)
        part[:, :, columns] = branch.reshape(TEAM, 64, 512)
        return carry

    lax.fori_loop(0, 4, project, 0)
    branch = TeamReduce(at, part, *reduce_scratch)
    branch.start()
    branch.middle()
    next(large)
    middle = residual + branch.finish()
    middle_out[...] = middle
    scale = lax.rsqrt(jnp.mean(middle * middle, axis=-1, keepdims=True) + EPS_NORM)
    ffn_out[me] = (middle * scale * wide_gain(gains_ref, 16)).astype(BF)
    second = TeamGather(at, ffn_out, gs.at[2], gr.at[2])
    second.start()
    next(large)
    second.forward()
    next(large)
    second.finish()
    run(large)
    cotangents.finish()
    local.wait()
    for transfer in (gather, cotangents, second, branch):
        transfer.done()
    for copy in parked:
        copy.wait()


def forward(x, ct, gains, cosine, sine, segs, weights, cid):
    rows = TEAM * 64

    def out(shape, kind=BF):
        return jax.ShapeDtypeStruct(shape, kind)

    return pl.pallas_call(
        forward_kernel,
        out_shape=[
            out((TEAM, 64, D)),
            out((TEAM, 64, D)),
            out((TEAMS, 128, 384)),
            out((TEAMS, 128, 256)),
            out((TEAMS, 128, 2048)),
            out((TEAMS, 128, 1024)),
            out((rows, 384), F32),
            out((GROUP_HEADS, rows, 128)),
            out((TEAMS, rows, 128)),
            out((GROUP_HEADS, rows, 128), F32),
            out((rows, 256)),
            out((64, D), F32),
            out((TEAM, 64, D)),
        ],
        in_specs=[VM, ANY] + [VM] * 9,
        out_specs=[ANY] * 6 + [VM, VM, ANY] + [VM] * 4,
        scratch_shapes=[pltpu.VMEM((GROUP_HEADS, rows, 128), F32), pltpu.VMEM((TEAM, 64, D), BF)]
        + TeamReduce.scratch(64, D)
        + Weights.scratch(2)
        + Weights.scratch(2)
        + [DMA((2, 20)), DMA((2, 20)), DMA((3, 7)), DMA((3, 7)), DMA]
        + [pltpu.VMEM((4, 32, n), BF) for n in (384, 256, 2048, 1024)]
        + [
            pltpu.VMEM((TEAM, 64, D), BF),
            pltpu.VMEM((TEAMS, 128, 384), BF),
            pltpu.VMEM((TEAMS, 128, 256), BF),
            pltpu.VMEM((TEAMS, rows, 128), BF),
            DMA((4,)),
        ],
        compiler_params=params(cid, 56),
    )(x, ct, gains, cosine, sine, segs, *weights)


def norm_back(value, gain, grad):
    scale = lax.rsqrt(jnp.mean(value * value, axis=-1, keepdims=True) + EPS_NORM)
    unit = value * scale
    inner = grad * gain
    back = scale * (inner - unit * jnp.mean(inner * unit, axis=-1, keepdims=True))
    return back, jnp.sum(grad * unit, axis=0, keepdims=True)


def back_kernel(*refs):
    (rows_any, grads_any, middle_ref, ct_ref, x_ref, gains_ref, cos_ref, sin_ref, seg_ref) = refs[:9]
    refs = refs[:7] + (None,) * 4 + refs[7:]
    expand_any, reduce_any = refs[13:15]
    late_any = refs[15:23]
    block_out, input_out, sum_out, expand_out, reduce_out, output_out, joined_out = refs[23:30]
    expand_one, reduce_one = refs[30:32]
    expand_ref, reduce_ref, hidden_ref, both_ref, part, branch_ref, back_ref, grad_ref = refs[32:40]
    (joined_ref, output_ref, q_ref, kv_ref, out_ref, attn_ref, projected_ref) = refs[40:47]
    inner_ref, innerm_ref, dq_ref, dkv_ref = refs[47:51]
    output_grad, joined_grad, output_one, joined_one = refs[51:55]
    expand_sems, reduce_sems, output_sems, joined_sems = (
        refs[55:61],
        refs[61:67],
        refs[67:73],
        refs[73:79],
    )
    first_scratch, second_scratch = refs[79:84], refs[84:89]
    kv_one, kv_two, ks, kr, stage, stage_sem, gs, gr, wsem, lsem = refs[89:99]
    rows_ref, grads_ref, isem = refs[99:102]
    sum_scratch = refs[102:]
    late_refs = refs[40:47] + (rows_ref,)
    slabs = [both_ref.at[:, pl.ds(128 * n, 128)] for n in range(3 * GROUP_HEADS)]
    do_refs, qm_refs, dom_refs = (slabs[n : n + GROUP_HEADS] for n in (0, 4, 8))
    q_refs = [q_ref.at[h] for h in range(GROUP_HEADS)]
    gp_ref = hidden_ref.at[:, pl.ds(0, 384)]
    at = here()
    me = place(at["zh"] * 2 + at["zl"], at["c"])
    team = at["y"] * SIDE + at["x"]
    rows = TEAM * 64
    late = [
        pltpu.make_async_copy(src, dst, lsem.at[n])
        for n, (src, dst) in enumerate(zip(late_any, late_refs))
    ]

    def loads(n):
        low = pl.ds(pl.multiple_of(n * 256, 256), 256)
        high = pl.ds(pl.multiple_of(n * 256 + 1024, 256), 256)
        return [
            pltpu.make_async_copy(any_.at[:, :, part_], ref.at[:, :, part_], wsem.at[n, k])
            for k, (any_, ref, part_) in enumerate(
                (
                    (expand_any, expand_ref, low),
                    (expand_any, expand_ref, high),
                    (reduce_any, reduce_ref, low),
                )
            )
        ]

    inputs = [
        pltpu.make_async_copy(rows_any, rows_ref, isem.at[0]),
        pltpu.make_async_copy(grads_any, grads_ref, isem.at[1]),
    ]
    for copy in inputs:
        copy.start()
    for n in range(4):
        for copy in loads(n):
            copy.start()
    greet(at, RING + FAR + QUAD[1:])
    for copy in late[:-1]:
        copy.start()
    for copy in inputs:
        copy.wait()
    ffn_values = rows_ref[...].reshape(rows, D)
    grad_values = grads_ref[...].reshape(rows, D)

    def feed(n, carry):
        for copy in loads(n):
            copy.wait()
        low = pl.ds(pl.multiple_of(n * 256, 256), 256)
        high = pl.ds(pl.multiple_of(n * 256 + 1024, 256), 256)
        gate = dot_plain(ffn_values, expand_ref[:, :, low].reshape(D, 256))
        up = dot_plain(ffn_values, expand_ref[:, :, high].reshape(D, 256))
        grad = dot_plain(grad_values, reduce_ref[:, :, low].reshape(D, 256))
        open_ = 1.0 / (1.0 + jnp.exp(-gate))
        silu = gate * open_
        hidden_ref[:, low] = (silu * up).astype(BF)
        both_ref[:, low] = (grad * up * (open_ + silu * (1.0 - open_))).astype(BF)
        both_ref[:, high] = (grad * silu).astype(BF)
        return carry

    lax.fori_loop(0, 4, feed, 0)

    def project(n, carry):
        columns = pl.ds(pl.multiple_of(n * 512, 512), 512)
        weight = expand_ref[pl.ds(n * 4, 4)].reshape(512, 2048)
        part[:, :, columns] = dot_last(both_ref[...], weight).astype(BF).reshape(TEAM, 64, 512)
        return carry

    lax.fori_loop(0, 4, project, 0)
    first = TeamReduce(at, part, *first_scratch)
    first.start()

    def branch(n, carry):
        columns = pl.ds(pl.multiple_of(n * 512, 512), 512)
        weight = reduce_ref[pl.ds(n * 4, 4)].reshape(512, 1024)
        value = dot_last(hidden_ref[...], weight).astype(BF)
        branch_ref[:, :, columns] = value.reshape(TEAM, 64, 512)
        return carry

    first.middle()
    lax.fori_loop(0, 4, branch, 0)

    def grad_reduce(n, carry):
        columns = pl.ds(pl.multiple_of(n * 256, 256), 256)
        grad = dot_first(grads_ref[:, :, columns].reshape(rows, 256), hidden_ref[...])
        reduce_ref[pl.ds(n * 2, 2)] = grad.astype(BF).reshape(2, 128, 1024)
        return carry

    lax.fori_loop(0, 8, grad_reduce, 0)
    reduced = Grads(at, reduce_ref, reduce_out, reduce_one, *reduce_sems)
    reduced.start()

    back, gain = norm_back(middle_ref[...], wide_gain(gains_ref, 16), first.finish())
    ffn_gain = gain
    grad_middle = ct_ref[...].astype(F32) + back
    grad_ref[...] = grad_middle
    back_ref[me] = grad_middle.astype(BF)
    gather = TeamGather(at, back_ref, gs, gr)
    gather.start()

    def grad_expand(n, carry):
        columns = pl.ds(pl.multiple_of(n * 256, 256), 256)
        grad = dot_first(rows_ref[:, :, columns].reshape(rows, 256), both_ref[...])
        expand_ref[pl.ds(n * 2, 2)] = grad.astype(BF).reshape(2, 128, 2048)
        return carry

    lax.fori_loop(0, 8, grad_expand, 0)
    late[-1].start()
    expanded = Grads(at, expand_ref, expand_out, expand_one, *expand_sems)
    expanded.start()
    gather.forward()
    gather.finish()
    for copy in late[:-1]:
        copy.wait()
    branch = TeamReduce(at, branch_ref, *second_scratch)
    branch.start()

    attended = dot_plain(back_ref[...].reshape(rows, D), output_ref[...].reshape(D, 256))
    left = lax.broadcasted_iota(jnp.int32, (rows, 128), 1) < 64
    ones = jnp.ones((8, 128), BF)
    own = numbers(seg_ref, team)
    main = (own == seg_ref[0:1, 127:128].astype(F32)).astype(F32)
    low = upright(main).astype(BF)
    dq_ref[...] = jnp.zeros_like(dq_ref)
    for h in range(GROUP_HEADS):
        grad = attended[:, 128 * (h // 2) : 128 * (h // 2) + 128]
        if h % 2 == 0:
            grad = pltpu.roll(grad, 64, 1)
        value = out_ref[h]
        scaled = jnp.where(left, 0.0, grad / value[:, :1]).astype(BF)
        do_refs[h][...] = scaled
        inner = jnp.where(left, 0.0, scaled.astype(F32) * value)
        high = inner.astype(BF)
        rest = (inner - high.astype(F32)).astype(BF)
        inner_ref[h] = (dot_last(ones, high) + dot_last(ones, rest))[0:1]
        qm_refs[h][...] = q_ref[h] * low
        dom_refs[h][...] = scaled * low
        innerm_ref[h] = inner_ref[h] * main

    def grad_output(n, carry):
        columns = pl.ds(pl.multiple_of(n * 256, 256), 256)
        grad = dot_first(back_ref[:, :, columns].reshape(rows, 256), attn_ref[...])
        output_grad[pl.ds(n * 2, 2)] = grad.astype(BF).reshape(2, 128, 256)
        return carry

    lax.fori_loop(0, 8, grad_output, 0, unroll=True)
    output = Grads(at, output_grad, output_out, output_one, *output_sems)
    output.start()
    branch.middle()

    def block(number, allowed, q, do, inner):
        pairs = kv_ref[number]
        total = jnp.zeros(pairs.shape, F32)
        for h in range(GROUP_HEADS):
            query, above = q[h][...], do[h][...]
            weights = jnp.exp(dot_last(pairs, query))
            if allowed is not None:
                weights = jnp.where(allowed, weights, 0.0)
            grad = (weights * (dot_last(pairs, above) - inner[h])).astype(BF)
            total = total + dot_plain(grad, query)
            total = total + dot_plain(weights.astype(BF), above)
            dq_ref[h] += dot_first(pairs, grad)
        dkv_ref[number] = total.astype(BF)

    def interior(number, carry):
        block(number, None, qm_refs, dom_refs, innerm_ref)
        return carry

    lax.fori_loop(1, team, interior, 0)

    def edge(step, carry):
        number = step * team
        ahead = (number - team) * rows
        row = lax.broadcasted_iota(jnp.int32, (rows, rows), 1)
        column = lax.broadcasted_iota(jnp.int32, (rows, rows), 0) + ahead
        allowed = (column <= row) & (upright(numbers(seg_ref, number)) == own)
        block(number, allowed, q_refs, do_refs, inner_ref)
        return carry

    lax.fori_loop(jnp.where(team == 0, 1, 0), 2, edge, 0)

    def rest_of(number, carry):
        dkv_ref[number] = jnp.zeros(dkv_ref.shape[1:], BF)
        return carry

    lax.fori_loop(team + 1, TEAMS, rest_of, 0)
    half = rows // 2
    pairs = [
        Gather(at, f, s, dkv_ref, half * n, half, kv_one.at[n], kv_two.at[n], ks.at[n], kr.at[n])
        for n, (f, s) in enumerate((("y", "x"), ("x", "y")))
    ]
    for h in pairs:
        h.start()
    block_out[...] = (middle_ref[...] + branch.finish()).astype(BF)

    cosine, sine = cos_ref[...], sin_ref[...]
    head_gain = head_gains(gains_ref)

    def prepare_back(raw, gain, grad):
        unit = normalize(raw)
        square = raw * raw
        across = jnp.sum(jnp.where(left, square, 0.0), axis=-1, keepdims=True)
        along = jnp.sum(jnp.where(left, 0.0, square), axis=-1, keepdims=True)
        scale = lax.rsqrt(jnp.where(left, across, along) / HD + EPS_NORM)
        grad = grad * cosine - turn(grad * sine)
        gain_grad = jnp.sum(grad * unit, axis=0, keepdims=True)
        grad = grad * gain
        inner = grad * unit
        across = jnp.sum(jnp.where(left, inner, 0.0), axis=-1, keepdims=True)
        along = jnp.sum(jnp.where(left, 0.0, inner), axis=-1, keepdims=True)
        return scale * (grad - unit * (jnp.where(left, across, along) / HD)), gain_grad

    query_gain = jnp.zeros((1, 128), F32)
    for n in range(2):
        both = jnp.concatenate([dq_ref[2 * n, :64], dq_ref[2 * n + 1, :64]], axis=0)
        columns = slice(128 * n, 128 * n + 128)
        grad, gain = prepare_back(
            projected_ref[:, columns], head_gain[0], both.T * (HD**-0.5)
        )
        query_gain = query_gain + gain
        gp_ref[:, columns] = grad.astype(BF)
    middle_staged(reduced.halves, stage.at[:, :, :, pl.ds(0, 1024)], stage_sem, False)
    middle_held(pairs)
    for h in reduced.halves:
        h.onward()
    middle_staged(expanded.halves, stage, stage_sem)
    middle_held(output.halves)
    pair_grad = jnp.concatenate([h.finish() for h in pairs], axis=0)
    grad, key_gain = prepare_back(projected_ref[:, 256:], head_gain[1], pair_grad)
    gp_ref[:, 256:] = jnp.where(left, grad, pair_grad).astype(BF)

    first.done()

    def project(n, carry):
        columns = pl.ds(pl.multiple_of(n * 512, 512), 512)
        weight = joined_ref[pl.ds(n * 4, 4)].reshape(512, 384)
        part[:, :, columns] = dot_last(gp_ref[...], weight).astype(BF).reshape(TEAM, 64, 512)
        return carry

    lax.fori_loop(0, 4, project, 0)
    last = TeamReduce(at, part, *first_scratch)
    last.start()
    late[-1].wait()

    def grad_joined(n, carry):
        columns = pl.ds(pl.multiple_of(n * 256, 256), 256)
        grad = dot_first(rows_ref[:, :, columns].reshape(rows, 256), gp_ref[...])
        joined_grad[pl.ds(n * 2, 2)] = grad.astype(BF).reshape(2, 128, 384)
        return carry

    last.middle()
    lax.fori_loop(0, 8, grad_joined, 0)
    joined = Grads(at, joined_grad, joined_out, joined_one, *joined_sems)
    joined.start()
    reduced.finish()
    back, gain = norm_back(x_ref[...].astype(F32), wide_gain(gains_ref, 0), last.finish())
    input_out[...] = (grad_ref[...] + back).astype(BF)
    for n in range(16):
        columns = slice(128 * n, 128 * n + 128)
        sum_out[n : n + 1, :] = gain[:, columns]
        sum_out[16 + n : 17 + n, :] = ffn_gain[:, columns]
    query_gain = query_gain + pltpu.roll(query_gain, 64, 1)
    lane = lax.broadcasted_iota(jnp.int32, (1, 128), 1)
    sum_out[32:33, :] = jnp.where(lane < 64, query_gain, pltpu.roll(key_gain, 64, 1))
    sums = Sum(at, sum_out, *sum_scratch).steps()
    next(sums)
    expanded.finish()
    next(sums)
    output.finish()
    middle_held(joined.halves)
    next(sums)
    next(sums)
    joined.finish()
    run(sums)
    for transfer in (reduced, expanded, output, joined, branch, last, gather):
        transfer.done()
    for h in pairs:
        h.done()


def backward(arrays, expand_all, reduce_all, late, cid):
    rows = TEAM * 64

    def out(shape, kind=BF):
        return jax.ShapeDtypeStruct(shape, kind)

    return pl.pallas_call(
        back_kernel,
        out_shape=[
            out((64, D)),
            out((64, D)),
            out((33, 128), F32),
            out((2, 32, 4096)),
            out((32, 4096)),
            out((32, 1024)),
            out((32, 1536)),
            out(Grads.shape(2048)),
            out(Grads.shape(1024)),
        ],
        in_specs=[ANY] * 2 + [VM] * (len(arrays) - 2) + [ANY] * (2 + len(late)),
        out_specs=[VM] * 7 + [ANY] * 2,
        scratch_shapes=[
            pltpu.VMEM((TEAMS, 128, 2048), BF),
            pltpu.VMEM((TEAMS, 128, 1024), BF),
            pltpu.VMEM((rows, 1024), BF),
            pltpu.VMEM((rows, 2048), BF),
            pltpu.VMEM((TEAM, 64, D), BF),
            pltpu.VMEM((TEAM, 64, D), BF),
            pltpu.VMEM((TEAM, 64, D), BF),
            pltpu.VMEM((64, D), F32),
        ]
        + [pltpu.VMEM(v.shape, v.dtype) for v in late[:-1]]
        + [
            pltpu.VMEM((GROUP_HEADS, 1, rows), F32),
            pltpu.VMEM((GROUP_HEADS, 1, rows), F32),
            pltpu.VMEM((GROUP_HEADS, 128, rows), F32),
            pltpu.VMEM((TEAMS, rows, 128), BF),
            pltpu.VMEM((TEAMS, 128, 256), BF),
            pltpu.VMEM((TEAMS, 128, 384), BF),
            pltpu.VMEM(Grads.shape(256), BF),
            pltpu.VMEM(Grads.shape(384), BF),
        ]
        + Grads.scratch(2048)
        + Grads.scratch(1024)
        + Grads.scratch(256)
        + Grads.scratch(384)
        + TeamReduce.scratch(64, D)
        + TeamReduce.scratch(64, D)
        + [
            pltpu.VMEM((2, 3, SIDE, rows // 2, 128), BF),
            pltpu.VMEM((2, 3, rows // 2, 128), BF),
            DMA((2, 15)),
            DMA((2, 15)),
            pltpu.VMEM((2, 3, 64, 2048), BF),
            DMA((2,)),
            DMA((7,)),
            DMA((7,)),
            DMA((4, 3)),
            DMA((len(late),)),
            pltpu.VMEM((TEAM, 64, D), BF),
            pltpu.VMEM((TEAM, 64, D), BF),
            DMA((2,)),
        ]
        + Sum.scratch((33, 128)),
        compiler_params=params(cid, 63),
    )(*arrays, expand_all, reduce_all, *late)[:7]


def on_device(
    block_in,
    cotangent,
    segments,
    gains,
    joined_weight,
    output_weight,
    expand_weight,
    reduce_weight,
    gains_first,
    gains_squares,
    joined_first,
    joined_squares,
    output_first,
    output_squares,
    expand_first,
    expand_squares,
    reduce_first,
    reduce_squares,
):
    team = lax.axis_index("y") * SIDE + lax.axis_index("x")
    rows = TEAM * 64
    positions = jnp.arange(rows, dtype=jnp.int32) + team * rows
    inverse = THETA ** (-(jnp.arange(0, HD, 2).astype(F32) / HD))
    angles = positions.astype(F32)[:, None] * inverse[None, :]
    cosine, sine = jnp.tile(jnp.cos(angles), (1, 4)), jnp.tile(jnp.sin(angles), (1, 4))
    lines = gains.reshape(33, 128)
    segs = segments.reshape(-1, 128)
    (
        attn_rows,
        grad_rows,
        joined_all,
        output_all,
        expand_all,
        reduce_all,
        projected,
        queries,
        every,
        attended,
        attn_out,
        middle,
        ffn_rows,
    ) = forward(
        block_in,
        cotangent,
        lines,
        cosine,
        sine,
        segs,
        [
            joined_weight.reshape(32, 1536),
            output_weight,
            expand_weight[:, 0],
            expand_weight[:, 1],
            reduce_weight,
        ],
        1,
    )
    (
        block_out,
        input_grad,
        gain_grad,
        shard_expand,
        shard_reduce,
        shard_output,
        shard_joined,
    ) = backward(
        [
            ffn_rows,
            grad_rows,
            middle,
            cotangent,
            block_in,
            lines,
            cosine,
            sine,
            segs,
        ],
        expand_all,
        reduce_all,
        [joined_all, output_all, queries, every, attended, attn_out, projected, attn_rows],
        2,
    )
    gain_grad = gain_grad.reshape(-1)
    shard_joined = shard_joined.reshape(32, 4, 384).astype(F32)
    shard_output = shard_output.astype(F32)
    shard_expand = shard_expand.transpose(1, 0, 2).astype(F32)
    shard_expand = with_layout_constraint(shard_expand, Layout(major_to_minor=(0, 1, 2)))
    shard_reduce = shard_reduce.astype(F32)
    joined = adamw(joined_weight, shard_joined, joined_first, joined_squares, D ** (-0.5))
    output = adamw(
        output_weight, shard_output, output_first, output_squares, max(1, H * HD // 128) ** (-0.5)
    )
    expand = adamw(expand_weight, shard_expand, expand_first, expand_squares, D ** (-0.5))
    reduce_new = adamw(reduce_weight, shard_reduce, reduce_first, reduce_squares, FF ** (-0.5))
    gain_new = adamw(gains, gain_grad, gains_first, gains_squares, GAIN_RATE)
    return (
        block_out,
        input_grad,
        joined[0],
        joined[1],
        joined[2],
        joined[2].astype(BF),
        output[0],
        output[1],
        output[2],
        output[2].astype(BF),
        expand[0],
        expand[1],
        expand[2],
        expand[2].astype(BF),
        reduce_new[0],
        reduce_new[1],
        reduce_new[2],
        reduce_new[2].astype(BF),
        gain_new[0],
        gain_new[1],
        gain_new[2],
    )


def solution(mesh):
    physical = Mesh(mesh.devices.reshape(SIDE, SIDE, 2, 2, 2), AXES)
    rows = P(AXES, None)
    joined = P(SEQ, "zh", None)
    plain = P(SEQ, "zh")
    expand = P(SEQ, None, "zh")
    placed = (
        (rows, rows, P(), P(), joined, plain, expand, plain, P(), P())
        + (joined,) * 2
        + (plain,) * 2
        + (expand,) * 2
        + (plain,) * 2
    )
    return jax.shard_map(
        on_device,
        mesh=physical,
        in_specs=placed,
        out_specs=(rows, rows)
        + (joined,) * 4
        + (plain,) * 4
        + (expand,) * 4
        + (plain,) * 4
        + (P(),) * 3,
        check_vma=False,
    )
```

```python
import functools

import jax
import jax.numpy as jnp
from jax import lax
from jax.experimental import pallas as pl
from jax.experimental.layout import Layout, with_layout_constraint
from jax.experimental.pallas import tpu as pltpu
from jax.sharding import Mesh
from jax.sharding import PartitionSpec as P

D = 2048
H = 32
HD = 64
FF = 8192
STEP = 10

EPS_NORM = 1e-05
THETA = 1000000.0
BETA_ONE = 0.5
BETA_TWO = 0.5
ADAM_EPS = 1e-08
DECAY = 0.1
GAIN_RATE = 0.2

AXES = ("y", "x", "zl", "c", "zh")
SEQ = ("y", "x", "zl", "c")
SIDE = 4
TEAMS = 16
TEAM = 8
GROUP_HEADS = 4
BF = jnp.bfloat16
F32 = jnp.float32
MESHID = pl.DeviceIdType.MESH
ANY = pl.BlockSpec(memory_space=pl.ANY)
VM = pl.BlockSpec(memory_space=pltpu.VMEM)
DMA = pltpu.SemaphoreType.DMA


def adamw(master, gradient, first, second, rate):
    moment = BETA_ONE * first + (1.0 - BETA_ONE) * gradient
    squares = BETA_TWO * second + (1.0 - BETA_TWO) * gradient * gradient
    scaled_one = moment / (1.0 - BETA_ONE**STEP)
    scaled_two = squares / (1.0 - BETA_TWO**STEP)
    updated = master - rate * (scaled_one / (jnp.sqrt(scaled_two) + ADAM_EPS) + DECAY * master)
    return (moment, squares, updated)


def here():
    return {a: lax.axis_index(a) for a in AXES}


def moved(at, axis, step=1):
    to = dict(at)
    if axis == "z":
        z = lax.rem(at["zh"] * 2 + at["zl"] + step + SIDE, SIDE)
        to["zh"] = z // 2
        to["zl"] = lax.rem(z, 2)
    elif axis == "quad":
        if step & 1:
            to["c"] = 1 - at["c"]
        if step & 2:
            to["zl"] = 1 - at["zl"]
    elif axis == "c":
        to["c"] = 1 - at["c"]
    else:
        to[axis] = lax.rem(at[axis] + step + SIDE, SIDE)
    return to


def ident(at):
    return tuple(at[a] for a in AXES)


def greet(at, moves):
    barrier = pltpu.get_barrier_semaphore()
    for axis, step in moves:
        pl.semaphore_signal(
            barrier, inc=1, device_id=ident(moved(at, axis, step)), device_id_type=MESHID
        )
    pl.semaphore_wait(barrier, len(moves))


def remote(src, dst, ssem, rsem, to):
    return pltpu.make_async_remote_copy(
        src_ref=src,
        dst_ref=dst,
        send_sem=ssem,
        recv_sem=rsem,
        device_id=ident(to),
        device_id_type=MESHID,
    )


def params(cid, vmem=48):
    return pltpu.CompilerParams(
        collective_id=cid, has_side_effects=True, vmem_limit_bytes=vmem << 20
    )


def place(z, c):
    return (lax.rem(z, 2) * 2 + c) * 2 + z // 2


QUAD = (("quad", 1), ("quad", 2), ("quad", 3))
NEAR = (("x", 1), ("x", -1), ("y", 1), ("y", -1))
FAR = tuple((axis, step) for axis in ("x", "y") for step in (1, 2, 3))
RING = (("z", 1), ("z", -1), ("z", 2), ("c", 1))


class Spread:
    def __init__(self, at, first, second, out, lo, rows, ssem, rsem):
        self.at, self.f, self.s, self.out = at, first, second, out
        self.lo, self.rows, self.ssem, self.rsem = lo, rows, ssem, rsem
        self.sent = []

    def slot(self, df, ds, part=None):
        f = lax.rem(self.at[self.f] + df + SIDE, SIDE)
        s = lax.rem(self.at[self.s] + ds + SIDE, SIDE)
        y, x = (f, s) if self.f == "y" else (s, f)
        lo, n = self.lo, self.rows
        if part is not None:
            n = n // 2
            lo = lo + part * n
        return self.out.at[y * SIDE + x, pl.ds(lo, n)]

    def send(self, block, k, axis, step):
        copy = remote(block, block, self.ssem.at[k], self.rsem.at[k], moved(self.at, axis, step))
        copy.start()
        self.sent.append(copy)

    def wait(self, block, k):
        to = moved(self.at, self.f, 1)
        remote(block, block, self.ssem.at[k], self.rsem.at[k], to).wait_recv()

    def one_a(self):
        self.send(self.slot(0, 0), 0, self.f, 1)
        self.send(self.slot(0, 0), 1, self.f, -1)

    def one_b(self, side):
        df = -1 if side == 0 else 1
        self.wait(self.slot(df, 0), side)
        self.send(self.slot(df, 0, side), 2 + side, self.f, -df)

    def one_c(self):
        self.wait(self.slot(2, 0, 0), 2)
        self.wait(self.slot(2, 0, 1), 3)

    STEPS = (0, -1, 1, 2)

    def two_a(self, j):
        block = self.slot(self.STEPS[j], 0)
        self.send(block, 4 + 4 * j, self.s, 1)
        self.send(block, 5 + 4 * j, self.s, -1)

    def two_b(self, j, side):
        ds = -1 if side == 0 else 1
        self.wait(self.slot(self.STEPS[j], ds), 4 + 4 * j + side)
        self.send(self.slot(self.STEPS[j], ds, side), 6 + 4 * j + side, self.s, -ds)

    def two_c(self, j):
        self.wait(self.slot(self.STEPS[j], 2, 0), 6 + 4 * j)
        self.wait(self.slot(self.STEPS[j], 2, 1), 7 + 4 * j)

    def done(self):
        for copy in self.sent:
            copy.wait_send()


def spread_rest(halves):
    for side in (0, 1):
        for h in halves:
            h.one_b(side)
            h.two_a(1 + side)
    yield
    for side in (0, 1):
        for h in halves:
            h.two_b(0, side)
    yield
    for h in halves:
        h.one_c()
        h.two_a(3)
    yield
    for j in (1, 2, 3):
        for side in (0, 1):
            for h in halves:
                h.two_b(j, side)
        yield
    for j in range(4):
        for h in halves:
            h.two_c(j)
    for h in halves:
        h.done()


class Weights:
    def __init__(self, at, pieces, outs, ssem, rsem, qs, qr, lsem):
        self.at, self.pieces, self.outs = at, pieces, outs
        self.ssem, self.rsem, self.qs, self.qr, self.lsem = ssem, rsem, qs, qr, lsem

    def steps(self):
        at = self.at
        mine = at["y"] * SIDE + at["x"]
        quad = at["zl"] * 2 + at["c"]
        near = pl.multiple_of(at["zl"] * 64, 64)
        far = pl.multiple_of(64 - at["zl"] * 64, 64)
        quads, owned = [], []
        for k, (piece, out) in enumerate(zip(self.pieces, self.outs)):
            rows = out.at[mine, pl.ds(pl.multiple_of(quad * 32, 32), 32)]
            local = pltpu.make_async_copy(piece.at[quad], rows, self.lsem.at[k])
            local.start()
            owned.append(local)
            for step in (1, 2, 3):
                to = moved(at, "quad", step)
                copy = remote(
                    piece.at[to["zl"] * 2 + to["c"]],
                    rows,
                    self.qs.at[k, step - 1],
                    self.qr.at[k, step - 1],
                    to,
                )
                copy.start()
                quads.append(copy)
        yield
        firsts, seconds = [], []
        for k, out in enumerate(self.outs):
            s, r = self.ssem, self.rsem
            firsts.append(Spread(at, "x", "y", out, near, 64, s.at[k, 0], r.at[k, 0]))
            seconds.append(Spread(at, "y", "x", out, far, 64, s.at[k, 1], r.at[k, 1]))
        for k, half in enumerate(firsts):
            owned[k].wait()
            quads[3 * k].wait_recv()
            half.one_a()
            half.two_a(0)
        yield
        for k, half in enumerate(seconds):
            quads[3 * k + 1].wait_recv()
            quads[3 * k + 2].wait_recv()
            half.one_a()
            half.two_a(0)
        yield
        yield from spread_rest(firsts + seconds)
        for copy in quads:
            copy.wait_send()

    @staticmethod
    def scratch(count):
        return [
            DMA((count, 2, 20)),
            DMA((count, 2, 20)),
            DMA((count, 3)),
            DMA((count, 3)),
            DMA((count,)),
        ]


def run(steps):
    for _ in steps:
        pass


class Gather:
    def __init__(self, at, first, second, src, lo, rows, one, two, ssem, rsem):
        self.at, self.f, self.s, self.src, self.lo, self.rows = at, first, second, src, lo, rows
        self.one, self.two, self.ssem, self.rsem = one, two, ssem, rsem

    def block(self, f, s):
        y, x = (f, s) if self.f == "y" else (s, f)
        return self.src.at[y * SIDE + x, pl.ds(self.lo, self.rows)]

    def start(self):
        self.sent = []
        for d in (2, 1, 3):
            f = lax.rem(self.at[self.f] + d, SIDE)
            for s in range(SIDE):
                k = (d - 1) * 4 + s
                copy = remote(
                    self.block(f, s),
                    self.one.at[d - 1, s],
                    self.ssem.at[k],
                    self.rsem.at[k],
                    moved(self.at, self.f, d),
                )
                copy.start()
                self.sent.append((d, s, copy))

    def arrived(self):
        for d, s, copy in self.sent:
            copy.wait_recv()

    def add(self, s, one):
        own = self.block(self.at[self.f], s)
        total = own[...].astype(F32)
        for d in range(3):
            total = total + one[d].astype(F32)
        own[...] = total.astype(BF)

    def onward(self):
        for d in (2, 1, 3):
            s = lax.rem(self.at[self.s] + d, SIDE)
            copy = remote(
                self.block(self.at[self.f], s),
                self.two.at[d - 1],
                self.ssem.at[11 + d],
                self.rsem.at[11 + d],
                moved(self.at, self.s, d),
            )
            copy.start()
            self.sent.append((d, 0, copy))

    def finish(self):
        for d, s, copy in self.sent[12:]:
            copy.wait_recv()
        total = self.block(self.at[self.f], self.at[self.s])[...].astype(F32)
        for d in range(3):
            total = total + self.two[d].astype(F32)
        return total

    def done(self):
        for d, s, copy in self.sent:
            copy.wait_send()


def middle_held(halves):
    for h in halves:
        h.arrived()

        def add(s, carry, h=h):
            h.add(s, h.one.at[:, s])
            return carry

        lax.fori_loop(0, SIDE, add, 0)
        h.onward()


def middle_staged(halves, stage, sems, onward=True):
    def load(k):
        h, s = halves[k // SIDE], k % SIDE
        return pltpu.make_async_copy(h.one.at[:, s], stage.at[k % 2], sems.at[k % 2])

    for k in range(SIDE * len(halves)):
        h, s = halves[k // SIDE], k % SIDE
        if s == 0:
            h.arrived()
        load(k).start()
        if k > 0:
            before = halves[(k - 1) // SIDE]
            load(k - 1).wait()
            before.add((k - 1) % SIDE, stage.at[(k - 1) % 2])
            if s == 0 and onward:
                before.onward()
    load(k).wait()
    h.add(s, stage.at[k % 2])
    if onward:
        h.onward()


class Grads:
    def __init__(self, at, src, out, one, two, total, ssem, rsem, qs, qr):
        self.at, self.out, self.total, self.qs, self.qr = at, out, total, qs, qr
        self.halves = [
            Gather(at, f, s, src, 64 * n, 64, one.at[n], two.at[n], ssem.at[n], rsem.at[n])
            for n, (f, s) in enumerate((("y", "x"), ("x", "y")))
        ]

    def start(self):
        for h in self.halves:
            h.start()

    def cut(self, quad):
        n = self.total.shape[2]
        if len(self.out.shape) == 2:
            return [(pl.ds(0, n), self.out.at[:, pl.ds(pl.multiple_of(quad * n, 128), n)])]
        n = n // 2
        columns = pl.ds(pl.multiple_of(quad * n, 128), n)
        return [(pl.ds(k * n, n), self.out.at[k, :, columns]) for k in (0, 1)]

    def finish(self):
        at, total = self.at, self.total
        quad = at["zl"] * 2 + at["c"]
        for n, h in enumerate(self.halves):
            total[n] = h.finish().astype(BF)
        self.quads = []
        for step in (3, 2, 1):
            to = moved(at, "quad", step)
            rows = pl.ds(pl.multiple_of(to["c"] * 32, 32), 32)
            for k, (columns, place_) in enumerate(self.cut(quad)):
                copy = remote(
                    total.at[to["zl"], rows, columns],
                    place_,
                    self.qs.at[step - 1, k],
                    self.qr.at[step - 1, k],
                    to,
                )
                copy.start()
                self.quads.append(copy)
        rows = pl.ds(pl.multiple_of(at["c"] * 32, 32), 32)
        for columns, place_ in self.cut(quad):
            place_[...] = total[at["zl"], rows, columns]

    def done(self):
        for copy in self.quads:
            copy.wait()
        for h in self.halves:
            h.done()

    @staticmethod
    def shape(n):
        return (2, 3, SIDE, 64, n)

    @staticmethod
    def scratch(n):
        return [
            pltpu.VMEM((2, 3, 64, n), BF),
            pltpu.VMEM((2, 64, n), BF),
            DMA((2, 15)),
            DMA((2, 15)),
            DMA((3, 2)),
            DMA((3, 2)),
        ]


class TeamGather:
    def __init__(self, at, out, ssem, rsem):
        self.at, self.out, self.ssem, self.rsem = at, out, ssem, rsem

    def start(self, src=None):
        at, out = self.at, self.out
        c, z = at["c"], at["zh"] * 2 + at["zl"]
        mine = out.at[place(z, c)]
        src = mine if src is None else src
        self.ring = []
        for k, d in enumerate((2, 1, -1)):
            copy = remote(src, mine, self.ssem.at[k], self.rsem.at[k], moved(at, "z", d))
            copy.start()
            self.ring.append(copy)
        copy = remote(src, mine, self.ssem.at[6], self.rsem.at[6], moved(at, "c"))
        copy.start()
        self.pair = [copy]

    def forward(self):
        at, out = self.at, self.out
        c, z = at["c"], at["zh"] * 2 + at["zl"]
        for k, d in ((1, 1), (2, -1), (0, 2)):
            slot = out.at[place(lax.rem(z - d + SIDE, SIDE), c)]
            self.ring[k].wait_recv()
            copy = remote(slot, slot, self.ssem.at[3 + k], self.rsem.at[3 + k], moved(at, "c"))
            copy.start()
            self.pair.append(copy)

    def finish(self):
        for copy in self.pair:
            copy.wait_recv()

    def done(self):
        for copy in self.ring + self.pair:
            copy.wait_send()


class TeamReduce:
    ORDER = (2, 1, -1, 0)

    def __init__(self, at, part, one, held, two, ssem, rsem):
        self.at, self.part, self.one, self.held, self.two = at, part, one, held, two
        self.ssem, self.rsem = ssem, rsem

    def slot(self, d, c):
        return place(lax.rem(self.at["zh"] * 2 + self.at["zl"] + d + SIDE, SIDE), c)

    def start(self):
        self.first, self.second = [], []
        for k, d in enumerate(self.ORDER):
            copy = remote(
                self.part.at[self.slot(d, 1 - self.at["c"])],
                self.one.at[k],
                self.ssem.at[k],
                self.rsem.at[k],
                moved(self.at, "c"),
            )
            copy.start()
            self.first.append(copy)

    def middle(self):
        for k, d in enumerate(self.ORDER):
            self.first[k].wait_recv()
            if d == 0:
                continue
            mine = self.part[self.slot(d, self.at["c"])].astype(F32)
            self.held[k] = (mine + self.one[k].astype(F32)).astype(BF)
            copy = remote(
                self.held.at[k],
                self.two.at[k],
                self.ssem.at[4 + k],
                self.rsem.at[4 + k],
                moved(self.at, "z", d),
            )
            copy.start()
            self.second.append(copy)

    def finish(self):
        total = self.part[self.slot(0, self.at["c"])].astype(F32) + self.one[3].astype(F32)
        for k in (1, 2, 0):
            self.second[k].wait_recv()
            total = total + self.two[k].astype(F32)
        return total

    def done(self):
        for copy in self.first + self.second:
            copy.wait_send()

    @staticmethod
    def scratch(count, width):
        return [
            pltpu.VMEM((4, count, width), BF),
            pltpu.VMEM((3, count, width), BF),
            pltpu.VMEM((3, count, width), BF),
            DMA((7,)),
            DMA((7,)),
        ]


class Sum:
    def __init__(self, at, value, pair, ring, row, column, ssem, rsem):
        self.at, self.value, self.ssem, self.rsem = at, value, ssem, rsem
        self.axes = (
            ("c", pair, at["c"]),
            ("z", ring, at["zh"] * 2 + at["zl"]),
            ("x", row, at["x"]),
            ("y", column, at["y"]),
        )

    def steps(self):
        k = 0
        for axis, buffer, me in self.axes:
            buffer[me] = self.value[...]
            copies = []
            for step in range(1, buffer.shape[0]):
                copy = remote(
                    buffer.at[me],
                    buffer.at[me],
                    self.ssem.at[k],
                    self.rsem.at[k],
                    moved(self.at, axis, step),
                )
                copy.start()
                copies.append(copy)
                k += 1
            yield
            for copy in copies:
                copy.wait()
            total = buffer[0]
            for n in range(1, buffer.shape[0]):
                total = total + buffer[n]
            self.value[...] = total

    @staticmethod
    def scratch(shape):
        return [pltpu.VMEM((n,) + shape, F32) for n in (2, 4, 4, 4)] + [DMA((10,)), DMA((10,))]


def dot_plain(a, b):
    return jnp.dot(a, b, preferred_element_type=F32)


def dot_last(a, b):
    return lax.dot_general(a, b, (((1,), (1,)), ((), ())), preferred_element_type=F32)


def dot_first(a, b):
    return lax.dot_general(a, b, (((0,), (0,)), ((), ())), preferred_element_type=F32)


def sweep(start, stop, body):
    pairs = jnp.maximum(stop - start, 0) // 2

    def two(n, carry):
        body(start + 2 * n)
        body(start + 2 * n + 1)
        return carry

    def one(n, carry):
        body(n)
        return carry

    lax.fori_loop(0, pairs, two, 0)
    lax.fori_loop(start + 2 * pairs, stop, one, 0)


def lanes_of(value):
    return lax.broadcasted_iota(jnp.int32, value.shape, 1)


def turn(value):
    low = lax.rem(lanes_of(value), 64) < 32
    return jnp.where(low, -pltpu.roll(value, 96, 1), pltpu.roll(value, 32, 1))


def head_gains(gains_ref):
    both = gains_ref[32:33]
    other = pltpu.roll(both, 64, 1)
    left = lanes_of(both) < 64
    return jnp.where(left, both, other), jnp.where(left, other, both)


def wide_gain(gains_ref, first):
    return jnp.concatenate([gains_ref[n : n + 1] for n in range(first, first + 16)], axis=1)


def numbers(seg_ref, block):
    parts = [seg_ref[pl.ds(block * 4 + n, 1)].astype(F32) for n in range(4)]
    return jnp.concatenate(parts, axis=1)


def upright(row):
    return jnp.broadcast_to(row, (8, row.shape[1])).T[:, :1]


def normalize(value):
    left = lanes_of(value) < 64
    square = value * value
    one = jnp.sum(jnp.where(left, square, 0.0), axis=-1, keepdims=True)
    two = jnp.sum(jnp.where(left, 0.0, square), axis=-1, keepdims=True)
    return value * lax.rsqrt(jnp.where(left, one, two) / HD + EPS_NORM)


def forward_kernel(*refs):
    (x_ref, ct_ref, gains_ref, cos_ref, sin_ref, seg_ref) = refs[:6]
    weights = refs[6:11]
    (rows_out, grads_out, joined_out, output_out, expand_out, reduce_out) = refs[11:17]
    (projected_out, queries_out, every_out, out_ref, attn_out, middle_out, ffn_out) = refs[17:24]
    sum_ref, part = refs[24:26]
    reduce_scratch = refs[26:31]
    small_scratch, large_scratch = refs[31:36], refs[36:41]
    ks, kr, gs, gr, lsem = refs[41:46]
    pieces = refs[46:50]
    results = (rows_out, joined_out, output_out, every_out)
    rows_out, joined_out, output_out, every_out = refs[50:54]
    buffers, psem = refs[50:54], refs[54]

    def park(n):
        copy = pltpu.make_async_copy(buffers[n], results[n], psem.at[n])
        copy.start()
        return copy

    at = here()
    team = at["y"] * SIDE + at["x"]
    me = place(at["zh"] * 2 + at["zl"], at["c"])
    rows = queries_out.shape[1]
    sources = ((0, 0, 0, 384), (1, 1, 0, 256), (2, 2, 0, 1024), (3, 2, 1024, 1024), (4, 3, 0, 1024))
    for source, piece, to, n in sources:
        for t in range(4):
            value = weights[source][:, n * t : n * t + n]
            pieces[piece][t, :, to : to + n] = value.astype(BF)
    greet(at, RING + NEAR + QUAD[1:])

    small = Weights(at, pieces[:2], [joined_out, output_out], *small_scratch).steps()
    large = Weights(at, pieces[2:], [expand_out, reduce_out], *large_scratch).steps()
    next(small)

    residual = x_ref[...].astype(F32)
    scale = lax.rsqrt(jnp.mean(residual * residual, axis=-1, keepdims=True) + EPS_NORM)
    rows_out[me] = (residual * scale * wide_gain(gains_ref, 0)).astype(BF)
    gather = TeamGather(at, rows_out, gs.at[0], gr.at[0])
    gather.start()
    run(small)
    gather.forward()
    next(large)
    gather.finish()

    projected_out[...] = jnp.dot(
        rows_out[...].reshape(rows, D),
        joined_out[...].reshape(D, 384),
        preferred_element_type=F32,
    )
    next(large)
    parked = [park(0), park(1), park(2)]
    query_gain, key_gain = head_gains(gains_ref)
    cosine, sine = cos_ref[...], sin_ref[...]
    left = lax.broadcasted_iota(jnp.int32, (rows, 128), 1) < 64
    raw = projected_out[:, 256:]
    key = normalize(raw) * key_gain
    key = key * cosine + turn(key) * sine
    every_out[team] = jnp.where(left, key, raw).astype(BF)
    halves = [
        Spread(at, "x", "y", every_out, 0, rows // 2, ks.at[0], kr.at[0]),
        Spread(at, "y", "x", every_out, rows // 2, rows // 2, ks.at[1], kr.at[1]),
    ]
    for h in halves:
        h.one_a()
        h.two_a(0)
    for n in range(2):
        query = normalize(projected_out[:, 128 * n : 128 * n + 128]) * query_gain
        query = query * cosine + turn(query) * sine
        query = query.astype(BF).astype(F32) * (HD**-0.5)
        queries_out[2 * n] = jnp.where(left, query, 0.0).astype(BF)
        queries_out[2 * n + 1] = jnp.where(left, pltpu.roll(query, 64, 1), 0.0).astype(BF)
    run(spread_rest(halves))
    parked.append(park(3))
    local = pltpu.make_async_copy(ct_ref, grads_out.at[me], lsem)
    local.start()
    cotangents = TeamGather(at, grads_out, gs.at[1], gr.at[1])
    cotangents.start(ct_ref)
    next(large)

    out_ref[...] = jnp.zeros_like(out_ref)
    sum_ref[...] = jnp.zeros_like(sum_ref)

    def block(number, allowed):
        pairs = every_out[number]
        for h in range(GROUP_HEADS):
            weights = jnp.exp(dot_last(queries_out[h], pairs))
            if allowed is not None:
                weights = jnp.where(allowed, weights, 0.0)
            add = weights[:, :128]
            for lane in range(128, rows, 128):
                add = add + weights[:, lane : lane + 128]
            sum_ref[h] += add
            out_ref[h] += jnp.dot(weights.astype(BF), pairs, preferred_element_type=F32)

    def inner(number):
        block(number, None)

    sweep(1, jnp.maximum(team - 6, 1), inner)
    next(large)
    sweep(jnp.maximum(team - 6, 1), team, inner)
    next(large)
    own = upright(numbers(seg_ref, team))
    main = (own == seg_ref[0:1, 127:128].astype(F32)).astype(F32)
    for h in range(GROUP_HEADS):
        out_ref[h] *= main
        sum_ref[h] *= main

    def edge(step, carry):
        number = step * team
        ahead = (number - team) * rows
        row = lax.broadcasted_iota(jnp.int32, (rows, rows), 0)
        column = lax.broadcasted_iota(jnp.int32, (rows, rows), 1) + ahead
        block(number, (column <= row) & (own == numbers(seg_ref, number)))
        return carry

    lax.fori_loop(jnp.where(team == 0, 1, 0), 2, edge, 0)
    cotangents.forward()
    for h in range(GROUP_HEADS):
        total = jnp.sum(sum_ref[h], axis=-1, keepdims=True)
        sum_ref[h] = jnp.broadcast_to(total, sum_ref.shape[1:])
        out_ref[h] = jnp.where(left, sum_ref[h], out_ref[h] / sum_ref[h])
    for n in range(2):
        one, two = out_ref[2 * n], out_ref[2 * n + 1]
        attn_out[:, 128 * n : 128 * n + 128] = jnp.where(left, pltpu.roll(one, 64, 1), two).astype(BF)

    def project(n, carry):
        columns = pl.ds(pl.multiple_of(n * 512, 512), 512)
        weight = output_out[pl.ds(n * 4, 4)].reshape(512, 256)
        branch = dot_last(attn_out[...], weight).astype(BF)
        part[:, :, columns] = branch.reshape(TEAM, 64, 512)
        return carry

    lax.fori_loop(0, 4, project, 0)
    branch = TeamReduce(at, part, *reduce_scratch)
    branch.start()
    branch.middle()
    next(large)
    middle = residual + branch.finish()
    middle_out[...] = middle
    scale = lax.rsqrt(jnp.mean(middle * middle, axis=-1, keepdims=True) + EPS_NORM)
    ffn_out[me] = (middle * scale * wide_gain(gains_ref, 16)).astype(BF)
    second = TeamGather(at, ffn_out, gs.at[2], gr.at[2])
    second.start()
    next(large)
    second.forward()
    next(large)
    second.finish()
    run(large)
    cotangents.finish()
    local.wait()
    for transfer in (gather, cotangents, second, branch):
        transfer.done()
    for copy in parked:
        copy.wait()


def forward(x, ct, gains, cosine, sine, segs, weights, cid):
    rows = TEAM * 64

    def out(shape, kind=BF):
        return jax.ShapeDtypeStruct(shape, kind)

    return pl.pallas_call(
        forward_kernel,
        out_shape=[
            out((TEAM, 64, D)),
            out((TEAM, 64, D)),
            out((TEAMS, 128, 384)),
            out((TEAMS, 128, 256)),
            out((TEAMS, 128, 2048)),
            out((TEAMS, 128, 1024)),
            out((rows, 384), F32),
            out((GROUP_HEADS, rows, 128)),
            out((TEAMS, rows, 128)),
            out((GROUP_HEADS, rows, 128), F32),
            out((rows, 256)),
            out((64, D), F32),
            out((TEAM, 64, D)),
        ],
        in_specs=[VM, ANY] + [VM] * 9,
        out_specs=[ANY] * 6 + [VM, VM, ANY] + [VM] * 4,
        scratch_shapes=[pltpu.VMEM((GROUP_HEADS, rows, 128), F32), pltpu.VMEM((TEAM, 64, D), BF)]
        + TeamReduce.scratch(64, D)
        + Weights.scratch(2)
        + Weights.scratch(2)
        + [DMA((2, 20)), DMA((2, 20)), DMA((3, 7)), DMA((3, 7)), DMA]
        + [pltpu.VMEM((4, 32, n), BF) for n in (384, 256, 2048, 1024)]
        + [
            pltpu.VMEM((TEAM, 64, D), BF),
            pltpu.VMEM((TEAMS, 128, 384), BF),
            pltpu.VMEM((TEAMS, 128, 256), BF),
            pltpu.VMEM((TEAMS, rows, 128), BF),
            DMA((4,)),
        ],
        compiler_params=params(cid, 56),
    )(x, ct, gains, cosine, sine, segs, *weights)


def norm_back(value, gain, grad):
    scale = lax.rsqrt(jnp.mean(value * value, axis=-1, keepdims=True) + EPS_NORM)
    unit = value * scale
    inner = grad * gain
    back = scale * (inner - unit * jnp.mean(inner * unit, axis=-1, keepdims=True))
    return back, jnp.sum(grad * unit, axis=0, keepdims=True)


def back_kernel(*refs):
    (rows_any, grads_any, middle_ref, ct_ref, x_ref, gains_ref, cos_ref, sin_ref, seg_ref) = refs[:9]
    refs = refs[:7] + (None,) * 4 + refs[7:]
    expand_any, reduce_any = refs[13:15]
    late_any = refs[15:23]
    block_out, input_out, sum_out, expand_out, reduce_out, output_out, joined_out = refs[23:30]
    expand_one, reduce_one = refs[30:32]
    expand_ref, reduce_ref, hidden_ref, both_ref, part, branch_ref, back_ref, grad_ref = refs[32:40]
    (joined_ref, output_ref, q_ref, kv_ref, out_ref, attn_ref, projected_ref) = refs[40:47]
    inner_ref, innerm_ref, dq_ref, dkv_ref = refs[47:51]
    output_grad, joined_grad, output_one, joined_one = refs[51:55]
    expand_sems, reduce_sems, output_sems, joined_sems = (
        refs[55:61],
        refs[61:67],
        refs[67:73],
        refs[73:79],
    )
    first_scratch, second_scratch = refs[79:84], refs[84:89]
    kv_one, kv_two, ks, kr, stage, stage_sem, gs, gr, wsem, lsem = refs[89:99]
    rows_ref, grads_ref, isem = refs[99:102]
    sum_scratch = refs[102:]
    late_refs = refs[40:47] + (rows_ref,)
    slabs = [both_ref.at[:, pl.ds(128 * n, 128)] for n in range(3 * GROUP_HEADS)]
    do_refs, qm_refs, dom_refs = (slabs[n : n + GROUP_HEADS] for n in (0, 4, 8))
    q_refs = [q_ref.at[h] for h in range(GROUP_HEADS)]
    gp_ref = hidden_ref.at[:, pl.ds(0, 384)]
    at = here()
    me = place(at["zh"] * 2 + at["zl"], at["c"])
    team = at["y"] * SIDE + at["x"]
    rows = TEAM * 64
    late = [
        pltpu.make_async_copy(src, dst, lsem.at[n])
        for n, (src, dst) in enumerate(zip(late_any, late_refs))
    ]

    def loads(n):
        low = pl.ds(pl.multiple_of(n * 256, 256), 256)
        high = pl.ds(pl.multiple_of(n * 256 + 1024, 256), 256)
        return [
            pltpu.make_async_copy(any_.at[:, :, part_], ref.at[:, :, part_], wsem.at[n, k])
            for k, (any_, ref, part_) in enumerate(
                (
                    (expand_any, expand_ref, low),
                    (expand_any, expand_ref, high),
                    (reduce_any, reduce_ref, low),
                )
            )
        ]

    inputs = [
        pltpu.make_async_copy(rows_any, rows_ref, isem.at[0]),
        pltpu.make_async_copy(grads_any, grads_ref, isem.at[1]),
    ]
    for copy in inputs:
        copy.start()
    for n in range(4):
        for copy in loads(n):
            copy.start()
    greet(at, RING + FAR + QUAD[1:])
    for copy in late[:-1]:
        copy.start()
    for copy in inputs:
        copy.wait()
    ffn_values = rows_ref[...].reshape(rows, D)
    grad_values = grads_ref[...].reshape(rows, D)

    def feed(n, carry):
        for copy in loads(n):
            copy.wait()
        low = pl.ds(pl.multiple_of(n * 256, 256), 256)
        high = pl.ds(pl.multiple_of(n * 256 + 1024, 256), 256)
        gate = dot_plain(ffn_values, expand_ref[:, :, low].reshape(D, 256))
        up = dot_plain(ffn_values, expand_ref[:, :, high].reshape(D, 256))
        grad = dot_plain(grad_values, reduce_ref[:, :, low].reshape(D, 256))
        open_ = 1.0 / (1.0 + jnp.exp(-gate))
        silu = gate * open_
        hidden_ref[:, low] = (silu * up).astype(BF)
        both_ref[:, low] = (grad * up * (open_ + silu * (1.0 - open_))).astype(BF)
        both_ref[:, high] = (grad * silu).astype(BF)
        return carry

    lax.fori_loop(0, 4, feed, 0)

    def project(n, carry):
        columns = pl.ds(pl.multiple_of(n * 512, 512), 512)
        weight = expand_ref[pl.ds(n * 4, 4)].reshape(512, 2048)
        part[:, :, columns] = dot_last(both_ref[...], weight).astype(BF).reshape(TEAM, 64, 512)
        return carry

    lax.fori_loop(0, 4, project, 0)
    first = TeamReduce(at, part, *first_scratch)
    first.start()

    def branch(n, carry):
        columns = pl.ds(pl.multiple_of(n * 512, 512), 512)
        weight = reduce_ref[pl.ds(n * 4, 4)].reshape(512, 1024)
        value = dot_last(hidden_ref[...], weight).astype(BF)
        branch_ref[:, :, columns] = value.reshape(TEAM, 64, 512)
        return carry

    first.middle()
    lax.fori_loop(0, 4, branch, 0)

    def grad_reduce(n, carry):
        columns = pl.ds(pl.multiple_of(n * 256, 256), 256)
        grad = dot_first(grads_ref[:, :, columns].reshape(rows, 256), hidden_ref[...])
        reduce_ref[pl.ds(n * 2, 2)] = grad.astype(BF).reshape(2, 128, 1024)
        return carry

    lax.fori_loop(0, 8, grad_reduce, 0, unroll=2)
    reduced = Grads(at, reduce_ref, reduce_out, reduce_one, *reduce_sems)
    reduced.start()

    back, gain = norm_back(middle_ref[...], wide_gain(gains_ref, 16), first.finish())
    ffn_gain = gain
    grad_middle = ct_ref[...].astype(F32) + back
    grad_ref[...] = grad_middle
    back_ref[me] = grad_middle.astype(BF)
    gather = TeamGather(at, back_ref, gs, gr)
    gather.start()

    def grad_expand(n, carry):
        columns = pl.ds(pl.multiple_of(n * 256, 256), 256)
        grad = dot_first(rows_ref[:, :, columns].reshape(rows, 256), both_ref[...])
        expand_ref[pl.ds(n * 2, 2)] = grad.astype(BF).reshape(2, 128, 2048)
        return carry

    lax.fori_loop(0, 8, grad_expand, 0)
    late[-1].start()
    expanded = Grads(at, expand_ref, expand_out, expand_one, *expand_sems)
    expanded.start()
    gather.forward()
    gather.finish()
    for copy in late[:-1]:
        copy.wait()
    branch = TeamReduce(at, branch_ref, *second_scratch)
    branch.start()

    attended = dot_plain(back_ref[...].reshape(rows, D), output_ref[...].reshape(D, 256))
    left = lax.broadcasted_iota(jnp.int32, (rows, 128), 1) < 64
    ones = jnp.ones((8, 128), BF)
    own = numbers(seg_ref, team)
    main = (own == seg_ref[0:1, 127:128].astype(F32)).astype(F32)
    low = upright(main).astype(BF)
    dq_ref[...] = jnp.zeros_like(dq_ref)
    for h in range(GROUP_HEADS):
        grad = attended[:, 128 * (h // 2) : 128 * (h // 2) + 128]
        if h % 2 == 0:
            grad = pltpu.roll(grad, 64, 1)
        value = out_ref[h]
        scaled = jnp.where(left, 0.0, grad / value[:, :1]).astype(BF)
        do_refs[h][...] = scaled
        inner = jnp.where(left, 0.0, scaled.astype(F32) * value)
        high = inner.astype(BF)
        rest = (inner - high.astype(F32)).astype(BF)
        inner_ref[h] = (dot_last(ones, high) + dot_last(ones, rest))[0:1]
        qm_refs[h][...] = q_ref[h] * low
        dom_refs[h][...] = scaled * low
        innerm_ref[h] = inner_ref[h] * main

    def grad_output(n, carry):
        columns = pl.ds(pl.multiple_of(n * 256, 256), 256)
        grad = dot_first(back_ref[:, :, columns].reshape(rows, 256), attn_ref[...])
        output_grad[pl.ds(n * 2, 2)] = grad.astype(BF).reshape(2, 128, 256)
        return carry

    lax.fori_loop(0, 8, grad_output, 0, unroll=True)
    output = Grads(at, output_grad, output_out, output_one, *output_sems)
    output.start()
    branch.middle()

    def block(number, allowed, q, do, inner):
        pairs = kv_ref[number]
        total = jnp.zeros(pairs.shape, F32)
        for h in range(GROUP_HEADS):
            query, above = q[h][...], do[h][...]
            weights = jnp.exp(dot_last(pairs, query))
            if allowed is not None:
                weights = jnp.where(allowed, weights, 0.0)
            grad = (weights * (dot_last(pairs, above) - inner[h])).astype(BF)
            total = total + dot_plain(grad, query)
            total = total + dot_plain(weights.astype(BF), above)
            dq_ref[h] += dot_first(pairs, grad)
        dkv_ref[number] = total.astype(BF)

    def interior(number, carry):
        block(number, None, qm_refs, dom_refs, innerm_ref)
        return carry

    lax.fori_loop(1, team, interior, 0)

    def edge(step, carry):
        number = step * team
        ahead = (number - team) * rows
        row = lax.broadcasted_iota(jnp.int32, (rows, rows), 1)
        column = lax.broadcasted_iota(jnp.int32, (rows, rows), 0) + ahead
        allowed = (column <= row) & (upright(numbers(seg_ref, number)) == own)
        block(number, allowed, q_refs, do_refs, inner_ref)
        return carry

    lax.fori_loop(jnp.where(team == 0, 1, 0), 2, edge, 0)

    def rest_of(number, carry):
        dkv_ref[number] = jnp.zeros(dkv_ref.shape[1:], BF)
        return carry

    lax.fori_loop(team + 1, TEAMS, rest_of, 0)
    half = rows // 2
    pairs = [
        Gather(at, f, s, dkv_ref, half * n, half, kv_one.at[n], kv_two.at[n], ks.at[n], kr.at[n])
        for n, (f, s) in enumerate((("y", "x"), ("x", "y")))
    ]
    for h in pairs:
        h.start()
    block_out[...] = (middle_ref[...] + branch.finish()).astype(BF)

    cosine, sine = cos_ref[...], sin_ref[...]
    head_gain = head_gains(gains_ref)

    def prepare_back(raw, gain, grad):
        unit = normalize(raw)
        square = raw * raw
        across = jnp.sum(jnp.where(left, square, 0.0), axis=-1, keepdims=True)
        along = jnp.sum(jnp.where(left, 0.0, square), axis=-1, keepdims=True)
        scale = lax.rsqrt(jnp.where(left, across, along) / HD + EPS_NORM)
        grad = grad * cosine - turn(grad * sine)
        gain_grad = jnp.sum(grad * unit, axis=0, keepdims=True)
        grad = grad * gain
        inner = grad * unit
        across = jnp.sum(jnp.where(left, inner, 0.0), axis=-1, keepdims=True)
        along = jnp.sum(jnp.where(left, 0.0, inner), axis=-1, keepdims=True)
        return scale * (grad - unit * (jnp.where(left, across, along) / HD)), gain_grad

    query_gain = jnp.zeros((1, 128), F32)
    for n in range(2):
        both = jnp.concatenate([dq_ref[2 * n, :64], dq_ref[2 * n + 1, :64]], axis=0)
        columns = slice(128 * n, 128 * n + 128)
        grad, gain = prepare_back(
            projected_ref[:, columns], head_gain[0], both.T * (HD**-0.5)
        )
        query_gain = query_gain + gain
        gp_ref[:, columns] = grad.astype(BF)
    middle_staged(reduced.halves, stage.at[:, :, :, pl.ds(0, 1024)], stage_sem, False)
    middle_held(pairs)
    for h in reduced.halves:
        h.onward()
    middle_staged(expanded.halves, stage, stage_sem)
    middle_held(output.halves)
    pair_grad = jnp.concatenate([h.finish() for h in pairs], axis=0)
    grad, key_gain = prepare_back(projected_ref[:, 256:], head_gain[1], pair_grad)
    gp_ref[:, 256:] = jnp.where(left, grad, pair_grad).astype(BF)

    first.done()

    def project(n, carry):
        columns = pl.ds(pl.multiple_of(n * 512, 512), 512)
        weight = joined_ref[pl.ds(n * 4, 4)].reshape(512, 384)
        part[:, :, columns] = dot_last(gp_ref[...], weight).astype(BF).reshape(TEAM, 64, 512)
        return carry

    lax.fori_loop(0, 4, project, 0)
    last = TeamReduce(at, part, *first_scratch)
    last.start()
    late[-1].wait()

    def grad_joined(n, carry):
        columns = pl.ds(pl.multiple_of(n * 256, 256), 256)
        grad = dot_first(rows_ref[:, :, columns].reshape(rows, 256), gp_ref[...])
        joined_grad[pl.ds(n * 2, 2)] = grad.astype(BF).reshape(2, 128, 384)
        return carry

    last.middle()
    lax.fori_loop(0, 8, grad_joined, 0, unroll=True)
    joined = Grads(at, joined_grad, joined_out, joined_one, *joined_sems)
    joined.start()
    reduced.finish()
    back, gain = norm_back(x_ref[...].astype(F32), wide_gain(gains_ref, 0), last.finish())
    input_out[...] = (grad_ref[...] + back).astype(BF)
    for n in range(16):
        columns = slice(128 * n, 128 * n + 128)
        sum_out[n : n + 1, :] = gain[:, columns]
        sum_out[16 + n : 17 + n, :] = ffn_gain[:, columns]
    query_gain = query_gain + pltpu.roll(query_gain, 64, 1)
    lane = lax.broadcasted_iota(jnp.int32, (1, 128), 1)
    sum_out[32:33, :] = jnp.where(lane < 64, query_gain, pltpu.roll(key_gain, 64, 1))
    sums = Sum(at, sum_out, *sum_scratch).steps()
    next(sums)
    expanded.finish()
    next(sums)
    output.finish()
    middle_held(joined.halves)
    next(sums)
    next(sums)
    joined.finish()
    run(sums)
    for transfer in (reduced, expanded, output, joined, branch, last, gather):
        transfer.done()
    for h in pairs:
        h.done()


def backward(arrays, expand_all, reduce_all, late, cid):
    rows = TEAM * 64

    def out(shape, kind=BF):
        return jax.ShapeDtypeStruct(shape, kind)

    return pl.pallas_call(
        back_kernel,
        out_shape=[
            out((64, D)),
            out((64, D)),
            out((33, 128), F32),
            out((2, 32, 4096)),
            out((32, 4096)),
            out((32, 1024)),
            out((32, 1536)),
            out(Grads.shape(2048)),
            out(Grads.shape(1024)),
        ],
        in_specs=[ANY] * 2 + [VM] * (len(arrays) - 2) + [ANY] * (2 + len(late)),
        out_specs=[VM] * 7 + [ANY] * 2,
        scratch_shapes=[
            pltpu.VMEM((TEAMS, 128, 2048), BF),
            pltpu.VMEM((TEAMS, 128, 1024), BF),
            pltpu.VMEM((rows, 1024), BF),
            pltpu.VMEM((rows, 2048), BF),
            pltpu.VMEM((TEAM, 64, D), BF),
            pltpu.VMEM((TEAM, 64, D), BF),
            pltpu.VMEM((TEAM, 64, D), BF),
            pltpu.VMEM((64, D), F32),
        ]
        + [pltpu.VMEM(v.shape, v.dtype) for v in late[:-1]]
        + [
            pltpu.VMEM((GROUP_HEADS, 1, rows), F32),
            pltpu.VMEM((GROUP_HEADS, 1, rows), F32),
            pltpu.VMEM((GROUP_HEADS, 128, rows), F32),
            pltpu.VMEM((TEAMS, rows, 128), BF),
            pltpu.VMEM((TEAMS, 128, 256), BF),
            pltpu.VMEM((TEAMS, 128, 384), BF),
            pltpu.VMEM(Grads.shape(256), BF),
            pltpu.VMEM(Grads.shape(384), BF),
        ]
        + Grads.scratch(2048)
        + Grads.scratch(1024)
        + Grads.scratch(256)
        + Grads.scratch(384)
        + TeamReduce.scratch(64, D)
        + TeamReduce.scratch(64, D)
        + [
            pltpu.VMEM((2, 3, SIDE, rows // 2, 128), BF),
            pltpu.VMEM((2, 3, rows // 2, 128), BF),
            DMA((2, 15)),
            DMA((2, 15)),
            pltpu.VMEM((2, 3, 64, 2048), BF),
            DMA((2,)),
            DMA((7,)),
            DMA((7,)),
            DMA((4, 3)),
            DMA((len(late),)),
            pltpu.VMEM((TEAM, 64, D), BF),
            pltpu.VMEM((TEAM, 64, D), BF),
            DMA((2,)),
        ]
        + Sum.scratch((33, 128)),
        compiler_params=params(cid, 63),
    )(*arrays, expand_all, reduce_all, *late)[:7]


def on_device(
    block_in,
    cotangent,
    segments,
    gains,
    joined_weight,
    output_weight,
    expand_weight,
    reduce_weight,
    gains_first,
    gains_squares,
    joined_first,
    joined_squares,
    output_first,
    output_squares,
    expand_first,
    expand_squares,
    reduce_first,
    reduce_squares,
):
    team = lax.axis_index("y") * SIDE + lax.axis_index("x")
    rows = TEAM * 64
    positions = jnp.arange(rows, dtype=jnp.int32) + team * rows
    inverse = THETA ** (-(jnp.arange(0, HD, 2).astype(F32) / HD))
    angles = positions.astype(F32)[:, None] * inverse[None, :]
    cosine, sine = jnp.tile(jnp.cos(angles), (1, 4)), jnp.tile(jnp.sin(angles), (1, 4))
    lines = gains.reshape(33, 128)
    segs = segments.reshape(-1, 128)
    (
        attn_rows,
        grad_rows,
        joined_all,
        output_all,
        expand_all,
        reduce_all,
        projected,
        queries,
        every,
        attended,
        attn_out,
        middle,
        ffn_rows,
    ) = forward(
        block_in,
        cotangent,
        lines,
        cosine,
        sine,
        segs,
        [
            joined_weight.reshape(32, 1536),
            output_weight,
            expand_weight[:, 0],
            expand_weight[:, 1],
            reduce_weight,
        ],
        1,
    )
    (
        block_out,
        input_grad,
        gain_grad,
        shard_expand,
        shard_reduce,
        shard_output,
        shard_joined,
    ) = backward(
        [
            ffn_rows,
            grad_rows,
            middle,
            cotangent,
            block_in,
            lines,
            cosine,
            sine,
            segs,
        ],
        expand_all,
        reduce_all,
        [joined_all, output_all, queries, every, attended, attn_out, projected, attn_rows],
        2,
    )
    gain_grad = gain_grad.reshape(-1)
    shard_joined = shard_joined.reshape(32, 4, 384).astype(F32)
    shard_output = shard_output.astype(F32)
    shard_expand = shard_expand.transpose(1, 0, 2).astype(F32)
    shard_expand = with_layout_constraint(shard_expand, Layout(major_to_minor=(0, 1, 2)))
    shard_reduce = shard_reduce.astype(F32)
    joined = adamw(joined_weight, shard_joined, joined_first, joined_squares, D ** (-0.5))
    output = adamw(
        output_weight, shard_output, output_first, output_squares, max(1, H * HD // 128) ** (-0.5)
    )
    expand = adamw(expand_weight, shard_expand, expand_first, expand_squares, D ** (-0.5))
    reduce_new = adamw(reduce_weight, shard_reduce, reduce_first, reduce_squares, FF ** (-0.5))
    gain_new = adamw(gains, gain_grad, gains_first, gains_squares, GAIN_RATE)
    return (
        block_out,
        input_grad,
        joined[0],
        joined[1],
        joined[2],
        joined[2].astype(BF),
        output[0],
        output[1],
        output[2],
        output[2].astype(BF),
        expand[0],
        expand[1],
        expand[2],
        expand[2].astype(BF),
        reduce_new[0],
        reduce_new[1],
        reduce_new[2],
        reduce_new[2].astype(BF),
        gain_new[0],
        gain_new[1],
        gain_new[2],
    )


def solution(mesh):
    physical = Mesh(mesh.devices.reshape(SIDE, SIDE, 2, 2, 2), AXES)
    rows = P(AXES, None)
    joined = P(SEQ, "zh", None)
    plain = P(SEQ, "zh")
    expand = P(SEQ, None, "zh")
    placed = (
        (rows, rows, P(), P(), joined, plain, expand, plain, P(), P())
        + (joined,) * 2
        + (plain,) * 2
        + (expand,) * 2
        + (plain,) * 2
    )
    return jax.shard_map(
        on_device,
        mesh=physical,
        in_specs=placed,
        out_specs=(rows, rows)
        + (joined,) * 4
        + (plain,) * 4
        + (expand,) * 4
        + (plain,) * 4
        + (P(),) * 3,
        check_vma=False,
    )
```
